32 devices in a mesh: dp: 8 (over y, x, core), tensor: 4 (over z).
Axes of the slice: x: 2, y: 2, z: 4, core: 2. Of those that a mesh axis runs over, the one named last changes fastest.
Arguments:
- tokens: bfloat16 [8, 584, 1024], P('dp', 'tensor'), may hold values from -6 to 6
- cotangent: bfloat16 [8, 584, 1024], P('dp', 'tensor'), may hold values from -6 to 6
- image_mask: int32 [8], P('dp'), may hold values 0 or 1
- qkv_weight: bfloat16 [2, 1024, 3, 1024], P(None, 'dp', None, 'tensor'), may hold values from -0.1875 to 0.1875
- out_weight: bfloat16 [2, 1024, 1024], P(None, 'dp', 'tensor'), may hold values from -2 to 2
- up_weight: bfloat16 [2, 1024, 4096], P(None, 'dp', 'tensor'), may hold values from -0.1875 to 0.1875
- down_weight: bfloat16 [2, 1024, 4096], P(None, 'dp', 'tensor'), may hold values from -0.09375 to 0.09375
- qv_bias: bfloat16 [2, 2, 1024], P(None, None, ('dp', 'tensor')), may hold values from -3 to 3
- up_bias: bfloat16 [2, 4096], P(None, ('dp', 'tensor')), may hold values from -3 to 3
- out_bias: bfloat16 [2, 1024], P(None, ('dp', 'tensor')), may hold values from -3 to 3
- down_bias: bfloat16 [2, 1024], P(None, ('dp', 'tensor')), may hold values from -3 to 3
- attn_gain: bfloat16 [2, 1024], P(None, ('dp', 'tensor')), may hold values from 0.5 to 1.5
- attn_shift: bfloat16 [2, 1024], P(None, ('dp', 'tensor')), may hold values from -3 to 3
- mlp_gain: bfloat16 [2, 1024], P(None, ('dp', 'tensor')), may hold values from 0.5 to 1.5
- mlp_shift: bfloat16 [2, 1024], P(None, ('dp', 'tensor')), may hold values from -3 to 3
Outputs:
- output: bfloat16 [8, 584, 1024], P('dp', 'tensor')
- input_grad: float32 [8, 584, 1024], P('dp', 'tensor')
- qkv_weight_grad: float32 [2, 1024, 3, 1024], P(None, 'dp', None, 'tensor')
- out_weight_grad: float32 [2, 1024, 1024], P(None, 'dp', 'tensor')
- up_weight_grad: float32 [2, 1024, 4096], P(None, 'dp', 'tensor')
- down_weight_grad: float32 [2, 1024, 4096], P(None, 'dp', 'tensor')
- qv_bias_grad: float32 [2, 2, 1024], P(None, None, ('dp', 'tensor'))
- up_bias_grad: float32 [2, 4096], P(None, ('dp', 'tensor'))
- out_bias_grad: float32 [2, 1024], P(None, ('dp', 'tensor'))
- down_bias_grad: float32 [2, 1024], P(None, ('dp', 'tensor'))
- attn_gain_grad: float32 [2, 1024], P(None, ('dp', 'tensor'))
- attn_shift_grad: float32 [2, 1024], P(None, ('dp', 'tensor'))
- mlp_gain_grad: float32 [2, 1024], P(None, ('dp', 'tensor'))
- mlp_shift_grad: float32 [2, 1024], P(None, ('dp', 'tensor'))
The draws below stay inside these ranges and needn't reach their ends.
All inputs are finite; a program needn't handle non-finite values. No bound on the sum of `image_mask` on one device may be relied on, other than what follows from the above.
Results may differ from the reference program's by a relative error of at most 0.017.
Values may be sent and summed in bfloat16 or wider, within the bound.
A program may use at most 192 MiB of HBM per device.

```python
import jax
import jax.numpy as jnp
from jax import lax

D = 1024
H = 16
HD = 64
FF = 4096
SEQ = 584
LAYERS = 2
IMG_DEV = 1
VALID = 577
IMAGES = 8


def plant(drawn, stream_key, low, largest):
    place = [jax.random.randint(jax.random.fold_in(stream_key, axis), (), 0, length) for axis, length in enumerate(drawn.shape)]
    longest = drawn.shape.index(max(drawn.shape))
    neighbour = place[:longest] + [(place[longest] + 1) % drawn.shape[longest]] + place[longest + 1:]
    return drawn.at[tuple(place)].set(low).at[tuple(neighbour)].set(largest)


def levels(own_key, shape, shards, least, high):
    level, own = 1.0, jax.random.fold_in(own_key, 6)
    for position, shards_of in shards:
        draws = jnp.exp(jax.random.uniform(jax.random.fold_in(own, position), (shards_of,), jnp.float32, least / len(shards), high / len(shards)))
        level = level * jnp.repeat(draws, shape[position] // shards_of).reshape([-1 if axis == position else 1 for axis in range(len(shape))])
    return level


def noise(own_key, dims, width, most, pieces=(), dtype=jnp.bfloat16):
    entries = jax.random.normal(own_key, dims, jnp.float32) * width
    if len(pieces) > 0:
        entries = levels(own_key, dims, pieces, -0.22, 0.18) * entries
    return jnp.clip(entries, min=-most, max=most).astype(dtype)


def setup_inputs(seed: int = 0) -> dict:
    arg_keys = jax.random.split(jax.random.key(seed), 16)
    tokens = noise(arg_keys[0], (IMAGES, SEQ, D), 1.0, 6.0, ((0, 8), (1, 4)))
    cotangent = noise(arg_keys[1], (IMAGES, SEQ, D), 1.0, 6.0, ((0, 8), (1, 4)))
    image_mask = plant((jax.random.randint(arg_keys[2], (IMAGES,), 0, 8) < 7).astype(jnp.int32), jax.random.fold_in(arg_keys[2], 1), 0, 1)
    qkv_weight = noise(arg_keys[3], (LAYERS, D, 3, D), D ** -0.5, 0.1875, ((1, 8), (3, 4)))
    out_weight = noise(arg_keys[4], (LAYERS, D, D), (D * 4 // SEQ) ** -0.5, 2.0, ((1, 8), (2, 4)))
    up_weight = noise(arg_keys[5], (LAYERS, D, FF), D ** -0.5, 0.1875, ((1, 8), (2, 4)))
    down_weight = noise(arg_keys[6], (LAYERS, D, FF), FF ** -0.5, 0.09375, ((1, 8), (2, 4)))
    qv_bias = noise(arg_keys[7], (LAYERS, 2, D), 0.3, 3.0, ((2, 32),))
    up_bias = noise(arg_keys[8], (LAYERS, FF), 0.3, 3.0, ((1, 32),))
    out_bias = noise(arg_keys[9], (LAYERS, D), 0.3, 3.0, ((1, 32),))
    down_bias = noise(arg_keys[10], (LAYERS, D), 0.3, 3.0, ((1, 32),))
    attn_gain = jnp.clip(1.0 + 0.1 * jax.random.normal(arg_keys[11], (LAYERS, D), jnp.float32), 0.5, 1.5).astype(jnp.bfloat16)
    attn_shift = noise(arg_keys[12], (LAYERS, D), 0.3, 3.0, ((1, 32),))
    mlp_gain = jnp.clip(1.0 + 0.1 * jax.random.normal(arg_keys[13], (LAYERS, D), jnp.float32), 0.5, 1.5).astype(jnp.bfloat16)
    mlp_shift = noise(arg_keys[14], (LAYERS, D), 0.3, 3.0, ((1, 32),))
    return {"tokens": tokens, "cotangent": cotangent, "image_mask": image_mask, "qkv_weight": qkv_weight, "out_weight": out_weight, "up_weight": up_weight, "down_weight": down_weight, "qv_bias": qv_bias, "up_bias": up_bias, "out_bias": out_bias, "down_bias": down_bias, "attn_gain": attn_gain, "attn_shift": attn_shift, "mlp_gain": mlp_gain, "mlp_shift": mlp_shift}


@jax.custom_vjp
def low(v):
    return lax.optimization_barrier(v.astype(jnp.bfloat16)).astype(jnp.float32)

@jax.custom_vjp
def low_back(v):
    return v

def low_keep(v):
    return (low(v), None)

def low_pass(kept, grad):
    return (grad,)

def back_keep(v):
    return (v, None)

def back_low(kept, grad):
    return (low(grad),)
low.defvjp(low_keep, low_pass)
low_back.defvjp(back_keep, back_low)
highest = lax.Precision.HIGHEST
norm_eps = 1e-06
root_half = 0.7071067811865476
far_below = -1e+30

def layer_norm(values, gain_vec, shift_vec):
    centre = values - lax.optimization_barrier(jnp.mean(values, axis=-1, keepdims=True))
    spread = lax.optimization_barrier(jnp.mean(centre * centre, axis=-1, keepdims=True))
    return centre * lax.rsqrt(spread + norm_eps) * gain_vec + shift_vec

def gelu_exact(values):
    return 0.5 * values * (1.0 + lax.erf(values * root_half))

def attend_image(triple, key_valid):
    queries, key_rows, value_rows = triple
    scores = jnp.einsum('qhd,khd->hqk', queries, key_rows, precision=highest) * HD ** (-0.5)
    scores = low_back(jnp.where(key_valid[None, None, :], scores, far_below))
    row_top = lax.optimization_barrier(jnp.max(scores, axis=-1, keepdims=True))
    weights = jnp.exp(scores - row_top)
    probabilities = low(weights / lax.optimization_barrier(jnp.sum(weights, axis=-1, keepdims=True)))
    return jnp.einsum('hqk,khd->qhd', probabilities, value_rows, precision=highest)

def block(stream, layer_params):
    qkv_weight, out_weight, up_weight, down_weight, qv_bias, up_bias, out_bias, down_bias, attn_gain, attn_shift, mlp_gain, mlp_shift = layer_params
    image_count = stream.shape[0]
    key_valid = jnp.arange(SEQ) < VALID
    normed_one = low(layer_norm(stream, attn_gain, attn_shift))
    bias_three = jnp.stack([qv_bias[0], jnp.zeros_like(qv_bias[0]), qv_bias[1]])
    projected = jnp.einsum('gsd,dce->gsce', normed_one, qkv_weight, precision=highest) + bias_three
    projected = low(low_back(projected))
    by_heads = projected.reshape(image_count, SEQ, 3, H, HD)
    mixed_rows = lax.map(jax.checkpoint(lambda triple: attend_image(triple, key_valid)), (by_heads[:, :, 0], by_heads[:, :, 1], by_heads[:, :, 2]))
    mixed_rows = low(low_back(mixed_rows.reshape(image_count, SEQ, D)))
    attn_rows = jnp.einsum('gse,de->gsd', mixed_rows, out_weight, precision=highest)
    hidden = stream + low_back(attn_rows) + out_bias
    normed_two = low(layer_norm(hidden, mlp_gain, mlp_shift))
    pre_act = low_back(jnp.einsum('gsd,df->gsf', normed_two, up_weight, precision=highest) + up_bias)
    activated = low(gelu_exact(pre_act))
    down_rows = jnp.einsum('gsf,df->gsd', activated, down_weight, precision=highest)
    return hidden + low_back(down_rows) + down_bias

def reference(tokens, cotangent, image_mask, qkv_weight, out_weight, up_weight, down_weight, qv_bias, up_bias, out_bias, down_bias, attn_gain, attn_shift, mlp_gain, mlp_shift):
    params = tuple((member.astype(jnp.float32) for member in (qkv_weight, out_weight, up_weight, down_weight, qv_bias, up_bias, out_bias, down_bias, attn_gain, attn_shift, mlp_gain, mlp_shift)))
    group_count = IMAGES // IMG_DEV
    row_valid = (jnp.arange(SEQ) < VALID).astype(jnp.float32)

    def forward(layer_params, stream):
        for layer_at in range(LAYERS):
            stream = block(stream, tuple((member[layer_at] for member in layer_params)))
        return stream

    def one_group(totals, group_item):
        group_tokens, group_cot, group_mask = group_item
        result, pullback = jax.vjp(forward, params, group_tokens.astype(jnp.float32))
        weighted = group_cot.astype(jnp.float32) * group_mask.astype(jnp.float32)[:, None, None] * row_valid[None, :, None]
        param_grads, token_grads = pullback(weighted)
        totals = jax.tree.map(jnp.add, totals, param_grads)
        return (totals, (result.astype(jnp.bfloat16), token_grads))
    zero_totals = tuple((jnp.zeros_like(member) for member in params))
    totals, (outputs, input_grads) = lax.scan(one_group, zero_totals, (tokens.reshape(group_count, IMG_DEV, SEQ, D), cotangent.reshape(group_count, IMG_DEV, SEQ, D), image_mask.reshape(group_count, IMG_DEV)))
    output = outputs.reshape(IMAGES, SEQ, D)
    input_grad = input_grads.reshape(IMAGES, SEQ, D)
    return (output, input_grad, totals[0], totals[1], totals[2], totals[3], totals[4], totals[5], totals[6], totals[7], totals[8], totals[9], totals[10], totals[11])
```

```python
import functools

import jax
import jax.numpy as jnp
from jax import lax
from jax.experimental import pallas as pl
from jax.experimental.pallas import tpu as pltpu
from jax.sharding import PartitionSpec as P

HD = 64
VALID = 577
EPS = 1e-06
ROOT_HALF = 0.7071067811865476
INV_ROOT_2PI = 0.3989422804014327
FAR_BELOW = -1e30
MESH = pl.DeviceIdType.MESH
F32 = jnp.float32
BF16 = jnp.bfloat16
TILE = 32
NT = 256


def dot_nn(a, b):
    return lax.dot_general(a, b, (((1,), (0,)), ((), ())), preferred_element_type=F32)


def dot_nt(a, b):
    return lax.dot_general(a, b, (((1,), (1,)), ((), ())), preferred_element_type=F32)


def dot_tn(a, b):
    return lax.dot_general(a, b, (((0,), (0,)), ((), ())), preferred_element_type=F32)


def loop(n, body):
    def step(i, carry):
        body(i)
        return carry

    lax.fori_loop(0, n, step, 0)


def aligned(v, m):
    return pl.multiple_of(v, m)


def kernel(
    layers, rows_real,
    tok, cot, wsh, small_in,
    out_ref, ig_ref, gw_ref, sg,
    W, xs, gs, n1, n2, r1, r2, a1, a2, qkv, o, act, dgl,
    gb, hb, ub, ob, dqkv, dk_acc, dv_acc, acc,
    sendA, recvA, sendB, recvB, tokst, cotst, igst, igrecv,
    small, smrecv, smf, qb, sgrecv,
    recv1, recv2, recv4,
    s0s, s0r, s1s, s1r, s2s, s2r,
    as_, ar, bs, br, cs, cr,
    tks, tkr, cts, ctr, oss, osr, sms, smr, sgs, sgr,
    g1s, g1r, g2s, g2r, g4s, g4r,
):
    width = xs.shape[1]
    half = xs.shape[0]
    slot = half // 2
    rows_all = 2 * half
    kb = wsh.shape[1]
    blk = 2 * kb
    hq = o.shape[2]
    fq = act.shape[2]
    heads = hq // HD
    wn = width // NT

    dp = lax.axis_index("dp")
    z = lax.axis_index("tensor")
    base = (dp // 8) * 8
    d8 = dp % 8
    y, x, c = d8 // 4, (d8 // 2) % 2, d8 % 2
    zh, zl = z // 2, z % 2
    q = zl + 2 * c
    z2 = (z + 2) % 4
    home = c == zh

    def dev(yy, xx, cc, zz):
        return (base + yy * 4 + xx * 2 + cc, zz)

    sib = dev(y, x, 1 - c, z)
    xn = dev(y, 1 - x, c, z)
    yn = dev(1 - y, x, c, z)
    zp = dev(y, x, c, z + 1 - 2 * zl)
    far = dev(y, x, c, z2)
    swap = dev(y, x, zh, 2 * c + zl)
    swap_pair = dev(y, x, zh, 2 * c + 1 - zl)

    def rc(src, dst, ss, rs, to):
        return pltpu.make_async_remote_copy(
            src_ref=src, dst_ref=dst, send_sem=ss, recv_sem=rs,
            device_id=to, device_id_type=MESH)

    def wait(ref, sem):
        pltpu.make_async_copy(ref, ref, sem).wait()

    barrier = pltpu.get_barrier_semaphore()
    greet = [xn, yn, sib]
    for k in range(1, 4):
        for cc in range(2):
            greet.append(dev(y, x, cc, (z + k) % 4))
    for to in greet:
        pl.semaphore_signal(barrier, inc=1, device_id=to, device_id_type=MESH)
    pl.semaphore_wait(barrier, len(greet))

    def rows_of(yy, xx):
        return aligned((2 * yy + xx) * blk, blk)

    my_rows = pl.ds(aligned(d8 * kb, kb), kb)
    own_blk = rows_of(y, x)
    x_blk = rows_of(y, 1 - x)
    y_blk = rows_of(1 - y, x)
    diag_blk = rows_of(1 - y, 1 - x)

    def s0_start(u):
        rc(wsh.at[u], W.at[u, my_rows], s0s.at[u, 0], s0r.at[u, c], dev(y, x, zh, z2)).start()

        @pl.when(home)
        def _():
            pltpu.make_async_copy(wsh.at[u], W.at[u, my_rows], s0r.at[u, c]).start()

        @pl.when(jnp.logical_not(home))
        def _():
            rc(wsh.at[u], W.at[u, my_rows], s0s.at[u, 1], s0r.at[u, c], sib).start()

    def s0_wait(u):
        for j in range(2):
            wait(W.at[u, pl.ds(own_blk + j * kb, kb)], s0r.at[u, j])

    def s1_start(u):
        ref = W.at[u, pl.ds(own_blk, blk)]
        rc(ref, ref, s1s.at[u, 0], s1r.at[u, 0], xn).start()
        rc(ref, ref, s1s.at[u, 1], s1r.at[u, 1], yn).start()

    def s1_wait(u):
        wait(W.at[u, pl.ds(x_blk, blk)], s1r.at[u, 0])
        wait(W.at[u, pl.ds(y_blk, blk)], s1r.at[u, 1])

    def s2_start(u):
        ref = W.at[u, pl.ds(x_blk, kb)]
        rc(ref, ref, s2s.at[u, 1], s2r.at[u, 1], yn).start()
        ref = W.at[u, pl.ds(y_blk + kb, kb)]
        rc(ref, ref, s2s.at[u, 0], s2r.at[u, 0], xn).start()

    def s2_wait(u):
        wait(W.at[u, pl.ds(diag_blk, kb)], s2r.at[u, 1])
        wait(W.at[u, pl.ds(diag_blk + kb, kb)], s2r.at[u, 0])

    def sends_done(u):
        ref = W.at[u, pl.ds(own_blk, kb)]
        wait(ref, s0s.at[u, 0])

        @pl.when(jnp.logical_not(home))
        def _():
            wait(ref, s0s.at[u, 1])

        for j in range(2):
            wait(W.at[u, pl.ds(own_blk, blk)], s1s.at[u, j])
            wait(ref, s2s.at[u, j])

    units = 3 * layers

    def pump(u):
        s1_wait(u)
        s2_start(u)
        if u + 1 < units:
            s0_wait(u + 1)
            s1_start(u + 1)
        if u >= 1 and u + 2 < units:
            s0_start(u + 2)

    def land_start(src, dst, ss, rs):
        @pl.when(home)
        def _():
            pltpu.make_async_copy(src, dst.at[zl], rs.at[zl]).start()

        @pl.when(jnp.logical_not(home))
        def _():
            rc(src, dst.at[zl], ss.at[0], rs.at[zl], swap).start()

        rc(src, dst.at[zl], ss.at[1], rs.at[zl], swap_pair).start()

    def land_wait(src, dst, ss, rs):
        for j in range(2):
            wait(dst.at[j], rs.at[j])

    def land_sent(src, ss):
        @pl.when(jnp.logical_not(home))
        def _():
            wait(src, ss.at[0])

        wait(src, ss.at[1])

    def back_start(src, dst, ss, rs):
        @pl.when(home)
        def _():
            pltpu.make_async_copy(src, dst, rs).start()

        @pl.when(jnp.logical_not(home))
        def _():
            rc(src, dst, ss, rs, swap).start()

    def back_wait(src, dst, ss, rs):
        wait(dst, rs)

        @pl.when(jnp.logical_not(home))
        def _():
            wait(src, ss)

    def small_round(k):
        cp = rc(small, smrecv.at[k], sms.at[k], smr.at[k], (sib, xn, yn, zp, far)[k])
        cp.start()
        cp.wait()
        small[...] = (small[...].astype(F32) + smrecv[k].astype(F32)).astype(BF16)

    def sg_round(k):
        cp = rc(sg, sgrecv.at[k], sgs.at[k], sgr.at[k], (sib, xn, yn, zp, far)[k])
        cp.start()
        cp.wait()
        sg[...] = sg[...] + sgrecv[k]

    half_at = aligned(c * half, half)
    other_at = aligned((1 - c) * half, half)

    def share_start(ref, k, qi):
        part = ref.at[pl.ds(half_at + qi * slot, slot)]
        rc(part, part, cs.at[k, qi], cr.at[k, qi], sib).start()

    def share_wait(ref, k):
        for qi in range(2):
            part = ref.at[pl.ds(other_at + qi * slot, slot)]
            wait(part, cr.at[k, qi])
            wait(part, cs.at[k, qi])

    def sum_start(k, lhs, cols, u, wcols):
        par = k % 2

        def part(at, qi, then):
            rows = pl.ds(at + qi * slot, slot)

            def step(n):
                wrows = pl.ds(aligned(n * NT, NT), NT)
                then(n, dot_nt(lhs[rows, cols], W[u, wrows, wcols]))

            loop(wn, step)

        for qi in range(2):
            lrows = pl.ds(qi * slot, slot)

            def keep(n, v):
                sendA[lrows, pl.ds(aligned(n * NT, NT), NT)] = v.astype(BF16)

            part(other_at, qi, keep)
            rc(sendA.at[lrows], recvA.at[par, lrows], as_.at[k, qi], ar.at[k, qi], sib).start()
        for qi in range(2):
            lrows = pl.ds(qi * slot, slot)
            wait(recvA.at[par, lrows], ar.at[k, qi])

            def add(n, v):
                ncols = pl.ds(aligned(n * NT, NT), NT)
                sendB[lrows, ncols] = (v + recvA[par, lrows, ncols].astype(F32)).astype(BF16)

            part(half_at, qi, add)
            rc(sendB.at[lrows], recvB.at[par, lrows], bs.at[k, qi], br.at[k, qi], zp).start()

    def sum_wait(k, qi):
        wait(recvB.at[k % 2, pl.ds(qi * slot, slot)], br.at[k, qi])

    def sum_sent(k):
        for qi in range(2):
            lrows = pl.ds(qi * slot, slot)
            wait(sendA.at[lrows], as_.at[k, qi])
            wait(sendB.at[lrows], bs.at[k, qi])

    def total(k, rows):
        return sendB[rows, :].astype(F32) + recvB[k % 2, rows, :].astype(F32)

    def tiles(qi, body):
        def step(i):
            body(aligned(qi * slot + i * TILE, TILE))

        loop(slot // TILE, step)

    def norm_tile(v, at, l, which, n_ref, r_ref, a_ref):
        gain = smf[pl.ds(16 * l + 2 * which, 1), :]
        shift = smf[pl.ds(16 * l + 2 * which + 1, 1), :]
        centre = v - jnp.mean(v, axis=1, keepdims=True)
        r = lax.rsqrt(jnp.mean(centre * centre, axis=1, keepdims=True) + EPS)
        n = centre * r
        rows = pl.ds(at, TILE)
        n_ref[l, rows, :] = n.astype(BF16)
        r_ref[l, rows, :] = r
        a_ref[l, pl.ds(aligned(half_at + at, TILE), TILE), :] = (n * gain + shift).astype(BF16)

    def key_valid():
        at = lax.broadcasted_iota(jnp.int32, (1, rows_all), 1)
        quarter = jnp.zeros_like(at)
        for k in range(1, 4):
            quarter = quarter + (at >= k * slot).astype(jnp.int32)
        within = at - quarter * slot
        return jnp.logical_and(within < rows_real, quarter * rows_real + within < VALID)

    lane = lax.broadcasted_iota(jnp.int32, (1, hq), 1)
    QC = 128

    def head_mask(h):
        return jnp.logical_and(lane >= h * HD, lane < (h + 1) * HD)

    qcols = slice(0, hq)
    kcols = slice(hq, 2 * hq)
    vcols = slice(2 * hq, 3 * hq)
    qkvcols = slice(0, 3 * hq)
    ocols = slice(3 * hq, 4 * hq)
    every = slice(0, fq)

    def softmax_of(qm, keys, ok):
        s = jnp.where(ok, dot_nt(qm, keys), FAR_BELOW)
        e = jnp.exp(s - jnp.max(s, axis=1, keepdims=True))
        return e * (1.0 / jnp.sum(e, axis=1, keepdims=True))

    def attention(l):
        def step(i):
            rows = pl.ds(aligned(i * QC, QC), QC)
            qc = qkv[l, rows, qcols].astype(F32)
            keys, values = qkv[l, :, kcols], qkv[l, :, vcols]
            ok = key_valid()
            mixed = jnp.zeros((QC, hq), F32)
            for h in range(heads):
                m = head_mask(h)
                qm = jnp.where(m, qc * (HD ** -0.5), 0.0).astype(BF16)
                p = softmax_of(qm, keys, ok).astype(BF16)
                mixed = jnp.where(m, dot_nn(p, values), mixed)
            o[l, rows, :] = mixed.astype(BF16)

        loop(rows_all // QC, step)

    def attention_back(l):
        dk_acc[...] = jnp.zeros_like(dk_acc)
        dv_acc[...] = jnp.zeros_like(dv_acc)

        def step(i):
            rows = pl.ds(aligned(i * QC, QC), QC)
            qc = qkv[l, rows, qcols].astype(F32)
            oc = ob[rows, :].astype(F32)
            keys, values = qkv[l, :, kcols], qkv[l, :, vcols]
            ok = key_valid()
            dq = jnp.zeros((QC, hq), F32)
            ps, dss, qms, oms = [], [], [], []
            for h in range(heads):
                m = head_mask(h)
                qm = jnp.where(m, qc * (HD ** -0.5), 0.0).astype(BF16)
                om = jnp.where(m, oc, 0.0).astype(BF16)
                p = softmax_of(qm, keys, ok)
                dprob = dot_nt(om, values)
                inner = jnp.sum(dprob * p, axis=1, keepdims=True)
                ds = (p * (dprob - inner)).astype(BF16)
                dq = jnp.where(m, dot_nn(ds, keys), dq)
                ps.append(p.astype(BF16))
                dss.append(ds)
                qms.append(qm)
                oms.append(om)
            dqkv[rows, qcols] = (dq * (HD ** -0.5)).astype(BF16)
            dk_acc[...] += dot_tn(jnp.concatenate(dss, 0), jnp.concatenate(qms, 0))
            dv_acc[...] += dot_tn(jnp.concatenate(ps, 0), jnp.concatenate(oms, 0))

        loop(rows_all // QC, step)
        dqkv[:, kcols] = dk_acc[...].astype(BF16)
        dqkv[:, vcols] = dv_acc[...].astype(BF16)

    def rs1(u):
        ref = W.at[u, pl.ds(diag_blk, kb)]
        rc(ref, recv1.at[u, 0], g1s.at[u, 0], g1r.at[u, 0], xn).start()
        ref = W.at[u, pl.ds(diag_blk + kb, kb)]
        rc(ref, recv1.at[u, 1], g1s.at[u, 1], g1r.at[u, 1], yn).start()

    RT = 64

    def add_rows(u, at, refs, n):
        def step(i):
            off = aligned(i * RT, RT)
            rows = pl.ds(aligned(at + off, RT), RT)
            v = W[u, rows, :].astype(F32)
            for ref in refs:
                v = v + ref[pl.ds(off, RT), :].astype(F32)
            W[u, rows, :] = v.astype(BF16)

        loop(n // RT, step)

    def rs2(u):
        for j in range(2):
            wait(recv1.at[u, j], g1r.at[u, j])
            wait(recv1.at[u, j], g1s.at[u, j])
        add_rows(u, y_blk, [recv1.at[u, 0]], kb)
        ref = W.at[u, pl.ds(y_blk, blk)]
        rc(ref, recv2.at[u, 1], g2s.at[u, 1], g2r.at[u, 1], yn).start()
        add_rows(u, x_blk + kb, [recv1.at[u, 1]], kb)
        ref = W.at[u, pl.ds(x_blk, blk)]
        rc(ref, recv2.at[u, 0], g2s.at[u, 0], g2r.at[u, 0], xn).start()

    def rs3(u):
        for j in range(2):
            wait(recv2.at[u, j], g2r.at[u, j])
            wait(recv2.at[u, j], g2s.at[u, j])
        add_rows(u, own_blk, [recv2.at[u, 0], recv2.at[u, 1]], blk)

        @pl.when(home)
        def _():
            ref = W.at[u, pl.ds(aligned(own_blk + (1 - c) * kb, kb), kb)]
            rc(ref, recv4.at[u, 0], g4s.at[u, 0], g4r.at[u, 0], sib).start()
            ref = W.at[u, pl.ds(aligned(own_blk + c * kb, kb), kb)]
            pltpu.make_async_copy(ref, recv4.at[u, 0], g4r.at[u, 0]).start()

        @pl.when(jnp.logical_not(home))
        def _():
            for j in range(2):
                ref = W.at[u, pl.ds(own_blk + j * kb, kb)]
                rc(ref, recv4.at[u, 1], g4s.at[u, j], g4r.at[u, 1], dev(y, x, j, z2)).start()

    def rs4(u):
        for j in range(2):
            wait(recv4.at[u, j], g4r.at[u, j])
        wait(recv4.at[u, 0], g4s.at[u, 0])

        @pl.when(jnp.logical_not(home))
        def _():
            wait(recv4.at[u, 0], g4s.at[u, 1])

        def step(i):
            rows = pl.ds(aligned(i * RT, RT), RT)
            gw_ref[u, rows, :] = recv4[u, 0, rows, :].astype(F32) + recv4[u, 1, rows, :].astype(F32)

        loop(kb // RT, step)

    def project(l):
        def step(i):
            rows = pl.ds(aligned(i * half, half), half)
            for j in range(3):
                cols = slice(j * hq, (j + 1) * hq)
                v = dot_nn(a1[l, rows, :], W[3 * l, :, cols])
                qkv[l, rows, cols] = (v + qb[8 * l + j:8 * l + j + 1, :]).astype(BF16)

        loop(2, step)

    def expand(l):
        bias_row = pl.ds(16 * l + 8 + q, 1)

        def step(j):
            cols = pl.ds(aligned(j * NT, NT), NT)
            bias = smf[bias_row, cols]

            for i in range(2):
                rows = slice(i * half, (i + 1) * half)
                u = dot_nn(a2[l, rows, :], W[3 * l + 1, :, cols]) + bias
                phi = 0.5 * (1.0 + lax.erf(u * ROOT_HALF))
                act[l, rows, cols] = (u * phi).astype(BF16)
                density = INV_ROOT_2PI * jnp.exp(-0.5 * u * u)
                dgl[l, rows, cols] = (phi + u * density).astype(BF16)

        loop(fq // NT, step)

    def expand_back(l):
        bias_row = pl.ds(16 * l + 8 + q, 1)

        def step(j):
            cols = pl.ds(aligned(j * NT, NT), NT)
            sums = jnp.zeros((1, NT), F32)
            for i in range(2):
                rows = slice(i * half, (i + 1) * half)
                v = dot_nn(gb[rows, :], W[3 * l + 2, :, cols]) * dgl[l, rows, cols].astype(F32)
                low = v.astype(BF16)
                ub[rows, cols] = low
                sums = sums + jnp.sum(low.astype(F32), axis=0, keepdims=True)
            sg[bias_row, cols] = sums

        loop(fq // NT, step)

    def weight_grad(u, lhs, rhs, cols):
        def step(t):
            rows = pl.ds(aligned(t * NT, NT), NT)
            W[u, rows, cols] = dot_tn(lhs[:, rows], rhs[...]).astype(BF16)

        loop(wn, step)

    def acc_add(j, v):
        acc[j] += jnp.sum(v.reshape(TILE // 8, 8, width), axis=0)

    once = (zl == 0).astype(F32)

    def acc_out(j, row):
        sg[row:row + 1, :] = jnp.sum(acc[j], axis=0, keepdims=True) * once

    def norm_back(k, l, which, n_ref, r_ref, low_ref, low_k):
        acc[...] = jnp.zeros_like(acc)
        for qi in range(2):
            sum_wait(k, qi)

            def body(at):
                rows = pl.ds(at, TILE)
                da = total(k, rows)
                n = n_ref[l, rows, :].astype(F32)
                e = da * smf[pl.ds(16 * l + 2 * which, 1), :]
                inner = jnp.mean(e * n, axis=1, keepdims=True)
                middle = jnp.mean(e, axis=1, keepdims=True)
                g = gs[rows, :] + r_ref[l, rows, :] * (e - middle - n * inner)
                gs[rows, :] = g
                acc_add(0, da * n)
                acc_add(1, da)
                acc_add(2, g)
                if low_ref is not None:
                    low_ref[pl.ds(aligned(half_at + at, TILE), TILE), :] = g.astype(BF16)

            tiles(qi, body)
            if low_ref is not None:
                share_start(low_ref, low_k, qi)
        sum_sent(k)
        acc_out(0, 16 * l + 2 * which)
        acc_out(1, 16 * l + 2 * which + 1)
        if which == 1:
            acc_out(2, 16 * l + 4)
        elif l > 0:
            acc_out(2, 16 * (l - 1) + 5)

    s0_start(0)
    land_start(tok, tokst, tks, tkr)
    small[...] = small_in[...]
    small_round(0)
    s0_wait(0)
    s1_start(0)
    s0_start(1)
    s0_start(2)
    land_start(cot, cotst, cts, ctr)
    for k in range(1, 5):
        small_round(k)
    smf[...] = small[...].astype(F32)
    sg[...] = jnp.zeros_like(sg)
    qb[...] = jnp.zeros_like(qb)
    mine = pl.ds(aligned(q * hq, hq), hq)
    for l in range(layers):
        for j, row in ((0, 6), (2, 7)):
            qb[8 * l + j:8 * l + j + 1, :] = smf[16 * l + row:16 * l + row + 1, mine]

    land_wait(tok, tokst, tks, tkr)
    for qi in range(2):
        def first(at, qi=qi):
            v = tokst[qi, pl.ds(aligned(at - qi * slot, TILE), TILE), :].astype(F32)
            xs[pl.ds(at, TILE), :] = v
            norm_tile(v, at, 0, 0, n1, r1, a1)

        tiles(qi, first)
        share_start(a1.at[0], 0, qi)
    pump(0)

    def stream_step(k, l_bias, row, l, which, n_ref, r_ref, a_ref, share_k):
        for qi in range(2):
            sum_wait(k, qi)

            def body(at):
                rows = pl.ds(at, TILE)
                v = xs[rows, :] + total(k, rows) + smf[pl.ds(16 * l_bias + row, 1), :]
                xs[rows, :] = v
                norm_tile(v, at, l, which, n_ref, r_ref, a_ref)

            tiles(qi, body)
            share_start(a_ref.at[l], share_k, qi)
        sum_sent(k)

    for l in range(layers):
        s2_wait(3 * l)
        share_wait(a1.at[l], 2 * l)
        project(l)
        attention(l)
        pump(3 * l + 1)
        sum_start(2 * l, o.at[l], slice(0, hq), 3 * l, ocols)
        if l == 0:
            land_wait(cot, cotst, cts, ctr)
            acc[...] = jnp.zeros_like(acc)
            for qi in range(2):
                def first_back(at, qi=qi):
                    low = cotst[qi, pl.ds(aligned(at - qi * slot, TILE), TILE), :]
                    gs[pl.ds(at, TILE), :] = low.astype(F32)
                    gb[pl.ds(aligned(half_at + at, TILE), TILE), :] = low
                    acc_add(2, low.astype(F32))

                tiles(qi, first_back)
                share_start(gb, 2 * layers, qi)
            acc_out(2, 16 * (layers - 1) + 5)
        stream_step(2 * l, l, 4, l, 1, n2, r2, a2, 2 * l + 1)
        pump(3 * l + 2)
        s2_wait(3 * l + 1)
        share_wait(a2.at[l], 2 * l + 1)
        expand(l)
        s2_wait(3 * l + 2)
        sum_start(2 * l + 1, act.at[l], every, 3 * l + 2, every)
        if l + 1 < layers:
            pump(3 * l + 3)
            stream_step(2 * l + 1, l, 5, l + 1, 0, n1, r1, a1, 2 * l + 2)

    share_wait(gb, 2 * layers)
    k_sum = 2 * layers
    k_share = 2 * layers + 1
    for l in reversed(range(layers)):
        top = l == layers - 1
        if not top:
            share_wait(gb, k_share - 1)
        expand_back(l)
        if top:
            last = k_sum - 1
            for qi in range(2):
                sum_wait(last, qi)

            def finish(i):
                at = aligned(zl * slot + i * TILE, TILE)
                rows = pl.ds(at, TILE)
                v = xs[rows, :] + total(last, rows) + smf[pl.ds(16 * l + 5, 1), :]
                igst[pl.ds(aligned(i * TILE, TILE), TILE), :] = v.astype(BF16)

            loop(slot // TILE, finish)
            sum_sent(last)
            back_start(igst, out_ref, oss.at[0], osr.at[0])
        sum_start(k_sum, ub, every, 3 * l + 1, every)
        for u in (3 * l + 2, 3 * l + 1):
            sends_done(u)
        weight_grad(3 * l + 2, gb, act.at[l], every)
        rs1(3 * l + 2)
        weight_grad(3 * l + 1, a2.at[l], ub, every)
        rs1(3 * l + 1)
        if not top:
            rs3(3 * l + 3)
            rs4(3 * l + 4)
        norm_back(k_sum, l, 1, n2, r2, hb, k_share)
        rs2(3 * l + 2)
        share_wait(hb, k_share)

        def mix_back(i):
            rows = pl.ds(aligned(i * half, half), half)
            ob[rows, :] = dot_nn(hb[rows, :], W[3 * l, :, ocols]).astype(BF16)

        loop(2, mix_back)
        rs2(3 * l + 1)
        attention_back(l)
        sum_start(k_sum + 1, dqkv, qkvcols, 3 * l, qkvcols)
        for row, cols in ((6, qcols), (7, vcols)):
            sg[16 * l + row:16 * l + row + 1, mine] = jnp.sum(
                dqkv[:, cols].astype(F32), axis=0, keepdims=True)
        sends_done(3 * l)
        weight_grad(3 * l, a1.at[l], dqkv, qkvcols)
        weight_grad(3 * l, hb, o.at[l], ocols)
        rs1(3 * l)
        rs3(3 * l + 2)
        if top:
            back_wait(igst, out_ref, oss.at[0], osr.at[0])
        else:
            rs4(3 * l + 3)
        if l > 0:
            norm_back(k_sum + 1, l, 0, n1, r1, gb, k_share + 1)
        else:
            norm_back(k_sum + 1, l, 0, n1, r1, None, None)
        rs2(3 * l)
        rs3(3 * l + 1)
        if l > 0:
            rs4(3 * l + 2)
        k_sum += 2
        k_share += 2

    def finish_grad(i):
        at = aligned(zl * slot + i * TILE, TILE)
        igst[pl.ds(aligned(i * TILE, TILE), TILE), :] = gs[pl.ds(at, TILE), :].astype(BF16)

    loop(slot // TILE, finish_grad)
    back_start(igst, igrecv, oss.at[1], osr.at[1])
    for k in range(3):
        sg_round(k)
    rs3(0)
    for k in range(3, 5):
        sg_round(k)
    rs4(2)
    rs4(1)
    back_wait(igst, igrecv, oss.at[1], osr.at[1])
    ig_ref[...] = igrecv[...].astype(F32)
    rs4(0)
    land_sent(tok, tks)
    land_sent(cot, cts)


def shards(tokens, cotangent, image_mask, qkv_weight, out_weight, up_weight, down_weight,
           qv_bias, up_bias, out_bias, down_bias, attn_gain, attn_shift, mlp_gain, mlp_shift):
    images_here, rows_real, width = tokens.shape
    layers = qkv_weight.shape[0]
    hq = qkv_weight.shape[3]
    fq = up_weight.shape[2]
    lanes = lax.axis_size("tensor")
    groups = lax.axis_size("dp") // 8
    assert images_here == 1 and lanes == 4 and width == fq == 4 * hq
    kb = width // 8
    slot = -(-rows_real // TILE) * TILE
    half = 2 * slot
    rows_all = 4 * slot
    units = 3 * layers
    dp = lax.axis_index("dp")
    z = lax.axis_index("tensor")
    d8 = dp % 8
    first = d8 == 0

    position = z * rows_real + jnp.arange(rows_real)
    keep = (position < VALID).astype(BF16)[:, None] * image_mask.astype(BF16)[0]
    pad = ((0, slot - rows_real), (0, 0))
    tok = jnp.pad(tokens[0], pad)
    cot = jnp.pad(cotangent[0] * keep, pad)

    here = qkv_weight.shape[1]
    wsh = jnp.stack([
        jnp.concatenate([qkv_weight.reshape(layers, here, 3 * hq), out_weight], axis=2),
        up_weight, down_weight], axis=1).reshape(units, here, fq)
    if groups > 1:
        wsh = lax.all_gather(wsh, "dp", axis=1, tiled=True)
        wsh = lax.dynamic_slice_in_dim(wsh, d8 * kb, kb, 1)

    shard = dp * lanes + z
    piece = attn_gain.shape[1]

    def window(values, at):
        wide = jnp.zeros((values.shape[0], width), BF16)
        return lax.dynamic_update_slice(wide, values, (0, at))

    ups = up_bias.shape[1]
    up_at = shard * ups
    rows = []
    for l in range(layers):
        six = jnp.stack([attn_gain[l], attn_shift[l], mlp_gain[l], mlp_shift[l],
                         out_bias[l], down_bias[l], qv_bias[l, 0], qv_bias[l, 1]])
        rows.append(window(six, shard * piece))
        up_row = window(up_bias[l][None], up_at % width)
        rows.append(jnp.where(jnp.arange(4)[:, None] == up_at // width, up_row, 0))
        rows.append(jnp.zeros((4, width), BF16))
    small_in = jnp.concatenate(rows)
    if groups > 1:
        small_in = lax.psum(small_in, "dp") * first.astype(BF16)

    out_shapes = (
        jax.ShapeDtypeStruct((slot, width), BF16),
        jax.ShapeDtypeStruct((slot, width), F32),
        jax.ShapeDtypeStruct((units, kb, fq), F32),
        jax.ShapeDtypeStruct((16 * layers, width), F32),
    )
    V = pltpu.VMEM
    D = lambda *s: pltpu.SemaphoreType.DMA(s)
    sums, shares = 4 * layers, 4 * layers
    scratch = [
        V((units, width, fq), BF16),
        V((half, width), F32), V((half, width), F32),
        V((layers, half, width), BF16), V((layers, half, width), BF16),
        V((layers, half, 1), F32), V((layers, half, 1), F32),
        V((layers, rows_all, width), BF16), V((layers, rows_all, width), BF16),
        V((layers, rows_all, 3 * hq), BF16), V((layers, rows_all, hq), BF16),
        V((layers, rows_all, fq), BF16), V((layers, rows_all, fq), BF16),
        V((rows_all, width), BF16), V((rows_all, width), BF16),
        V((rows_all, fq), BF16), V((rows_all, hq), BF16), V((rows_all, 3 * hq), BF16),
        V((rows_all, hq), F32), V((rows_all, hq), F32), V((3, 8, width), F32),
        V((half, width), BF16), V((2, half, width), BF16),
        V((half, width), BF16), V((2, half, width), BF16),
        V((2, slot, width), BF16), V((2, slot, width), BF16),
        V((slot, width), BF16), V((slot, width), BF16),
        V((16 * layers, width), BF16), V((5, 16 * layers, width), BF16),
        V((16 * layers, width), F32), V((8 * layers, hq), F32),
        V((5, 16 * layers, width), F32),
        V((units, 2, kb, fq), BF16), V((units, 2, 2 * kb, fq), BF16), V((units, 2, kb, fq), BF16),
        D(units, 2), D(units, 2), D(units, 2), D(units, 2), D(units, 2), D(units, 2),
        D(sums, 2), D(sums, 2), D(sums, 2), D(sums, 2), D(shares, 2), D(shares, 2),
        D(2), D(2), D(2), D(2), D(2), D(2), D(5), D(5), D(5), D(5),
        D(units, 2), D(units, 2), D(units, 2), D(units, 2), D(units, 2), D(units, 2),
    ]
    any_spec = pl.BlockSpec(memory_space=pl.ANY)
    vmem_spec = pl.BlockSpec(memory_space=pltpu.VMEM)
    out, ig, gw, sg = pl.pallas_call(
        functools.partial(kernel, layers, rows_real),
        out_shape=out_shapes,
        in_specs=[any_spec, any_spec, any_spec, vmem_spec],
        out_specs=(any_spec, vmem_spec, vmem_spec, vmem_spec),
        scratch_shapes=scratch,
        compiler_params=pltpu.CompilerParams(
            collective_id=0, has_side_effects=True, vmem_limit_bytes=63 * 2 ** 20),
        cost_estimate=pl.CostEstimate(
            flops=int(1e11), bytes_accessed=int(1e8), transcendentals=0),
    )(tok, cot, wsh, small_in)

    if groups > 1:
        wide = lax.dynamic_update_slice_in_dim(
            jnp.zeros((units, width, fq), F32), gw, d8 * kb, 1)
        gw = lax.psum_scatter(wide, "dp", scatter_dimension=1, tiled=True)
        sg = lax.psum(sg * first.astype(F32), "dp")
    gw = gw.reshape(layers, 3, here, fq)
    sg = sg.reshape(layers, 16, width)
    mine = lax.dynamic_slice_in_dim(sg[:, :8], shard * piece, piece, 2)
    ups_grad = lax.dynamic_slice_in_dim(sg[:, 8:12].reshape(layers, 4 * width), up_at, ups, 1)
    return (
        out[:rows_real][None],
        ig[:rows_real][None],
        gw[:, 0, :, :3 * hq].reshape(layers, here, 3, hq),
        gw[:, 0, :, 3 * hq:],
        gw[:, 1],
        gw[:, 2],
        mine[:, 6:8],
        ups_grad,
        mine[:, 4],
        mine[:, 5],
        mine[:, 0],
        mine[:, 1],
        mine[:, 2],
        mine[:, 3],
    )


def solution(mesh):
    both = ("dp", "tensor")
    rows = P("dp", "tensor", None)
    cols = P(None, "dp", "tensor")
    vec = P(None, both)
    return jax.shard_map(
        shards,
        mesh=mesh,
        in_specs=(rows, rows, P("dp"), P(None, "dp", None, "tensor"), cols, cols, cols,
                  P(None, None, both), vec, vec, vec, vec, vec, vec, vec),
        out_specs=(rows, rows, P(None, "dp", None, "tensor"), cols, cols, cols,
                   P(None, None, both), vec, vec, vec, vec, vec, vec, vec),
        check_vma=False,
    )
```

```python
import functools

import jax
import jax.numpy as jnp
from jax import lax
from jax.experimental import pallas as pl
from jax.experimental.pallas import tpu as pltpu
from jax.sharding import PartitionSpec as P

HD = 64
VALID = 577
EPS = 1e-06
ROOT_HALF = 0.7071067811865476
INV_ROOT_2PI = 0.3989422804014327
FAR_BELOW = -1e30
MESH = pl.DeviceIdType.MESH
F32 = jnp.float32
BF16 = jnp.bfloat16
TILE = 32
NT = 256


def dot_nn(a, b):
    return lax.dot_general(a, b, (((1,), (0,)), ((), ())), preferred_element_type=F32)


def dot_nt(a, b):
    return lax.dot_general(a, b, (((1,), (1,)), ((), ())), preferred_element_type=F32)


def dot_tn(a, b):
    return lax.dot_general(a, b, (((0,), (0,)), ((), ())), preferred_element_type=F32)


def loop(n, body):
    def step(i, carry):
        body(i)
        return carry

    lax.fori_loop(0, n, step, 0)


def aligned(v, m):
    return pl.multiple_of(v, m)


def kernel(
    layers, rows_real,
    tok, cot, wsh, small_in,
    out_ref, ig_ref, gqkv, gout, gup, gdown, sg,
    W, xs, gs, n1, n2, r1, r2, a1, a2, qkv, o, act, dgl,
    gb, hb, ub, ob, dqkv, dk_acc, dv_acc, acc, kmask,
    own, sendA, recvA, sendB, recvB, tokst, cotst, igrecv,
    small, smrecv, smf, qb, sgrecv,
    recv1, recv2, recv4,
    s0s, s0r, s1s, s1r, s2s, s2r,
    as_, ar, bs, br, cs, cr,
    tks, tkr, cts, ctr, oss, osr, sms, smr, sgs, sgr,
    g1s, g1r, g2s, g2r, g4s, g4r, stage, sts,
):
    width = xs.shape[1]
    half = xs.shape[0]
    slot = half // 2
    rows_all = 2 * half
    kb = wsh.shape[1]
    blk = 2 * kb
    hq = o.shape[2]
    fq = act.shape[2]
    heads = hq // HD
    wn = width // NT

    dp = lax.axis_index("dp")
    z = lax.axis_index("tensor")
    base = (dp // 8) * 8
    d8 = dp % 8
    y, x, c = d8 // 4, (d8 // 2) % 2, d8 % 2
    zh, zl = z // 2, z % 2
    q = zl + 2 * c
    z2 = (z + 2) % 4
    home = c == zh

    def dev(yy, xx, cc, zz):
        return (base + yy * 4 + xx * 2 + cc, zz)

    sib = dev(y, x, 1 - c, z)
    xn = dev(y, 1 - x, c, z)
    yn = dev(1 - y, x, c, z)
    zp = dev(y, x, c, z + 1 - 2 * zl)
    far = dev(y, x, c, z2)
    swap = dev(y, x, zh, 2 * c + zl)

    def rc(src, dst, ss, rs, to):
        return pltpu.make_async_remote_copy(
            src_ref=src, dst_ref=dst, send_sem=ss, recv_sem=rs,
            device_id=to, device_id_type=MESH)

    def wait(ref, sem):
        pltpu.make_async_copy(ref, ref, sem).wait()

    barrier = pltpu.get_barrier_semaphore()
    greet = [xn, yn, sib]
    for k in range(1, 4):
        for cc in range(2):
            greet.append(dev(y, x, cc, (z + k) % 4))
    for to in greet:
        pl.semaphore_signal(barrier, inc=1, device_id=to, device_id_type=MESH)
    pl.semaphore_wait(barrier, len(greet))

    def rows_of(yy, xx):
        return aligned((2 * yy + xx) * blk, blk)

    my_rows = pl.ds(aligned(d8 * kb, kb), kb)
    own_blk = rows_of(y, x)
    x_blk = rows_of(y, 1 - x)
    y_blk = rows_of(1 - y, x)
    diag_blk = rows_of(1 - y, 1 - x)

    def s0_start(u):
        rc(wsh.at[u], W.at[u, my_rows], s0s.at[u, 0], s0r.at[u, c], dev(y, x, zh, z2)).start()

        @pl.when(home)
        def _():
            pltpu.make_async_copy(wsh.at[u], W.at[u, my_rows], s0r.at[u, c]).start()

        @pl.when(jnp.logical_not(home))
        def _():
            rc(wsh.at[u], W.at[u, my_rows], s0s.at[u, 1], s0r.at[u, c], sib).start()

    def s0_wait(u):
        for j in range(2):
            wait(W.at[u, pl.ds(own_blk + j * kb, kb)], s0r.at[u, j])

    def s1_start(u):
        ref = W.at[u, pl.ds(own_blk, blk)]
        rc(ref, ref, s1s.at[u, 0], s1r.at[u, 0], xn).start()
        rc(ref, ref, s1s.at[u, 1], s1r.at[u, 1], yn).start()

    def s1_wait(u):
        wait(W.at[u, pl.ds(x_blk, blk)], s1r.at[u, 0])
        wait(W.at[u, pl.ds(y_blk, blk)], s1r.at[u, 1])

    def s2_start(u):
        ref = W.at[u, pl.ds(x_blk, kb)]
        rc(ref, ref, s2s.at[u, 1], s2r.at[u, 1], yn).start()
        ref = W.at[u, pl.ds(y_blk + kb, kb)]
        rc(ref, ref, s2s.at[u, 0], s2r.at[u, 0], xn).start()

    def s2_wait(u):
        wait(W.at[u, pl.ds(diag_blk, kb)], s2r.at[u, 1])
        wait(W.at[u, pl.ds(diag_blk + kb, kb)], s2r.at[u, 0])

    def sends_done(u):
        ref = W.at[u, pl.ds(own_blk, kb)]
        wait(ref, s0s.at[u, 0])

        @pl.when(jnp.logical_not(home))
        def _():
            wait(ref, s0s.at[u, 1])

        for j in range(2):
            wait(W.at[u, pl.ds(own_blk, blk)], s1s.at[u, j])
            wait(ref, s2s.at[u, j])

    units = 3 * layers

    def pump(u):
        s1_wait(u)
        s2_start(u)
        ahead = u + 1 if u == 0 else u + 2
        if ahead < units:
            s0_wait(ahead)
            s1_start(ahead)

    def land_start(src, dst, ss, rs):
        @pl.when(home)
        def _():
            pltpu.make_async_copy(src, dst.at[zl], rs.at[zl]).start()

        @pl.when(jnp.logical_not(home))
        def _():
            rc(src, dst.at[zl], ss.at[0], rs.at[zl], swap).start()

    def land_pass(src, dst, ss, rs):
        wait(dst.at[zl], rs.at[zl])
        rc(dst.at[zl], dst.at[zl], ss.at[1], rs.at[zl], zp).start()

    def land_wait(src, dst, ss, rs):
        wait(dst.at[1 - zl], rs.at[1 - zl])

    def land_sent(src, ss):
        @pl.when(jnp.logical_not(home))
        def _():
            wait(src, ss.at[0])

        wait(src, ss.at[1])

    def back_start(src, dst, ss, rs):
        @pl.when(home)
        def _():
            pltpu.make_async_copy(src, dst, rs).start()

        @pl.when(jnp.logical_not(home))
        def _():
            rc(src, dst, ss, rs, swap).start()

    def back_wait(src, dst, ss, rs):
        wait(dst, rs)

        @pl.when(jnp.logical_not(home))
        def _():
            wait(src, ss)

    def small_round(k):
        cp = rc(small, smrecv.at[k], sms.at[k], smr.at[k], (sib, xn, yn, zp, far)[k])
        cp.start()
        cp.wait()
        small[...] = (small[...].astype(F32) + smrecv[k].astype(F32)).astype(BF16)

    def sg_round(k):
        cp = rc(sg, sgrecv.at[k], sgs.at[k], sgr.at[k], (sib, xn, yn, zp, far)[k])
        cp.start()
        cp.wait()
        sg[...] = sg[...] + sgrecv[k]

    def round_rows(r):
        return pl.ds(r * half, half)

    def slot_at(r, h):
        return aligned(r * half + h * slot, slot)

    def share_start(ref, k, r):
        part = ref.at[pl.ds(slot_at(r, c), slot)]
        rc(part, part, cs.at[k, r], cr.at[k, r], sib).start()

    def share_wait(ref, k, r):
        part = ref.at[pl.ds(slot_at(r, 1 - c), slot)]
        wait(part, cr.at[k, r])
        wait(part, cs.at[k, r])

    last_out = 2 * layers - 1
    last_sum = 4 * layers - 1

    def bank(k):
        return 2 if k == last_out else (k + (k > last_out)) % 2

    def sum_part(k, r, lhs, cols, u, wcols):
        def step(n):
            ncols = pl.ds(aligned(n * NT, NT), NT)
            rows = jnp.concatenate(
                [lhs[pl.ds(slot_at(r, c), slot), cols], lhs[pl.ds(slot_at(r, 1 - c), slot), cols]], 0)
            v = dot_nt(rows, W[u, ncols, wcols])
            own[r, :, ncols] = v[:slot]
            sendA[r, :, ncols] = v[slot:].astype(BF16)

        loop(wn, step)
        rc(sendA.at[r], recvA.at[k % 2, r], as_.at[k, r], ar.at[k, r], sib).start()

    def sum_mid(k, r):
        wait(recvA.at[k % 2, r], ar.at[k, r])
        wait(sendA.at[r], as_.at[k, r])

        def step(i):
            rows = pl.ds(aligned(i * TILE, TILE), TILE)
            sendB[bank(k), r, rows, :] = (own[r, rows, :] + recvA[k % 2, r, rows, :].astype(F32)).astype(BF16)

        loop(slot // TILE, step)
        if k not in (last_out, last_sum):
            rc(sendB.at[bank(k), r], recvB.at[bank(k), r], bs.at[k, r], br.at[k, r], zp).start()

    def sum_only(k):
        rc(sendB.at[bank(k), 1 - zl], recvB.at[bank(k), 1 - zl], bs.at[k, 0], br.at[k, 0], zp).start()

    def sum_wait(k, r):
        wait(recvB.at[bank(k), r], br.at[k, r])

    def sum_sent(k, r):
        wait(sendB.at[bank(k), r], bs.at[k, r])

    def total(k, r, rows):
        return sendB[bank(k), r, rows, :].astype(F32) + recvB[bank(k), r, rows, :].astype(F32)

    def tiles(body):
        def step(i):
            body(aligned(i * TILE, TILE))

        loop(slot // TILE, step)

    def stream_rows(r, at):
        return pl.ds(aligned(r * slot + at, TILE), TILE)

    def full_rows(r, at):
        return pl.ds(aligned(slot_at(r, c) + at, TILE), TILE)

    def norm_tile(v, r, at, l, which, n_ref, r_ref, a_ref):
        gain = smf[pl.ds(16 * l + 2 * which, 1), :]
        shift = smf[pl.ds(16 * l + 2 * which + 1, 1), :]
        centre = v - jnp.mean(v, axis=1, keepdims=True)
        inv = lax.rsqrt(jnp.mean(centre * centre, axis=1, keepdims=True) + EPS)
        n = centre * inv
        rows = stream_rows(r, at)
        n_ref[l, rows, :] = n.astype(BF16)
        r_ref[l, rows, :] = inv
        a_ref[l, full_rows(r, at), :] = (n * gain + shift).astype(BF16)

    lane = lax.broadcasted_iota(jnp.int32, (1, hq), 1)
    QC = half

    def head_mask(h):
        return jnp.logical_and(lane >= h * HD, lane < (h + 1) * HD)

    def spare(h):
        return lane == (hq - 1 if h < heads - 1 else 0)

    qcols = slice(0, hq)
    kcols = slice(hq, 2 * hq)
    vcols = slice(2 * hq, 3 * hq)
    qkvcols = slice(0, 3 * hq)
    ocols = slice(3 * hq, 4 * hq)
    every = slice(0, fq)

    def mask_keys(l):
        for s in range(4):
            r, h = s // 2, s % 2
            rows = pl.ds(s * slot, slot)
            within = lax.broadcasted_iota(jnp.int32, (slot, 1), 0)
            valid = jnp.logical_and(within < rows_real, (2 * h + r) * rows_real + within < VALID)
            low = jnp.where(valid, 0.0, FAR_BELOW)
            keys = qkv[l, rows, kcols].astype(F32)
            for j, h in ((0, 0), (1, heads - 1)):
                kmask[j, rows, :] = jnp.where(spare(h), low, keys).astype(BF16)

    def softmax_of(qm, h):
        s = dot_nt(jnp.where(spare(h), 1.0, qm).astype(BF16), kmask[0 if h < heads - 1 else 1])
        e = jnp.exp(s - jnp.max(s, axis=1, keepdims=True))
        return e * (1.0 / jnp.sum(e, axis=1, keepdims=True))

    def attention(l, r, which):
        rows = round_rows(r)
        qc = qkv[l, rows, qcols].astype(F32)
        values = qkv[l, :, vcols]
        for h in which:
            m = head_mask(h)
            qm = jnp.where(m, qc * (HD ** -0.5), 0.0)
            p = softmax_of(qm, h).astype(BF16)
            mixed = dot_nn(p, values)
            pair = slice(h // 2 * 2 * HD, (h // 2 + 1) * 2 * HD)
            old = o[l, rows, pair]
            o[l, rows, pair] = jnp.where(m[:, pair], mixed[:, pair], old.astype(F32)).astype(BF16)

    def attention_back(l, r):
        rows = round_rows(r)
        qc = qkv[l, rows, qcols].astype(F32)
        oc = ob[rows, :].astype(F32)
        keys, values = qkv[l, :, kcols], qkv[l, :, vcols]
        dq = jnp.zeros((QC, hq), F32)
        for h in range(heads):
            m = head_mask(h)
            qm = jnp.where(m, qc * (HD ** -0.5), 0.0)
            om = jnp.where(m, oc, 0.0).astype(BF16)
            p = softmax_of(qm, h)
            dprob = dot_nt(om, values)
            inner = jnp.sum(dprob * p, axis=1, keepdims=True)
            ds = (p * (dprob - inner)).astype(BF16)
            dq = jnp.where(m, dot_nn(ds, keys), dq)
            dk = dot_tn(ds, qm.astype(BF16))
            dv = dot_tn(p.astype(BF16), om)
            if r == 0 and h == 0:
                dk_acc[...] = dk
                dv_acc[...] = dv
            else:
                dk_acc[...] += dk
                dv_acc[...] += dv
        dqkv[rows, qcols] = (dq * (HD ** -0.5)).astype(BF16)
        if r == 1:
            dqkv[:, kcols] = dk_acc[...].astype(BF16)
            dqkv[:, vcols] = dv_acc[...].astype(BF16)

    def rs1(u):
        ref = W.at[u, pl.ds(diag_blk, kb)]
        rc(ref, recv1.at[u, 0], g1s.at[u, 0], g1r.at[u, 0], xn).start()
        ref = W.at[u, pl.ds(diag_blk + kb, kb)]
        rc(ref, recv1.at[u, 1], g1s.at[u, 1], g1r.at[u, 1], yn).start()

    RT = 64

    def add_rows(u, at, refs, n):
        def step(i):
            off = aligned(i * RT, RT)
            rows = pl.ds(aligned(at + off, RT), RT)
            v = W[u, rows, :].astype(F32)
            for ref in refs:
                v = v + ref[pl.ds(off, RT), :].astype(F32)
            W[u, rows, :] = v.astype(BF16)

        loop(n // RT, step)

    def rs2(u):
        for j in range(2):
            wait(recv1.at[u, j], g1r.at[u, j])
            wait(recv1.at[u, j], g1s.at[u, j])
        add_rows(u, y_blk, [recv1.at[u, 0]], kb)
        ref = W.at[u, pl.ds(y_blk, blk)]
        rc(ref, recv2.at[u, 1], g2s.at[u, 1], g2r.at[u, 1], yn).start()
        add_rows(u, x_blk + kb, [recv1.at[u, 1]], kb)
        ref = W.at[u, pl.ds(x_blk, blk)]
        rc(ref, recv2.at[u, 0], g2s.at[u, 0], g2r.at[u, 0], xn).start()

    def rs3(u):
        for j in range(2):
            wait(recv2.at[u, j], g2r.at[u, j])
            wait(recv2.at[u, j], g2s.at[u, j])
        add_rows(u, own_blk, [recv2.at[u, 0], recv2.at[u, 1]], blk)

        @pl.when(home)
        def _():
            ref = W.at[u, pl.ds(aligned(own_blk + (1 - c) * kb, kb), kb)]
            rc(ref, recv4.at[u, 0], g4s.at[u, 0], g4r.at[u, 0], sib).start()
            ref = W.at[u, pl.ds(aligned(own_blk + c * kb, kb), kb)]
            pltpu.make_async_copy(ref, recv4.at[u, 0], g4r.at[u, 0]).start()

        @pl.when(jnp.logical_not(home))
        def _():
            for j in range(2):
                ref = W.at[u, pl.ds(own_blk + j * kb, kb)]
                rc(ref, recv4.at[u, 1], g4s.at[u, j], g4r.at[u, 1], dev(y, x, j, z2)).start()

    def rs4(u):
        for j in range(2):
            wait(recv4.at[u, j], g4r.at[u, j])
        wait(recv4.at[u, 0], g4s.at[u, 0])

        @pl.when(jnp.logical_not(home))
        def _():
            wait(recv4.at[u, 0], g4s.at[u, 1])

        slot_of = stored.index(None) if None in stored else len(order) % 2
        if stored[slot_of] is not None:
            store_wait(slot_of)

        def step(i):
            rows = pl.ds(aligned(i * RT, RT), RT)
            stage[slot_of, rows, :] = (recv4[u, 0, rows, :].astype(F32)
                                       + recv4[u, 1, rows, :].astype(F32))

        loop(kb // RT, step)
        stored[slot_of] = u
        order.append(u)
        for src, dst, sem in stores(slot_of):
            pltpu.make_async_copy(src, dst, sem).start()

    stored, order = [None, None], []

    def stores(slot_of):
        u = stored[slot_of]
        l, part = u // 3, u % 3
        if part:
            return [(stage.at[slot_of], (gup, gdown)[part - 1].at[l], sts.at[slot_of, 0])]
        return [(stage.at[slot_of, :, qkvcols], gqkv.at[l], sts.at[slot_of, 0]),
                (stage.at[slot_of, :, ocols], gout.at[l], sts.at[slot_of, 1])]

    def store_wait(slot_of):
        for src, dst, sem in stores(slot_of):
            pltpu.make_async_copy(src, dst, sem).wait()

    def project(l, r):
        rows = round_rows(r)
        for j in range(3):
            cols = slice(j * hq, (j + 1) * hq)
            v = dot_nn(a1[l, rows, :], W[3 * l, :, cols])
            qkv[l, rows, cols] = (v + qb[8 * l + j:8 * l + j + 1, :]).astype(BF16)

    def expand(l, r):
        rows = round_rows(r)
        bias_row = pl.ds(16 * l + 8 + q, 1)

        def step(j):
            cols = pl.ds(aligned(j * NT, NT), NT)
            u = dot_nn(a2[l, rows, :], W[3 * l + 1, :, cols]) + smf[bias_row, cols]
            phi = 0.5 * (1.0 + lax.erf(u * ROOT_HALF))
            act[l, rows, cols] = (u * phi).astype(BF16)
            density = INV_ROOT_2PI * jnp.exp(-0.5 * u * u)
            dgl[l, rows, cols] = (phi + u * density).astype(BF16)

        loop(fq // NT, step)

    def expand_back(l, r):
        rows = round_rows(r)
        bias_row = pl.ds(16 * l + 8 + q, 1)

        def step(j):
            cols = pl.ds(aligned(j * NT, NT), NT)
            v = dot_nn(gb[rows, :], W[3 * l + 2, :, cols]) * dgl[l, rows, cols].astype(F32)
            low = v.astype(BF16)
            ub[rows, cols] = low
            sg[bias_row, cols] += jnp.sum(low.astype(F32), axis=0, keepdims=True)

        loop(fq // NT, step)

    def mix_back(l, r):
        rows = round_rows(r)
        ob[rows, :] = dot_nn(hb[rows, :], W[3 * l, :, ocols]).astype(BF16)

    def weight_grad(u, lhs, rhs, cols):
        def step(t):
            rows = pl.ds(aligned(t * NT, NT), NT)
            W[u, rows, cols] = dot_tn(lhs[:, rows], rhs[...]).astype(BF16)

        loop(wn, step)

    def acc_add(j, v):
        acc[j] += jnp.sum(v.reshape(TILE // 8, 8, width), axis=0)

    once = (zl == 0).astype(F32)

    def acc_out(j, row, share):
        v = jnp.sum(acc[j], axis=0, keepdims=True)
        sg[row:row + 1, :] = v if share is None else v * share

    def acc_clear():
        acc[...] = jnp.zeros_like(acc)

    def norm_back_tile(k, r, at, l, which, n_ref, r_ref, low_ref):
        rows = stream_rows(r, at)
        da = total(k, r, pl.ds(at, TILE))
        n = n_ref[l, rows, :].astype(F32)
        e = da * smf[pl.ds(16 * l + 2 * which, 1), :]
        inner = jnp.mean(e * n, axis=1, keepdims=True)
        middle = jnp.mean(e, axis=1, keepdims=True)
        g = gs[rows, :] + r_ref[l, rows, :] * (e - middle - n * inner)
        acc_add(0, da * n)
        acc_add(1, da)
        if low_ref is None:
            tokst[0, pl.ds(at, TILE), :] = g.astype(BF16)
        else:
            acc_add(2, g)
            gs[rows, :] = g
            low_ref[full_rows(r, at), :] = g.astype(BF16)

    def norm_back(k, r, l, which, n_ref, r_ref, low_ref, low_k):
        sum_wait(k, r)
        if r == 0:
            acc_clear()
        tiles(lambda at: norm_back_tile(k, r, at, l, which, n_ref, r_ref, low_ref))
        share_start(low_ref, low_k, r)
        sum_sent(k, r)
        if r == 1:
            acc_out(0, 16 * l + 2 * which, once)
            acc_out(1, 16 * l + 2 * which + 1, once)
            acc_out(2, 16 * l + 4 if which == 1 else 16 * (l - 1) + 5, once)

    s0_start(0)
    land_start(tok, tokst, tks, tkr)
    small[...] = small_in[...]
    small_round(0)
    s0_wait(0)
    s1_start(0)
    s0_start(1)
    land_pass(tok, tokst, tks, tkr)
    s0_start(2)
    land_start(cot, cotst, cts, ctr)
    for k in range(1, 5):
        small_round(k)
    for u in range(3, units):
        s0_start(u)
    smf[...] = small[...].astype(F32)
    sg[...] = jnp.zeros_like(sg)
    qb[...] = jnp.zeros_like(qb)
    mine = pl.ds(aligned(q * hq, hq), hq)
    for l in range(layers):
        for j, row in ((0, 6), (2, 7)):
            qb[8 * l + j:8 * l + j + 1, :] = smf[16 * l + row:16 * l + row + 1, mine]

    land_wait(tok, tokst, tks, tkr)
    for r in range(2):
        def first(at, r=r):
            v = tokst[r, pl.ds(at, TILE), :].astype(F32)
            xs[stream_rows(r, at), :] = v
            norm_tile(v, r, at, 0, 0, n1, r1, a1)

        tiles(first)
        share_start(a1.at[0], 0, r)
    pump(0)
    land_pass(cot, cotst, cts, ctr)
    s2_wait(0)
    s0_wait(2)
    s1_start(2)
    for r in range(2):
        share_wait(a1.at[0], 0, r)
        project(0, r)

    def stream_step(k, r, l_bias, row, l, which, n_ref, r_ref, a_ref, share_k):
        sum_wait(k, r)

        def body(at):
            rows = stream_rows(r, at)
            v = xs[rows, :] + total(k, r, pl.ds(at, TILE)) + smf[pl.ds(16 * l_bias + row, 1), :]
            xs[rows, :] = v
            norm_tile(v, r, at, l, which, n_ref, r_ref, a_ref)

        tiles(body)
        share_start(a_ref.at[l], share_k, r)
        sum_sent(k, r)

    for l in range(layers):
        final = l + 1 == layers
        k = 2 * l
        mask_keys(l)
        attention(l, 0, range(heads))
        sum_part(k, 0, o.at[l], slice(0, hq), 3 * l, ocols)
        attention(l, 1, range(heads // 2))
        sum_mid(k, 0)
        attention(l, 1, range(heads // 2, heads))
        sum_part(k, 1, o.at[l], slice(0, hq), 3 * l, ocols)
        pump(3 * l + 1)
        sum_mid(k, 1)
        if l == 0:
            land_wait(cot, cotst, cts, ctr)
            acc_clear()
            for r in range(2):
                def first_back(at, r=r):
                    low = cotst[r, pl.ds(at, TILE), :]
                    gs[stream_rows(r, at), :] = low.astype(F32)
                    gb[full_rows(r, at), :] = low
                    acc_add(2, low.astype(F32))

                tiles(first_back)
                share_start(gb, 2 * layers, r)
            acc_out(2, 16 * (layers - 1) + 5, once)
        stream_step(k, 0, l, 4, l, 1, n2, r2, a2, 2 * l + 1)
        pump(3 * l + 2)
        s2_wait(3 * l + 1)
        share_wait(a2.at[l], 2 * l + 1, 0)
        expand(l, 0)
        s2_wait(3 * l + 2)
        sum_part(k + 1, 0, act.at[l], every, 3 * l + 2, every)
        stream_step(k, 1, l, 4, l, 1, n2, r2, a2, 2 * l + 1)
        sum_mid(k + 1, 0)
        share_wait(a2.at[l], 2 * l + 1, 1)
        expand(l, 1)
        sum_part(k + 1, 1, act.at[l], every, 3 * l + 2, every)
        if not final:
            pump(3 * l + 3)
        sum_mid(k + 1, 1)
        if final:
            sum_only(k + 1)
        else:
            stream_step(k + 1, 0, l, 5, l + 1, 0, n1, r1, a1, 2 * l + 2)
            s2_wait(3 * l + 3)
            share_wait(a1.at[l + 1], 2 * l + 2, 0)
            project(l + 1, 0)
            stream_step(k + 1, 1, l, 5, l + 1, 0, n1, r1, a1, 2 * l + 2)
            share_wait(a1.at[l + 1], 2 * l + 2, 1)
            project(l + 1, 1)

    land_sent(tok, tks)
    k = 2 * layers
    ks = 2 * layers
    for l in reversed(range(layers)):
        top, bottom = l == layers - 1, l == 0
        share_wait(gb, ks, 0)
        expand_back(l, 0)
        sum_part(k, 0, ub, every, 3 * l + 1, every)
        share_wait(gb, ks, 1)
        expand_back(l, 1)
        sum_mid(k, 0)
        sum_part(k, 1, ub, every, 3 * l + 1, every)
        for u in (3 * l + 2, 3 * l + 1):
            sends_done(u)
        sum_mid(k, 1)
        weight_grad(3 * l + 2, gb, act.at[l], every)
        rs1(3 * l + 2)
        weight_grad(3 * l + 1, a2.at[l], ub, every)
        rs1(3 * l + 1)
        if top:
            wait(recvB.at[bank(last_out), zl], br.at[last_out, 0])

            def finish(at):
                v = (xs[stream_rows(zl, at), :] + total(last_out, zl, pl.ds(at, TILE))
                     + smf[pl.ds(16 * l + 5, 1), :])
                tokst[0, pl.ds(at, TILE), :] = v.astype(BF16)

            tiles(finish)
            wait(sendB.at[bank(last_out), 1 - zl], bs.at[last_out, 0])
            back_start(tokst.at[0], out_ref, oss.at[0], osr.at[0])
        else:
            rs3(3 * l + 3)
            rs4(3 * l + 4)
        mask_keys(l)
        norm_back(k, 0, l, 1, n2, r2, hb, ks + 1)
        rs2(3 * l + 2)
        share_wait(hb, ks + 1, 0)
        mix_back(l, 0)
        attention_back(l, 0)
        norm_back(k, 1, l, 1, n2, r2, hb, ks + 1)
        rs2(3 * l + 1)
        share_wait(hb, ks + 1, 1)
        mix_back(l, 1)
        attention_back(l, 1)
        k += 1
        sum_part(k, 0, dqkv, qkvcols, 3 * l, qkvcols)
        sum_part(k, 1, dqkv, qkvcols, 3 * l, qkvcols)
        sum_mid(k, 0)
        sum_mid(k, 1)
        if bottom:
            sum_only(k)
        for row, cols in ((6, qcols), (7, vcols)):
            sg[16 * l + row:16 * l + row + 1, mine] = jnp.sum(
                dqkv[:, cols].astype(F32), axis=0, keepdims=True)
        sends_done(3 * l)
        weight_grad(3 * l, a1.at[l], dqkv, qkvcols)
        weight_grad(3 * l, hb, o.at[l], ocols)
        rs1(3 * l)
        rs3(3 * l + 2)
        if top:
            back_wait(tokst.at[0], out_ref, oss.at[0], osr.at[0])
        else:
            rs4(3 * l + 3)
        if not bottom:
            norm_back(k, 0, l, 0, n1, r1, gb, ks + 2)
            norm_back(k, 1, l, 0, n1, r1, gb, ks + 2)
        else:
            wait(recvB.at[bank(k), zl], br.at[k, 0])
            acc_clear()
            tiles(lambda at: norm_back_tile(k, zl, at, l, 0, n1, r1, None))
            acc_out(0, 16 * l, None)
            acc_out(1, 16 * l + 1, None)
            wait(sendB.at[bank(k), 1 - zl], bs.at[k, 0])
            back_start(tokst.at[0], igrecv, oss.at[1], osr.at[1])
        rs2(3 * l)
        rs3(3 * l + 1)
        if not bottom:
            rs4(3 * l + 2)
        k += 1
        ks += 2

    for j in range(3):
        sg_round(j)
    rs3(0)
    for j in range(3, 5):
        sg_round(j)
    rs4(2)
    rs4(1)
    back_wait(tokst.at[0], igrecv, oss.at[1], osr.at[1])
    ig_ref[...] = igrecv[...].astype(F32)
    rs4(0)
    store_wait(0)
    store_wait(1)
    land_sent(cot, cts)


def shards(tokens, cotangent, image_mask, qkv_weight, out_weight, up_weight, down_weight,
           qv_bias, up_bias, out_bias, down_bias, attn_gain, attn_shift, mlp_gain, mlp_shift):
    images_here, rows_real, width = tokens.shape
    layers = qkv_weight.shape[0]
    hq = qkv_weight.shape[3]
    fq = up_weight.shape[2]
    lanes = lax.axis_size("tensor")
    groups = lax.axis_size("dp") // 8
    assert images_here == 1 and lanes == 4 and width == fq == 4 * hq
    kb = width // 8
    slot = -(-rows_real // TILE) * TILE
    half = 2 * slot
    rows_all = 4 * slot
    units = 3 * layers
    dp = lax.axis_index("dp")
    z = lax.axis_index("tensor")
    d8 = dp % 8
    first = d8 == 0

    position = z * rows_real + jnp.arange(rows_real)
    keep = (position < VALID).astype(BF16)[:, None] * image_mask.astype(BF16)[0]
    pad = ((0, slot - rows_real), (0, 0))
    tok = jnp.pad(tokens[0], pad)
    cot = jnp.pad(cotangent[0] * keep, pad)

    here = qkv_weight.shape[1]
    wsh = jnp.stack([
        jnp.concatenate([qkv_weight.reshape(layers, here, 3 * hq), out_weight], axis=2),
        up_weight, down_weight], axis=1).reshape(units, here, fq)
    if groups > 1:
        wsh = lax.all_gather(wsh, "dp", axis=1, tiled=True)
        wsh = lax.dynamic_slice_in_dim(wsh, d8 * kb, kb, 1)

    shard = dp * lanes + z
    piece = attn_gain.shape[1]

    def window(values, at):
        wide = jnp.zeros((values.shape[0], width), BF16)
        return lax.dynamic_update_slice(wide, values, (0, at))

    ups = up_bias.shape[1]
    up_at = shard * ups
    rows = []
    for l in range(layers):
        six = jnp.stack([attn_gain[l], attn_shift[l], mlp_gain[l], mlp_shift[l],
                         out_bias[l], down_bias[l], qv_bias[l, 0], qv_bias[l, 1]])
        rows.append(window(six, shard * piece))
        up_row = window(up_bias[l][None], up_at % width)
        rows.append(jnp.where(jnp.arange(4)[:, None] == up_at // width, up_row, 0))
        rows.append(jnp.zeros((4, width), BF16))
    small_in = jnp.concatenate(rows)
    if groups > 1:
        small_in = lax.psum(small_in, "dp") * first.astype(BF16)

    out_shapes = (
        jax.ShapeDtypeStruct((slot, width), BF16),
        jax.ShapeDtypeStruct((slot, width), F32),
        jax.ShapeDtypeStruct((layers, kb, 3 * hq), F32),
        jax.ShapeDtypeStruct((layers, kb, hq), F32),
        jax.ShapeDtypeStruct((layers, kb, fq), F32),
        jax.ShapeDtypeStruct((layers, kb, fq), F32),
        jax.ShapeDtypeStruct((16 * layers, width), F32),
    )
    V = pltpu.VMEM
    D = lambda *s: pltpu.SemaphoreType.DMA(s)
    sums, shares = 4 * layers, 4 * layers
    scratch = [
        V((units, width, fq), BF16),
        V((half, width), F32), V((half, width), F32),
        V((layers, half, width), BF16), V((layers, half, width), BF16),
        V((layers, half, 1), F32), V((layers, half, 1), F32),
        V((layers, rows_all, width), BF16), V((layers, rows_all, width), BF16),
        V((layers, rows_all, 3 * hq), BF16), V((layers, rows_all, hq), BF16),
        V((layers, rows_all, fq), BF16), V((layers, rows_all, fq), BF16),
        V((rows_all, width), BF16), V((rows_all, width), BF16),
        V((rows_all, fq), BF16), V((rows_all, hq), BF16), V((rows_all, 3 * hq), BF16),
        V((rows_all, hq), F32), V((rows_all, hq), F32), V((3, 8, width), F32),
        V((2, rows_all, hq), BF16),
        V((2, slot, width), F32),
        V((2, slot, width), BF16), V((2, 2, slot, width), BF16),
        V((3, 2, slot, width), BF16), V((3, 2, slot, width), BF16),
        V((2, slot, width), BF16), V((2, slot, width), BF16),
        V((slot, width), BF16),
        V((16 * layers, width), BF16), V((5, 16 * layers, width), BF16),
        V((16 * layers, width), F32), V((8 * layers, hq), F32),
        V((5, 16 * layers, width), F32),
        V((units, 2, kb, fq), BF16), V((units, 2, 2 * kb, fq), BF16), V((units, 2, kb, fq), BF16),
        D(units, 2), D(units, 2), D(units, 2), D(units, 2), D(units, 2), D(units, 2),
        D(sums, 2), D(sums, 2), D(sums, 2), D(sums, 2), D(shares, 2), D(shares, 2),
        D(2), D(2), D(2), D(2), D(2), D(2), D(5), D(5), D(5), D(5),
        D(units, 2), D(units, 2), D(units, 2), D(units, 2), D(units, 2), D(units, 2),
        V((2, kb, fq), F32), D(2, 2),
    ]
    any_spec = pl.BlockSpec(memory_space=pl.ANY)
    vmem_spec = pl.BlockSpec(memory_space=pltpu.VMEM)
    out, ig, *gws, sg = pl.pallas_call(
        functools.partial(kernel, layers, rows_real),
        out_shape=out_shapes,
        in_specs=[any_spec, any_spec, any_spec, vmem_spec],
        out_specs=(any_spec, vmem_spec, any_spec, any_spec, any_spec, any_spec, vmem_spec),
        scratch_shapes=scratch,
        compiler_params=pltpu.CompilerParams(
            collective_id=0, has_side_effects=True, vmem_limit_bytes=int(63.5 * 2 ** 20)),
        cost_estimate=pl.CostEstimate(
            flops=int(1e11), bytes_accessed=int(1e8), transcendentals=0),
    )(tok, cot, wsh, small_in)

    if groups > 1:
        wide = (jnp.zeros((layers, width, gw.shape[2]), F32) for gw in gws)
        gws = [lax.psum_scatter(lax.dynamic_update_slice_in_dim(zero, gw, d8 * kb, 1), "dp",
                                scatter_dimension=1, tiled=True) for zero, gw in zip(wide, gws)]
        sg = lax.psum(sg * first.astype(F32), "dp")
    sg = sg.reshape(layers, 16, width)
    mine = lax.dynamic_slice_in_dim(sg[:, :8], shard * piece, piece, 2)
    ups_grad = lax.dynamic_slice_in_dim(sg[:, 8:12].reshape(layers, 4 * width), up_at, ups, 1)
    return (
        out[:rows_real][None],
        ig[:rows_real][None],
        gws[0].reshape(layers, here, 3, hq),
        gws[1],
        gws[2],
        gws[3],
        mine[:, 6:8],
        ups_grad,
        mine[:, 4],
        mine[:, 5],
        mine[:, 0],
        mine[:, 1],
        mine[:, 2],
        mine[:, 3],
    )


def solution(mesh):
    both = ("dp", "tensor")
    rows = P("dp", "tensor", None)
    cols = P(None, "dp", "tensor")
    vec = P(None, both)
    return jax.shard_map(
        shards,
        mesh=mesh,
        in_specs=(rows, rows, P("dp"), P(None, "dp", None, "tensor"), cols, cols, cols,
                  P(None, None, both), vec, vec, vec, vec, vec, vec, vec),
        out_specs=(rows, rows, P(None, "dp", None, "tensor"), cols, cols, cols,
                   P(None, None, both), vec, vec, vec, vec, vec, vec, vec),
        check_vma=False,
    )
```

```python
import functools

import jax
import jax.numpy as jnp
from jax import lax
from jax.experimental import pallas as pl
from jax.experimental.pallas import tpu as pltpu
from jax.sharding import PartitionSpec as P

HD = 64
VALID = 577
EPS = 1e-06
ROOT_HALF = 0.7071067811865476
INV_ROOT_2PI = 0.3989422804014327
FAR_BELOW = -1e30
MESH = pl.DeviceIdType.MESH
F32 = jnp.float32
BF16 = jnp.bfloat16
TILE = 32
NT = 256


def dot_nn(a, b):
    return lax.dot_general(a, b, (((1,), (0,)), ((), ())), preferred_element_type=F32)


def dot_nt(a, b):
    return lax.dot_general(a, b, (((1,), (1,)), ((), ())), preferred_element_type=F32)


def dot_tn(a, b):
    return lax.dot_general(a, b, (((0,), (0,)), ((), ())), preferred_element_type=F32)


def loop(n, body):
    def step(i, carry):
        body(i)
        return carry

    lax.fori_loop(0, n, step, 0)


def aligned(v, m):
    return pl.multiple_of(v, m)


def kernel(
    layers, rows_real,
    tok, cot, wqkv, wout, wup, wdown, small_in,
    out_ref, ig_ref, gqkv, gout, gup, gdown, sg_out,
    W, xs, gs, n1, n2, r1, r2, a1, a2, qkv, o, act, dgl,
    gb, hb, ub, ob, dqkv, dk_acc, dv_acc, acc, kmask,
    own, sendA, recvA, sendB, recvB, tokst, cotst, igrecv,
    small, smz, smf, qb, upb, upg, sg, sgy, sgx, sgc, sgz,
    recv1, recv2, recv4,
    s0s, s0r, s1s, s1r, s2s, s2r,
    as_, ar, bs, br, cs, cr,
    tks, tkr, cts, ctr, oss, osr, sms, smr, smzs, smzr, sgs, sgr, sgzs, sgzr,
    g1s, g1r, g2s, g2r, g4s, g4r, stage, sts,
):
    width = xs.shape[1]
    half = xs.shape[0]
    slot = half // 2
    rows_all = 2 * half
    kb = wup.shape[1]
    blk = 2 * kb
    hq = o.shape[2]
    fq = act.shape[2]
    heads = hq // HD
    wn = width // NT

    dp = lax.axis_index("dp")
    z = lax.axis_index("tensor")
    base = (dp // 8) * 8
    d8 = dp % 8
    y, x, c = d8 // 4, (d8 // 2) % 2, d8 % 2
    zh, zl = z // 2, z % 2
    q = zl + 2 * c
    z2 = (z + 2) % 4
    home = c == zh

    def dev(yy, xx, cc, zz):
        return (base + yy * 4 + xx * 2 + cc, zz)

    sib = dev(y, x, 1 - c, z)
    xn = dev(y, 1 - x, c, z)
    yn = dev(1 - y, x, c, z)
    zp = dev(y, x, c, z + 1 - 2 * zl)
    far = dev(y, x, c, z2)
    swap = dev(y, x, zh, 2 * c + zl)

    def rc(src, dst, ss, rs, to):
        return pltpu.make_async_remote_copy(
            src_ref=src, dst_ref=dst, send_sem=ss, recv_sem=rs,
            device_id=to, device_id_type=MESH)

    def wait(ref, sem):
        pltpu.make_async_copy(ref, ref, sem).wait()

    barrier = pltpu.get_barrier_semaphore()
    greet = [xn, yn, sib]
    for k in range(1, 4):
        for cc in range(2):
            greet.append(dev(y, x, cc, (z + k) % 4))
    for to in greet:
        pl.semaphore_signal(barrier, inc=1, device_id=to, device_id_type=MESH)
    pl.semaphore_wait(barrier, len(greet))

    def rows_of(yy, xx):
        return aligned((2 * yy + xx) * blk, blk)

    my_rows = pl.ds(aligned(d8 * kb, kb), kb)
    own_blk = rows_of(y, x)
    x_blk = rows_of(y, 1 - x)
    y_blk = rows_of(1 - y, x)
    diag_blk = rows_of(1 - y, 1 - x)

    units = 3 * layers
    cut = 2 * hq
    pieces = [(0, slice(0, cut)), (0, slice(cut, fq))] + [(u, slice(0, fq)) for u in range(1, units)]

    def piece(p, at, n):
        u, cols = pieces[p]
        return W.at[u, pl.ds(at, n), cols]

    def sources(p):
        u, cols = pieces[p]
        l, part = u // 3, u % 3
        if part:
            return [((wup, wdown)[part - 1].at[l], cols)]
        found = [(wqkv.at[l, :, slice(cols.start, min(cols.stop, 3 * hq))],
                  slice(cols.start, min(cols.stop, 3 * hq)))]
        if cols.stop > 3 * hq:
            found.append((wout.at[l], slice(3 * hq, 4 * hq)))
        return found

    def s0_start(p):
        u = pieces[p][0]
        for i, (src, cols) in enumerate(sources(p)):
            dst = W.at[u, my_rows, cols]
            rc(src, dst, s0s.at[p, 0, i], s0r.at[p, c, i], dev(y, x, zh, z2)).start()

            @pl.when(home)
            def _():
                pltpu.make_async_copy(src, dst, s0r.at[p, c, i]).start()

            @pl.when(jnp.logical_not(home))
            def _():
                rc(src, dst, s0s.at[p, 1, i], s0r.at[p, c, i], sib).start()

    def s0_wait(p):
        u = pieces[p][0]
        for j in range(2):
            for i, (src, cols) in enumerate(sources(p)):
                wait(W.at[u, pl.ds(own_blk + j * kb, kb), cols], s0r.at[p, j, i])

    def s1_start(p):
        for j in range(2):
            ref = piece(p, own_blk + j * kb, kb)
            rc(ref, ref, s1s.at[p, 0, j], s1r.at[p, 0, j], xn).start()
            ref = piece(p, own_blk + (1 - j) * kb, kb)
            rc(ref, ref, s1s.at[p, 1, j], s1r.at[p, 1, j], yn).start()

    def s1_wait(p, j):
        wait(piece(p, x_blk + j * kb, kb), s1r.at[p, 0, j])
        wait(piece(p, y_blk + (1 - j) * kb, kb), s1r.at[p, 1, j])

    def s2_start(p):
        ref = piece(p, x_blk, kb)
        rc(ref, ref, s2s.at[p, 1], s2r.at[p, 1], yn).start()
        ref = piece(p, y_blk + kb, kb)
        rc(ref, ref, s2s.at[p, 0], s2r.at[p, 0], xn).start()

    def s2_wait(p):
        s1_wait(p, 1)
        wait(piece(p, diag_blk, kb), s2r.at[p, 1])
        wait(piece(p, diag_blk + kb, kb), s2r.at[p, 0])

    def ready(u):
        for p in range(len(pieces)):
            if pieces[p][0] == u:
                s2_wait(p)

    def sends_done(unit):
        for p in range(len(pieces)):
            if pieces[p][0] != unit:
                continue
            for i, (src, cols) in enumerate(sources(p)):
                ref = W.at[unit, my_rows, cols]
                wait(ref, s0s.at[p, 0, i])

                @pl.when(jnp.logical_not(home))
                def _():
                    wait(ref, s0s.at[p, 1, i])

            ref = piece(p, own_blk, kb)
            for j in range(2):
                for i in range(2):
                    wait(ref, s1s.at[p, j, i])
                wait(ref, s2s.at[p, j])

    def pump(p):
        s1_wait(p, 0)
        s2_start(p)
        if p + 1 < len(pieces):
            s0_wait(p + 1)
            s1_start(p + 1)
        if p + 3 < len(pieces):
            s0_start(p + 3)
        elif p + 3 == len(pieces):
            land_start(cot, cotst, cts, ctr)

    def land_start(src, dst, ss, rs):
        @pl.when(home)
        def _():
            pltpu.make_async_copy(src, dst.at[zl], rs.at[zl]).start()

        @pl.when(jnp.logical_not(home))
        def _():
            rc(src, dst.at[zl], ss.at[0], rs.at[zl], swap).start()

    def land_pass(src, dst, ss, rs):
        wait(dst.at[zl], rs.at[zl])
        rc(dst.at[zl], dst.at[zl], ss.at[1], rs.at[zl], zp).start()

    def land_wait(src, dst, ss, rs):
        wait(dst.at[1 - zl], rs.at[1 - zl])

    def land_sent(src, ss):
        @pl.when(jnp.logical_not(home))
        def _():
            wait(src, ss.at[0])

        wait(src, ss.at[1])

    def back_start(src, dst, ss, rs):
        @pl.when(home)
        def _():
            pltpu.make_async_copy(src, dst, rs).start()

        @pl.when(jnp.logical_not(home))
        def _():
            rc(src, dst, ss, rs, swap).start()

    def back_wait(src, dst, ss, rs):
        wait(dst, rs)

        @pl.when(jnp.logical_not(home))
        def _():
            wait(src, ss)

    tile_lanes = small_in.shape[1]

    def lanes_at(at, n):
        return pl.ds(aligned(at * tile_lanes, tile_lanes), n * tile_lanes)

    def column_start(src, dst, ss, rs):
        for k in range(1, 4):
            rc(src, dst.at[z], ss.at[k - 1], rs.at[z], dev(y, x, c, (z + k) % 4)).start()

    def column_wait(src, dst, ss, rs):
        for k in range(1, 4):
            wait(dst.at[(z + k) % 4], rs.at[(z + k) % 4])
            wait(src, ss.at[k - 1])

    def small_gather():
        column_wait(small_in, smz, smzs, smzr)
        smz[z] = small_in[...]
        v = smz[0].astype(F32)
        for k in range(1, 4):
            v = v + smz[k].astype(F32)
        small[:, lanes_at(d8, 1)] = v.astype(BF16)
        land_pass(tok, tokst, tks, tkr)
        for k, (at, n, to) in enumerate(((d8, 1, sib), (2 * (d8 // 2), 2, xn), (4 * y, 4, yn))):
            mine_now = small.at[:, lanes_at(at, n)]
            cp = rc(mine_now, mine_now, sms.at[k], smr.at[k], to)
            cp.start()
            cp.wait()

    def small_scatter(k):
        if k < 3:
            at, other, n, into, to = (
                (4 * y, 4 * (1 - y), 4, sgy, yn),
                (4 * y + 2 * x, 4 * y + 2 * (1 - x), 2, sgx, xn),
                (d8, 4 * y + 2 * x + 1 - c, 1, sgc, sib))[k]
            cp = rc(sg.at[:, lanes_at(other, n)], into, sgs.at[k], sgr.at[k], to)
            cp.start()
            cp.wait()
            sg[:, lanes_at(at, n)] += into[...]
        else:
            sgz[z] = sg[:, lanes_at(d8, 1)]
            column_start(sgz.at[z], sgz, sgzs, sgzr)
            column_wait(sgz.at[z], sgz, sgzs, sgzr)
            sg_out[...] = (sgz[0] + sgz[1]) + (sgz[2] + sgz[3])

    def round_rows(r):
        return pl.ds(r * half, half)

    def slot_at(r, h):
        return aligned(r * half + h * slot, slot)

    def share_start(ref, k, r):
        part = ref.at[pl.ds(slot_at(r, c), slot)]
        rc(part, part, cs.at[k, r], cr.at[k, r], sib).start()

    def share_wait(ref, k, r):
        part = ref.at[pl.ds(slot_at(r, 1 - c), slot)]
        wait(part, cr.at[k, r])
        wait(part, cs.at[k, r])

    last_out = 2 * layers - 1
    last_sum = 4 * layers - 1

    def bank(k):
        return 2 if k == last_out else (k + (k > last_out)) % 2

    def sum_part(k, r, lhs, cols, u, wcols):
        def step(n):
            ncols = pl.ds(aligned(n * NT, NT), NT)
            rows = jnp.concatenate(
                [lhs[pl.ds(slot_at(r, c), slot), cols], lhs[pl.ds(slot_at(r, 1 - c), slot), cols]], 0)
            v = dot_nt(rows, W[u, ncols, wcols])
            own[r, :, ncols] = v[:slot]
            sendA[r, :, ncols] = v[slot:].astype(BF16)

        loop(wn, step)
        rc(sendA.at[r], recvA.at[k % 2, r], as_.at[k, r], ar.at[k, r], sib).start()

    def sum_mid(k, r):
        wait(recvA.at[k % 2, r], ar.at[k, r])
        wait(sendA.at[r], as_.at[k, r])

        def step(i):
            rows = pl.ds(aligned(i * TILE, TILE), TILE)
            sendB[bank(k), r, rows, :] = (own[r, rows, :] + recvA[k % 2, r, rows, :].astype(F32)).astype(BF16)

        loop(slot // TILE, step)
        if k not in (last_out, last_sum):
            rc(sendB.at[bank(k), r], recvB.at[bank(k), r], bs.at[k, r], br.at[k, r], zp).start()

    def sum_only(k):
        rc(sendB.at[bank(k), 1 - zl], recvB.at[bank(k), 1 - zl], bs.at[k, 0], br.at[k, 0], zp).start()

    def sum_wait(k, r):
        wait(recvB.at[bank(k), r], br.at[k, r])

    def sum_sent(k, r):
        wait(sendB.at[bank(k), r], bs.at[k, r])

    def total(k, r, rows):
        return sendB[bank(k), r, rows, :].astype(F32) + recvB[bank(k), r, rows, :].astype(F32)

    def tiles(body):
        def step(i):
            body(aligned(i * TILE, TILE))

        loop(slot // TILE, step)

    def stream_rows(r, at):
        return pl.ds(aligned(r * slot + at, TILE), TILE)

    def full_rows(r, at):
        return pl.ds(aligned(slot_at(r, c) + at, TILE), TILE)

    def norm_tile(v, r, at, l, which, n_ref, r_ref, a_ref):
        gain = smf[pl.ds(16 * l + 2 * which, 1), :]
        shift = smf[pl.ds(16 * l + 2 * which + 1, 1), :]
        centre = v - jnp.mean(v, axis=1, keepdims=True)
        inv = lax.rsqrt(jnp.mean(centre * centre, axis=1, keepdims=True) + EPS)
        n = centre * inv
        rows = stream_rows(r, at)
        n_ref[l, rows, :] = n.astype(BF16)
        r_ref[l, rows, :] = inv
        a_ref[l, full_rows(r, at), :] = (n * gain + shift).astype(BF16)

    lane = lax.broadcasted_iota(jnp.int32, (1, hq), 1)
    QC = half

    def head_mask(h):
        return jnp.logical_and(lane >= h * HD, lane < (h + 1) * HD)

    def spare(h):
        return lane == (hq - 1 if h < heads - 1 else 0)

    qcols = slice(0, hq)
    kcols = slice(hq, 2 * hq)
    vcols = slice(2 * hq, 3 * hq)
    qkvcols = slice(0, 3 * hq)
    ocols = slice(3 * hq, 4 * hq)
    every = slice(0, fq)

    def mask_keys(l):
        for s in range(4):
            r, h = s // 2, s % 2
            rows = pl.ds(s * slot, slot)
            within = lax.broadcasted_iota(jnp.int32, (slot, 1), 0)
            valid = jnp.logical_and(within < rows_real, (2 * h + r) * rows_real + within < VALID)
            low = jnp.where(valid, 0.0, FAR_BELOW)
            keys = qkv[l, rows, kcols].astype(F32)
            for j, h in ((0, 0), (1, heads - 1)):
                kmask[j, rows, :] = jnp.where(spare(h), low, keys).astype(BF16)

    def softmax_of(qm, h):
        s = dot_nt(jnp.where(spare(h), 1.0, qm).astype(BF16), kmask[0 if h < heads - 1 else 1])
        e = jnp.exp(s - jnp.max(s, axis=1, keepdims=True))
        return e * (1.0 / jnp.sum(e, axis=1, keepdims=True))

    def attention(l, r, which):
        rows = round_rows(r)
        qc = qkv[l, rows, qcols].astype(F32)
        values = qkv[l, :, vcols]
        for h in which:
            m = head_mask(h)
            qm = jnp.where(m, qc * (HD ** -0.5), 0.0)
            p = softmax_of(qm, h).astype(BF16)
            mixed = dot_nn(p, values)
            pair = slice(h // 2 * 2 * HD, (h // 2 + 1) * 2 * HD)
            old = o[l, rows, pair]
            o[l, rows, pair] = jnp.where(m[:, pair], mixed[:, pair], old.astype(F32)).astype(BF16)

    def attention_back(l, r):
        rows = round_rows(r)
        qc = qkv[l, rows, qcols].astype(F32)
        oc = ob[rows, :].astype(F32)
        keys, values = qkv[l, :, kcols], qkv[l, :, vcols]
        dq = jnp.zeros((QC, hq), F32)
        for h in range(heads):
            m = head_mask(h)
            qm = jnp.where(m, qc * (HD ** -0.5), 0.0)
            om = jnp.where(m, oc, 0.0).astype(BF16)
            p = softmax_of(qm, h)
            dprob = dot_nt(om, values)
            inner = jnp.sum(dprob * p, axis=1, keepdims=True)
            ds = (p * (dprob - inner)).astype(BF16)
            dq = jnp.where(m, dot_nn(ds, keys), dq)
            dk = dot_tn(ds, qm.astype(BF16))
            dv = dot_tn(p.astype(BF16), om)
            if r == 0 and h == 0:
                dk_acc[...] = dk
                dv_acc[...] = dv
            else:
                dk_acc[...] += dk
                dv_acc[...] += dv
        dqkv[rows, qcols] = (dq * (HD ** -0.5)).astype(BF16)
        if r == 1:
            dqkv[:, kcols] = dk_acc[...].astype(BF16)
            dqkv[:, vcols] = dv_acc[...].astype(BF16)

    def rs1(u):
        ref = W.at[u, pl.ds(diag_blk, kb)]
        rc(ref, recv1.at[u, 0], g1s.at[u, 0], g1r.at[u, 0], xn).start()
        ref = W.at[u, pl.ds(diag_blk + kb, kb)]
        rc(ref, recv1.at[u, 1], g1s.at[u, 1], g1r.at[u, 1], yn).start()
        part = pl.ds(0, kb)
        ref = W.at[u, pl.ds(x_blk, kb)]
        rc(ref, recv2.at[u, 0, part], g2s.at[u, 0, 0], g2r.at[u, 0, 0], xn).start()
        part = pl.ds(kb, kb)
        ref = W.at[u, pl.ds(y_blk + kb, kb)]
        rc(ref, recv2.at[u, 1, part], g2s.at[u, 1, 1], g2r.at[u, 1, 1], yn).start()

    RT = 64

    def add_rows(u, at, refs, n):
        def step(i):
            off = aligned(i * RT, RT)
            rows = pl.ds(aligned(at + off, RT), RT)
            v = W[u, rows, :].astype(F32)
            for ref in refs:
                v = v + ref[pl.ds(off, RT), :].astype(F32)
            W[u, rows, :] = v.astype(BF16)

        loop(n // RT, step)

    def rs2(u):
        for j in range(2):
            wait(recv1.at[u, j], g1r.at[u, j])
            wait(recv1.at[u, j], g1s.at[u, j])
        add_rows(u, y_blk, [recv1.at[u, 0]], kb)
        part = pl.ds(0, kb)
        ref = W.at[u, pl.ds(y_blk, kb)]
        rc(ref, recv2.at[u, 1, part], g2s.at[u, 1, 0], g2r.at[u, 1, 0], yn).start()
        add_rows(u, x_blk + kb, [recv1.at[u, 1]], kb)
        part = pl.ds(kb, kb)
        ref = W.at[u, pl.ds(x_blk + kb, kb)]
        rc(ref, recv2.at[u, 0, part], g2s.at[u, 0, 1], g2r.at[u, 0, 1], xn).start()

    def rs3(u):
        for j in range(2):
            for i in range(2):
                part = recv2.at[u, j, pl.ds(i * kb, kb)]
                wait(part, g2r.at[u, j, i])
                wait(part, g2s.at[u, j, i])
        add_rows(u, own_blk, [recv2.at[u, 0], recv2.at[u, 1]], blk)

        @pl.when(home)
        def _():
            ref = W.at[u, pl.ds(aligned(own_blk + (1 - c) * kb, kb), kb)]
            rc(ref, recv4.at[u, 0], g4s.at[u, 0], g4r.at[u, 0], sib).start()
            ref = W.at[u, pl.ds(aligned(own_blk + c * kb, kb), kb)]
            pltpu.make_async_copy(ref, recv4.at[u, 0], g4r.at[u, 0]).start()

        @pl.when(jnp.logical_not(home))
        def _():
            for j in range(2):
                ref = W.at[u, pl.ds(own_blk + j * kb, kb)]
                rc(ref, recv4.at[u, 1], g4s.at[u, j], g4r.at[u, 1], dev(y, x, j, z2)).start()

    def rs4(u):
        for j in range(2):
            wait(recv4.at[u, j], g4r.at[u, j])
        wait(recv4.at[u, 0], g4s.at[u, 0])

        @pl.when(jnp.logical_not(home))
        def _():
            wait(recv4.at[u, 0], g4s.at[u, 1])

        slot_of = stored.index(None) if None in stored else len(order) % 2
        if stored[slot_of] is not None:
            store_wait(slot_of)

        def step(i):
            rows = pl.ds(aligned(i * RT, RT), RT)
            stage[slot_of, rows, :] = (recv4[u, 0, rows, :].astype(F32)
                                       + recv4[u, 1, rows, :].astype(F32))

        loop(kb // RT, step)
        stored[slot_of] = u
        order.append(u)
        for src, dst, sem in stores(slot_of):
            pltpu.make_async_copy(src, dst, sem).start()

    stored, order = [None, None], []

    def stores(slot_of):
        u = stored[slot_of]
        l, part = u // 3, u % 3
        if part:
            return [(stage.at[slot_of], (gup, gdown)[part - 1].at[l], sts.at[slot_of, 0])]
        return [(stage.at[slot_of, :, qkvcols], gqkv.at[l], sts.at[slot_of, 0]),
                (stage.at[slot_of, :, ocols], gout.at[l], sts.at[slot_of, 1])]

    def store_wait(slot_of):
        for src, dst, sem in stores(slot_of):
            pltpu.make_async_copy(src, dst, sem).wait()

    def project(l, r):
        rows = round_rows(r)
        for j in range(3):
            cols = slice(j * hq, (j + 1) * hq)
            v = dot_nn(a1[l, rows, :], W[3 * l, :, cols])
            qkv[l, rows, cols] = (v + qb[8 * l + j:8 * l + j + 1, :]).astype(BF16)

    def expand(l, r):
        rows = round_rows(r)

        def step(j):
            cols = pl.ds(aligned(j * NT, NT), NT)
            u = dot_nn(a2[l, rows, :], W[3 * l + 1, :, cols]) + upb[8 * l:8 * l + 1, cols]
            phi = 0.5 * (1.0 + lax.erf(u * ROOT_HALF))
            act[l, rows, cols] = (u * phi).astype(BF16)
            density = INV_ROOT_2PI * jnp.exp(-0.5 * u * u)
            dgl[l, rows, cols] = (phi + u * density).astype(BF16)

        loop(fq // NT, step)

    def expand_back(l, r):
        rows = round_rows(r)

        def step(j):
            cols = pl.ds(aligned(j * NT, NT), NT)
            v = dot_nn(gb[rows, :], W[3 * l + 2, :, cols]) * dgl[l, rows, cols].astype(F32)
            low = v.astype(BF16)
            ub[rows, cols] = low
            upg[8 * l:8 * l + 1, cols] += jnp.sum(low.astype(F32), axis=0, keepdims=True)

        loop(fq // NT, step)

    def mix_back(l, r):
        rows = round_rows(r)
        ob[rows, :] = dot_nn(hb[rows, :], W[3 * l, :, ocols]).astype(BF16)

    def weight_grad(u, lhs, rhs, cols):
        def step(t):
            rows = pl.ds(aligned(t * NT, NT), NT)
            W[u, rows, cols] = dot_tn(lhs[:, rows], rhs[...]).astype(BF16)

        loop(wn, step)

    def acc_add(j, v):
        acc[j] += jnp.sum(v.reshape(TILE // 8, 8, width), axis=0)

    once = (zl == 0).astype(F32)

    def acc_out(j, row, share):
        v = jnp.sum(acc[j], axis=0, keepdims=True)
        sg[row:row + 1, :] = v if share is None else v * share

    def acc_clear():
        acc[...] = jnp.zeros_like(acc)

    def norm_back_tile(k, r, at, l, which, n_ref, r_ref, low_ref):
        rows = stream_rows(r, at)
        da = total(k, r, pl.ds(at, TILE))
        n = n_ref[l, rows, :].astype(F32)
        e = da * smf[pl.ds(16 * l + 2 * which, 1), :]
        inner = jnp.mean(e * n, axis=1, keepdims=True)
        middle = jnp.mean(e, axis=1, keepdims=True)
        g = gs[rows, :] + r_ref[l, rows, :] * (e - middle - n * inner)
        acc_add(0, da * n)
        acc_add(1, da)
        if low_ref is None:
            tokst[0, pl.ds(at, TILE), :] = g.astype(BF16)
        else:
            acc_add(2, g)
            gs[rows, :] = g
            low_ref[full_rows(r, at), :] = g.astype(BF16)

    def norm_back(k, r, l, which, n_ref, r_ref, low_ref, low_k):
        sum_wait(k, r)
        if r == 0:
            acc_clear()
        tiles(lambda at: norm_back_tile(k, r, at, l, which, n_ref, r_ref, low_ref))
        share_start(low_ref, low_k, r)
        sum_sent(k, r)
        if r == 1:
            acc_out(0, 16 * l + 2 * which, once)
            acc_out(1, 16 * l + 2 * which + 1, once)
            acc_out(2, 16 * l + 4 if which == 1 else 16 * (l - 1) + 5, once)

    column_start(small_in, smz, smzs, smzr)
    land_start(tok, tokst, tks, tkr)
    s0_start(0)
    s0_start(1)
    sg[...] = jnp.zeros_like(sg)
    qb[...] = jnp.zeros_like(qb)
    upg[...] = jnp.zeros_like(upg)
    small_gather()
    s0_wait(0)
    s1_start(0)
    s0_start(2)
    smf[...] = small[...].astype(F32)
    mine = pl.ds(aligned(q * hq, hq), hq)
    up_tiles = [(slice(j * tile_lanes, (j + 1) * tile_lanes), j % 4, 2 * q + j // 4)
                for j in range(fq // tile_lanes)]
    for l in range(layers):
        for j, row in ((0, 6), (2, 7)):
            qb[8 * l + j:8 * l + j + 1, :] = smf[16 * l + row:16 * l + row + 1, mine]
        for cols, row, at in up_tiles:
            row = 16 * l + 8 + row
            upb[8 * l:8 * l + 1, cols] = smf[row:row + 1, lanes_at(at, 1)]

    s0_wait(1)
    s1_start(1)
    s0_start(3)
    s1_wait(0, 0)
    s2_start(0)
    land_wait(tok, tokst, tks, tkr)
    for r in range(2):
        def first(at, r=r):
            v = tokst[r, pl.ds(at, TILE), :].astype(F32)
            xs[stream_rows(r, at), :] = v
            norm_tile(v, r, at, 0, 0, n1, r1, a1)

        tiles(first)
        share_start(a1.at[0], 0, r)
    pump(1)
    ready(0)
    for r in range(2):
        share_wait(a1.at[0], 0, r)
        project(0, r)

    def stream_step(k, r, l_bias, row, l, which, n_ref, r_ref, a_ref, share_k):
        sum_wait(k, r)

        def body(at):
            rows = stream_rows(r, at)
            v = xs[rows, :] + total(k, r, pl.ds(at, TILE)) + smf[pl.ds(16 * l_bias + row, 1), :]
            xs[rows, :] = v
            norm_tile(v, r, at, l, which, n_ref, r_ref, a_ref)

        tiles(body)
        share_start(a_ref.at[l], share_k, r)
        sum_sent(k, r)

    for l in range(layers):
        final = l + 1 == layers
        k = 2 * l
        mask_keys(l)
        attention(l, 0, range(heads))
        if l == 0:
            pump(2)
        sum_part(k, 0, o.at[l], slice(0, hq), 3 * l, ocols)
        attention(l, 1, range(heads // 2))
        sum_mid(k, 0)
        attention(l, 1, range(heads // 2, heads))
        sum_part(k, 1, o.at[l], slice(0, hq), 3 * l, ocols)
        sum_mid(k, 1)
        if final:
            if layers == 1:
                land_pass(cot, cotst, cts, ctr)
            land_wait(cot, cotst, cts, ctr)
            acc_clear()
            for r in range(2):
                def first_back(at, r=r):
                    low = cotst[r, pl.ds(at, TILE), :]
                    gs[stream_rows(r, at), :] = low.astype(F32)
                    gb[full_rows(r, at), :] = low
                    acc_add(2, low.astype(F32))

                tiles(first_back)
                share_start(gb, 2 * layers, r)
            acc_out(2, 16 * (layers - 1) + 5, once)
        if final:
            pump(3 * l + 3)
        stream_step(k, 0, l, 4, l, 1, n2, r2, a2, 2 * l + 1)
        if not final:
            pump(3 * l + 3)
        ready(3 * l + 1)
        share_wait(a2.at[l], 2 * l + 1, 0)
        expand(l, 0)
        stream_step(k, 1, l, 4, l, 1, n2, r2, a2, 2 * l + 1)
        share_wait(a2.at[l], 2 * l + 1, 1)
        expand(l, 1)
        ready(3 * l + 2)
        if not final:
            for r in range(2):
                sum_part(k + 1, r, act.at[l], every, 3 * l + 2, every)
            for r in range(2):
                sum_mid(k + 1, r)
            pump(3 * l + 4)
            stream_step(k + 1, 0, l, 5, l + 1, 0, n1, r1, a1, 2 * l + 2)
            ready(3 * l + 3)
            share_wait(a1.at[l + 1], 2 * l + 2, 0)
            project(l + 1, 0)
            stream_step(k + 1, 1, l, 5, l + 1, 0, n1, r1, a1, 2 * l + 2)
            pump(3 * l + 5)
            share_wait(a1.at[l + 1], 2 * l + 2, 1)
            project(l + 1, 1)
            if l + 2 == layers:
                land_pass(cot, cotst, cts, ctr)

    land_sent(tok, tks)
    k = 2 * layers
    ks = 2 * layers
    for l in reversed(range(layers)):
        top, bottom = l == layers - 1, l == 0
        share_wait(gb, ks, 0)
        expand_back(l, 0)
        sum_part(k, 0, ub, every, 3 * l + 1, every)
        share_wait(gb, ks, 1)
        expand_back(l, 1)
        sum_mid(k, 0)
        sum_part(k, 1, ub, every, 3 * l + 1, every)
        sum_mid(k, 1)
        if top:
            for r in range(2):
                sum_part(last_out, r, act.at[l], every, 3 * l + 2, every)
            for r in range(2):
                sum_mid(last_out, r)
            sum_only(last_out)
        for u in (3 * l + 2, 3 * l + 1):
            sends_done(u)
        weight_grad(3 * l + 2, gb, act.at[l], every)
        rs1(3 * l + 2)
        weight_grad(3 * l + 1, a2.at[l], ub, every)
        rs1(3 * l + 1)
        if top:
            wait(recvB.at[bank(last_out), zl], br.at[last_out, 0])

            def finish(at):
                v = (xs[stream_rows(zl, at), :] + total(last_out, zl, pl.ds(at, TILE))
                     + smf[pl.ds(16 * l + 5, 1), :])
                tokst[0, pl.ds(at, TILE), :] = v.astype(BF16)

            tiles(finish)
            wait(sendB.at[bank(last_out), 1 - zl], bs.at[last_out, 0])
            back_start(tokst.at[0], out_ref, oss.at[0], osr.at[0])
        else:
            rs3(3 * l + 3)
            rs4(3 * l + 4)
        mask_keys(l)
        norm_back(k, 0, l, 1, n2, r2, hb, ks + 1)
        rs2(3 * l + 2)
        share_wait(hb, ks + 1, 0)
        mix_back(l, 0)
        attention_back(l, 0)
        norm_back(k, 1, l, 1, n2, r2, hb, ks + 1)
        rs2(3 * l + 1)
        share_wait(hb, ks + 1, 1)
        mix_back(l, 1)
        attention_back(l, 1)
        k += 1
        sum_part(k, 0, dqkv, qkvcols, 3 * l, qkvcols)
        sum_part(k, 1, dqkv, qkvcols, 3 * l, qkvcols)
        sum_mid(k, 0)
        sum_mid(k, 1)
        if bottom:
            sum_only(k)
        for row, cols in ((6, qcols), (7, vcols)):
            sg[16 * l + row:16 * l + row + 1, mine] = jnp.sum(
                dqkv[:, cols].astype(F32), axis=0, keepdims=True)
        sends_done(3 * l)
        weight_grad(3 * l, a1.at[l], dqkv, qkvcols)
        weight_grad(3 * l, hb, o.at[l], ocols)
        rs1(3 * l)
        rs3(3 * l + 2)
        if top:
            back_wait(tokst.at[0], out_ref, oss.at[0], osr.at[0])
        else:
            rs4(3 * l + 3)
        if not bottom:
            norm_back(k, 0, l, 0, n1, r1, gb, ks + 2)
            norm_back(k, 1, l, 0, n1, r1, gb, ks + 2)
        else:
            wait(recvB.at[bank(k), zl], br.at[k, 0])
            acc_clear()
            tiles(lambda at: norm_back_tile(k, zl, at, l, 0, n1, r1, None))
            acc_out(0, 16 * l, None)
            acc_out(1, 16 * l + 1, None)
            wait(sendB.at[bank(k), 1 - zl], bs.at[k, 0])
            back_start(tokst.at[0], igrecv, oss.at[1], osr.at[1])
        if bottom:
            rs3(3 * l + 1)
            rs2(3 * l)
        else:
            rs2(3 * l)
            rs3(3 * l + 1)
            rs4(3 * l + 2)
        k += 1
        ks += 2

    for l in range(layers):
        for cols, row, at in up_tiles:
            row = 16 * l + 8 + row
            sg[row:row + 1, lanes_at(at, 1)] = upg[8 * l:8 * l + 1, cols]
    for j in range(3):
        small_scatter(j)
    rs3(0)
    small_scatter(3)
    rs4(2)
    rs4(1)
    back_wait(tokst.at[0], igrecv, oss.at[1], osr.at[1])
    ig_ref[...] = igrecv[...].astype(F32)
    rs4(0)
    store_wait(0)
    store_wait(1)
    land_sent(cot, cts)


def shards(tokens, cotangent, image_mask, qkv_weight, out_weight, up_weight, down_weight,
           qv_bias, up_bias, out_bias, down_bias, attn_gain, attn_shift, mlp_gain, mlp_shift):
    images_here, rows_real, width = tokens.shape
    layers = qkv_weight.shape[0]
    hq = qkv_weight.shape[3]
    fq = up_weight.shape[2]
    lanes = lax.axis_size("tensor")
    groups = lax.axis_size("dp") // 8
    assert images_here == 1 and lanes == 4 and width == fq == 4 * hq
    kb = width // 8
    slot = -(-rows_real // TILE) * TILE
    half = 2 * slot
    rows_all = 4 * slot
    units = 3 * layers
    dp = lax.axis_index("dp")
    z = lax.axis_index("tensor")
    d8 = dp % 8

    position = z * rows_real + jnp.arange(rows_real)
    keep = (position < VALID).astype(BF16)[:, None] * image_mask.astype(BF16)[0]
    pad = ((0, slot - rows_real), (0, 0))
    tok = jnp.pad(tokens[0], pad)
    cot = jnp.pad(cotangent[0] * keep, pad)

    here = qkv_weight.shape[1]
    weights = (qkv_weight.reshape(layers, here, 3 * hq), out_weight, up_weight, down_weight)
    smalls = (jnp.concatenate([attn_gain[:, None], attn_shift[:, None], mlp_gain[:, None],
                               mlp_shift[:, None], out_bias[:, None], down_bias[:, None], qv_bias], 1),
              up_bias)
    if groups > 1:
        weights = tuple(lax.dynamic_slice_in_dim(
            lax.all_gather(w, "dp", axis=1, tiled=True), d8 * kb, kb, 1) for w in weights)
        both = ("dp", "tensor")
        at = d8 * lanes + z
        smalls = tuple(lax.dynamic_slice_in_dim(
            lax.all_gather(v, both, axis=v.ndim - 1, tiled=True),
            at * (n // (8 * lanes)), n // (8 * lanes), v.ndim - 1)
            for v, n in zip(smalls, (width, 4 * fq)))

    window = smalls[0].shape[2]
    tile = lanes * window
    wide = jnp.where(jnp.arange(tile) // window == z, jnp.tile(smalls[0], (1, 1, lanes)), 0)
    ups = jnp.where(jnp.arange(lanes)[:, None] == z, smalls[1][:, None, :], 0)
    small_in = jnp.concatenate([wide, ups, jnp.zeros((layers, 4, tile), BF16)], 1)
    small_in = small_in.reshape(16 * layers, tile)

    out_shapes = (
        jax.ShapeDtypeStruct((slot, width), BF16),
        jax.ShapeDtypeStruct((slot, width), F32),
        jax.ShapeDtypeStruct((layers, kb, 3 * hq), F32),
        jax.ShapeDtypeStruct((layers, kb, hq), F32),
        jax.ShapeDtypeStruct((layers, kb, fq), F32),
        jax.ShapeDtypeStruct((layers, kb, fq), F32),
        jax.ShapeDtypeStruct((16 * layers, tile), F32),
    )
    V = pltpu.VMEM
    D = lambda *s: pltpu.SemaphoreType.DMA(s)
    sums, shares = 4 * layers, 4 * layers
    scratch = [
        V((units, width, fq), BF16),
        V((half, width), F32), V((half, width), F32),
        V((layers, half, width), BF16), V((layers, half, width), BF16),
        V((layers, half, 1), F32), V((layers, half, 1), F32),
        V((layers, rows_all, width), BF16), V((layers, rows_all, width), BF16),
        V((layers, rows_all, 3 * hq), BF16), V((layers, rows_all, hq), BF16),
        V((layers, rows_all, fq), BF16), V((layers, rows_all, fq), BF16),
        V((rows_all, width), BF16), V((rows_all, width), BF16),
        V((rows_all, fq), BF16), V((rows_all, hq), BF16), V((rows_all, 3 * hq), BF16),
        V((rows_all, hq), F32), V((rows_all, hq), F32), V((3, 8, width), F32),
        V((2, rows_all, hq), BF16),
        V((2, slot, width), F32),
        V((2, slot, width), BF16), V((2, 2, slot, width), BF16),
        V((3, 2, slot, width), BF16), V((3, 2, slot, width), BF16),
        V((2, slot, width), BF16), V((2, slot, width), BF16),
        V((slot, width), BF16),
        V((16 * layers, width), BF16), V((4, 16 * layers, tile), BF16),
        V((16 * layers, width), F32), V((8 * layers, hq), F32),
        V((8 * layers, fq), F32), V((8 * layers, fq), F32), V((16 * layers, width), F32),
        V((16 * layers, width // 2), F32), V((16 * layers, width // 4), F32),
        V((16 * layers, tile), F32), V((4, 16 * layers, tile), F32),
        V((units, 2, kb, fq), BF16), V((units, 2, 2 * kb, fq), BF16), V((units, 2, kb, fq), BF16),
        D(units + 1, 2, 2), D(units + 1, 2, 2), D(units + 1, 2, 2), D(units + 1, 2, 2),
        D(units + 1, 2), D(units + 1, 2),
        D(sums, 2), D(sums, 2), D(sums, 2), D(sums, 2), D(shares, 2), D(shares, 2),
        D(2), D(2), D(2), D(2), D(2), D(2), D(3), D(3), D(3), D(4), D(3), D(3), D(3), D(4),
        D(units, 2), D(units, 2), D(units, 2, 2), D(units, 2, 2), D(units, 2), D(units, 2),
        V((2, kb, fq), F32), D(2, 2),
    ]
    any_spec = pl.BlockSpec(memory_space=pl.ANY)
    vmem_spec = pl.BlockSpec(memory_space=pltpu.VMEM)
    out, ig, *gws, sg = pl.pallas_call(
        functools.partial(kernel, layers, rows_real),
        out_shape=out_shapes,
        in_specs=[any_spec] * 6 + [vmem_spec],
        out_specs=(any_spec, vmem_spec, any_spec, any_spec, any_spec, any_spec, vmem_spec),
        scratch_shapes=scratch,
        compiler_params=pltpu.CompilerParams(
            collective_id=0, has_side_effects=True, vmem_limit_bytes=int(63.5 * 2 ** 20)),
        cost_estimate=pl.CostEstimate(
            flops=int(1e11), bytes_accessed=int(1e8), transcendentals=0),
    )(tok, cot, *weights, small_in)

    if groups > 1:
        wide = (jnp.zeros((layers, width, gw.shape[2]), F32) for gw in gws)
        gws = [lax.psum_scatter(lax.dynamic_update_slice_in_dim(zero, gw, d8 * kb, 1), "dp",
                                scatter_dimension=1, tiled=True) for zero, gw in zip(wide, gws)]
    sg = sg.reshape(layers, 16, tile)
    vecs = lax.dynamic_slice_in_dim(sg[:, :8], z * window, window, 2)
    ups_grad = lax.dynamic_slice_in_dim(sg[:, 8:12], z, 1, 1)[:, 0]
    if groups > 1:
        def own_part(v, n):
            wide = lax.dynamic_update_slice_in_dim(
                jnp.zeros(v.shape[:-1] + (n,), F32), v, at * v.shape[-1], v.ndim - 1)
            return lax.psum_scatter(wide, both, scatter_dimension=v.ndim - 1, tiled=True)

        vecs, ups_grad = own_part(vecs, width), own_part(ups_grad, 4 * fq)
    return (
        out[:rows_real][None],
        ig[:rows_real][None],
        gws[0].reshape(layers, here, 3, hq),
        gws[1],
        gws[2],
        gws[3],
        vecs[:, 6:8],
        ups_grad,
        vecs[:, 4],
        vecs[:, 5],
        vecs[:, 0],
        vecs[:, 1],
        vecs[:, 2],
        vecs[:, 3],
    )


def solution(mesh):
    both = ("dp", "tensor")
    rows = P("dp", "tensor", None)
    cols = P(None, "dp", "tensor")
    vec = P(None, both)
    return jax.shard_map(
        shards,
        mesh=mesh,
        in_specs=(rows, rows, P("dp"), P(None, "dp", None, "tensor"), cols, cols, cols,
                  P(None, None, both), vec, vec, vec, vec, vec, vec, vec),
        out_specs=(rows, rows, P(None, "dp", None, "tensor"), cols, cols, cols,
                   P(None, None, both), vec, vec, vec, vec, vec, vec, vec),
        check_vma=False,
    )
```

```python
import functools

import jax
import jax.numpy as jnp
from jax import lax
from jax.experimental import pallas as pl
from jax.experimental.pallas import tpu as pltpu
from jax.sharding import PartitionSpec as P

HD = 64
VALID = 577
EPS = 1e-06
ROOT_HALF = 0.7071067811865476
INV_ROOT_2PI = 0.3989422804014327
FAR_BELOW = -1e30
MESH = pl.DeviceIdType.MESH
F32 = jnp.float32
BF16 = jnp.bfloat16
TILE = 32
NT = 256


def dot_nn(a, b):
    return lax.dot_general(a, b, (((1,), (0,)), ((), ())), preferred_element_type=F32)


def dot_nt(a, b):
    return lax.dot_general(a, b, (((1,), (1,)), ((), ())), preferred_element_type=F32)


def dot_tn(a, b):
    return lax.dot_general(a, b, (((0,), (0,)), ((), ())), preferred_element_type=F32)


def loop(n, body):
    def step(i, carry):
        body(i)
        return carry

    lax.fori_loop(0, n, step, 0)


def aligned(v, m):
    return pl.multiple_of(v, m)


def kernel(
    layers, rows_real,
    tok, cot, wqkv, wout, wup, wdown, *more,
):
    vecs, qv_in, up_in, rest = more[:6], more[6], more[7], more[8:]
    (
        out_ref, ig_ref, gqkv, gout, gup, gdown, sg_out,
        W, xs, gs, n1, n2, r1, r2, a1, a2, qkv, o, act, dgl,
        gb, hb, ub, ob, dqkv, dk_acc, dv_acc, acc, kmask,
        own, sendA, recvA, sendB, recvB, tokst, cotst, igrecv,
        small, smz, smf, qb, upb, upg, sg, sgy, sgx, sgc, sgz,
        recv1, recv2, recv4,
        s0s, s0r, s1s, s1r, s2s, s2r,
        as_, ar, bs, br, cs, cr,
        tks, tkr, cts, ctr, oss, osr, sms, smr, smzs, smzr, sgs, sgr, sgzs, sgzr,
        g1s, g1r, g2s, g2r, g4s, g4r, stage, sts, smrows, small_in,
    ) = rest
    width = xs.shape[1]
    half = xs.shape[0]
    slot = half // 2
    rows_all = 2 * half
    kb = wup.shape[1]
    blk = 2 * kb
    hq = o.shape[2]
    fq = act.shape[2]
    heads = hq // HD
    wn = width // NT

    dp = lax.axis_index("dp")
    z = lax.axis_index("tensor")
    base = (dp // 8) * 8
    d8 = dp % 8
    y, x, c = d8 // 4, (d8 // 2) % 2, d8 % 2
    zh, zl = z // 2, z % 2
    q = zl + 2 * c
    z2 = (z + 2) % 4
    home = c == zh

    def dev(yy, xx, cc, zz):
        return (base + yy * 4 + xx * 2 + cc, zz)

    sib = dev(y, x, 1 - c, z)
    xn = dev(y, 1 - x, c, z)
    yn = dev(1 - y, x, c, z)
    zp = dev(y, x, c, z + 1 - 2 * zl)
    far = dev(y, x, c, z2)
    swap = dev(y, x, zh, 2 * c + zl)

    def rc(src, dst, ss, rs, to):
        return pltpu.make_async_remote_copy(
            src_ref=src, dst_ref=dst, send_sem=ss, recv_sem=rs,
            device_id=to, device_id_type=MESH)

    def wait(ref, sem):
        pltpu.make_async_copy(ref, ref, sem).wait()

    barrier = pltpu.get_barrier_semaphore()
    greet = [xn, yn, sib]
    for k in range(1, 4):
        for cc in range(2):
            greet.append(dev(y, x, cc, (z + k) % 4))
    for to in greet:
        pl.semaphore_signal(barrier, inc=1, device_id=to, device_id_type=MESH)
    pl.semaphore_wait(barrier, len(greet))

    def rows_of(yy, xx):
        return aligned((2 * yy + xx) * blk, blk)

    my_rows = pl.ds(aligned(d8 * kb, kb), kb)
    own_blk = rows_of(y, x)
    x_blk = rows_of(y, 1 - x)
    y_blk = rows_of(1 - y, x)
    diag_blk = rows_of(1 - y, 1 - x)

    units = 3 * layers
    cut = 2 * hq
    pieces = [(0, slice(0, cut)), (0, slice(cut, fq))] + [(u, slice(0, fq)) for u in range(1, units)]

    def piece(p, at, n):
        u, cols = pieces[p]
        return W.at[u, pl.ds(at, n), cols]

    def sources(p):
        u, cols = pieces[p]
        l, part = u // 3, u % 3
        if part:
            return [((wup, wdown)[part - 1].at[l], cols)]
        found = [(wqkv.at[l, :, slice(cols.start, min(cols.stop, 3 * hq))],
                  slice(cols.start, min(cols.stop, 3 * hq)))]
        if cols.stop > 3 * hq:
            found.append((wout.at[l], slice(3 * hq, 4 * hq)))
        return found

    def s0_start(p):
        u = pieces[p][0]
        for i, (src, cols) in enumerate(sources(p)):
            dst = W.at[u, my_rows, cols]
            rc(src, dst, s0s.at[p, 0, i], s0r.at[p, c, i], dev(y, x, zh, z2)).start()

            @pl.when(home)
            def _():
                pltpu.make_async_copy(src, dst, s0r.at[p, c, i]).start()

            @pl.when(jnp.logical_not(home))
            def _():
                rc(src, dst, s0s.at[p, 1, i], s0r.at[p, c, i], sib).start()

    def s0_wait(p):
        u = pieces[p][0]
        for j in range(2):
            for i, (src, cols) in enumerate(sources(p)):
                wait(W.at[u, pl.ds(own_blk + j * kb, kb), cols], s0r.at[p, j, i])

    def s1_start(p):
        for j in range(2):
            ref = piece(p, own_blk + j * kb, kb)
            rc(ref, ref, s1s.at[p, 0, j], s1r.at[p, 0, j], xn).start()
            ref = piece(p, own_blk + (1 - j) * kb, kb)
            rc(ref, ref, s1s.at[p, 1, j], s1r.at[p, 1, j], yn).start()

    def s1_wait(p, j):
        wait(piece(p, x_blk + j * kb, kb), s1r.at[p, 0, j])
        wait(piece(p, y_blk + (1 - j) * kb, kb), s1r.at[p, 1, j])

    def s2_start(p):
        ref = piece(p, x_blk, kb)
        rc(ref, ref, s2s.at[p, 1], s2r.at[p, 1], yn).start()
        ref = piece(p, y_blk + kb, kb)
        rc(ref, ref, s2s.at[p, 0], s2r.at[p, 0], xn).start()

    def s2_wait(p):
        s1_wait(p, 1)
        wait(piece(p, diag_blk, kb), s2r.at[p, 1])
        wait(piece(p, diag_blk + kb, kb), s2r.at[p, 0])

    def ready(u):
        for p in range(len(pieces)):
            if pieces[p][0] == u:
                s2_wait(p)

    def sends_done(unit):
        for p in range(len(pieces)):
            if pieces[p][0] != unit:
                continue
            for i, (src, cols) in enumerate(sources(p)):
                ref = W.at[unit, my_rows, cols]
                wait(ref, s0s.at[p, 0, i])

                @pl.when(jnp.logical_not(home))
                def _():
                    wait(ref, s0s.at[p, 1, i])

            ref = piece(p, own_blk, kb)
            for j in range(2):
                for i in range(2):
                    wait(ref, s1s.at[p, j, i])
                wait(ref, s2s.at[p, j])

    def pump(p):
        s1_wait(p, 0)
        s2_start(p)
        if p + 1 < len(pieces):
            s0_wait(p + 1)
            s1_start(p + 1)
        if p + 3 < len(pieces):
            s0_start(p + 3)
        elif p + 3 == len(pieces):
            land_start(cot, cotst, cts, ctr)

    def land_start(src, dst, ss, rs):
        @pl.when(home)
        def _():
            pltpu.make_async_copy(src, dst.at[zl], rs.at[zl]).start()

        @pl.when(jnp.logical_not(home))
        def _():
            rc(src, dst.at[zl], ss.at[0], rs.at[zl], swap).start()

    def land_pass(src, dst, ss, rs):
        wait(dst.at[zl], rs.at[zl])
        rc(dst.at[zl], dst.at[zl], ss.at[1], rs.at[zl], zp).start()

    def land_wait(src, dst, ss, rs):
        wait(dst.at[1 - zl], rs.at[1 - zl])

    def land_sent(src, ss):
        @pl.when(jnp.logical_not(home))
        def _():
            wait(src, ss.at[0])

        wait(src, ss.at[1])

    def back_start(src, dst, ss, rs):
        @pl.when(home)
        def _():
            pltpu.make_async_copy(src, dst, rs).start()

        @pl.when(jnp.logical_not(home))
        def _():
            rc(src, dst, ss, rs, swap).start()

    def back_wait(src, dst, ss, rs):
        wait(dst, rs)

        @pl.when(jnp.logical_not(home))
        def _():
            wait(src, ss)

    tile_lanes = small_in.shape[1]

    def lanes_at(at, n):
        return pl.ds(aligned(at * tile_lanes, tile_lanes), n * tile_lanes)

    def column_start(src, dst, ss, rs):
        for k in range(1, 4):
            rc(src, dst.at[z], ss.at[k - 1], rs.at[z], dev(y, x, c, (z + k) % 4)).start()

    def column_wait(src, dst, ss, rs):
        for k in range(1, 4):
            wait(dst.at[(z + k) % 4], rs.at[(z + k) % 4])
            wait(src, ss.at[k - 1])

    def small_gather():
        column_wait(small_in, smz, smzs, smzr)
        smz[z] = small_in[...]
        v = smz[0].astype(F32)
        for k in range(1, 4):
            v = v + smz[k].astype(F32)
        small[:, lanes_at(d8, 1)] = v.astype(BF16)
        land_pass(tok, tokst, tks, tkr)
        for k, (at, n, to) in enumerate(((d8, 1, sib), (2 * (d8 // 2), 2, xn), (4 * y, 4, yn))):
            mine_now = small.at[:, lanes_at(at, n)]
            cp = rc(mine_now, mine_now, sms.at[k], smr.at[k], to)
            cp.start()
            cp.wait()

    def small_scatter(k):
        if k < 3:
            at, other, n, into, to = (
                (4 * y, 4 * (1 - y), 4, sgy, yn),
                (4 * y + 2 * x, 4 * y + 2 * (1 - x), 2, sgx, xn),
                (d8, 4 * y + 2 * x + 1 - c, 1, sgc, sib))[k]
            cp = rc(sg.at[:, lanes_at(other, n)], into, sgs.at[k], sgr.at[k], to)
            cp.start()
            cp.wait()
            sg[:, lanes_at(at, n)] += into[...]
        else:
            sgz[z] = sg[:, lanes_at(d8, 1)]
            column_start(sgz.at[z], sgz, sgzs, sgzr)
            column_wait(sgz.at[z], sgz, sgzs, sgzr)
            sg_out[...] = (sgz[0] + sgz[1]) + (sgz[2] + sgz[3])

    def round_rows(r):
        return pl.ds(r * half, half)

    def slot_at(r, h):
        return aligned(r * half + h * slot, slot)

    def share_start(ref, k, r):
        part = ref.at[pl.ds(slot_at(r, c), slot)]
        rc(part, part, cs.at[k, r], cr.at[k, r], sib).start()

    def share_wait(ref, k, r):
        part = ref.at[pl.ds(slot_at(r, 1 - c), slot)]
        wait(part, cr.at[k, r])
        wait(part, cs.at[k, r])

    last_out = 2 * layers - 1
    last_sum = 4 * layers - 1

    def bank(k):
        return 2 if k == last_out else (k + (k > last_out)) % 2

    def sum_part(k, r, lhs, cols, u, wcols):
        def step(n):
            ncols = pl.ds(aligned(n * NT, NT), NT)
            rows = jnp.concatenate(
                [lhs[pl.ds(slot_at(r, c), slot), cols], lhs[pl.ds(slot_at(r, 1 - c), slot), cols]], 0)
            v = dot_nt(rows, W[u, ncols, wcols])
            own[r, :, ncols] = v[:slot]
            sendA[r, :, ncols] = v[slot:].astype(BF16)

        loop(wn, step)
        rc(sendA.at[r], recvA.at[k % 2, r], as_.at[k, r], ar.at[k, r], sib).start()

    def sum_mid(k, r):
        wait(recvA.at[k % 2, r], ar.at[k, r])
        wait(sendA.at[r], as_.at[k, r])

        def step(i):
            rows = pl.ds(aligned(i * TILE, TILE), TILE)
            sendB[bank(k), r, rows, :] = (own[r, rows, :] + recvA[k % 2, r, rows, :].astype(F32)).astype(BF16)

        loop(slot // TILE, step)
        if k not in (last_out, last_sum):
            rc(sendB.at[bank(k), r], recvB.at[bank(k), r], bs.at[k, r], br.at[k, r], zp).start()

    def sum_only(k):
        rc(sendB.at[bank(k), 1 - zl], recvB.at[bank(k), 1 - zl], bs.at[k, 0], br.at[k, 0], zp).start()

    def sum_wait(k, r):
        wait(recvB.at[bank(k), r], br.at[k, r])

    def sum_sent(k, r):
        wait(sendB.at[bank(k), r], bs.at[k, r])

    def total(k, r, rows):
        return sendB[bank(k), r, rows, :].astype(F32) + recvB[bank(k), r, rows, :].astype(F32)

    def tiles(body):
        def step(i):
            body(aligned(i * TILE, TILE))

        loop(slot // TILE, step)

    def stream_rows(r, at):
        return pl.ds(aligned(r * slot + at, TILE), TILE)

    def full_rows(r, at):
        return pl.ds(aligned(slot_at(r, c) + at, TILE), TILE)

    def norm_tile(v, r, at, l, which, n_ref, r_ref, a_ref):
        gain = smf[pl.ds(16 * l + 2 * which, 1), :]
        shift = smf[pl.ds(16 * l + 2 * which + 1, 1), :]
        centre = v - jnp.mean(v, axis=1, keepdims=True)
        inv = lax.rsqrt(jnp.mean(centre * centre, axis=1, keepdims=True) + EPS)
        n = centre * inv
        rows = stream_rows(r, at)
        n_ref[l, rows, :] = n.astype(BF16)
        r_ref[l, rows, :] = inv
        a_ref[l, full_rows(r, at), :] = (n * gain + shift).astype(BF16)

    lane = lax.broadcasted_iota(jnp.int32, (1, hq), 1)
    QC = half

    def head_mask(h):
        return jnp.logical_and(lane >= h * HD, lane < (h + 1) * HD)

    def spare(h):
        return lane == (hq - 1 if h < heads - 1 else 0)

    qcols = slice(0, hq)
    kcols = slice(hq, 2 * hq)
    vcols = slice(2 * hq, 3 * hq)
    qkvcols = slice(0, 3 * hq)
    ocols = slice(3 * hq, 4 * hq)
    every = slice(0, fq)

    def mask_keys(l):
        for s in range(4):
            r, h = s // 2, s % 2
            rows = pl.ds(s * slot, slot)
            within = lax.broadcasted_iota(jnp.int32, (slot, 1), 0)
            valid = jnp.logical_and(within < rows_real, (2 * h + r) * rows_real + within < VALID)
            low = jnp.where(valid, 0.0, FAR_BELOW)
            keys = qkv[l, rows, kcols].astype(F32)
            for j, h in ((0, 0), (1, heads - 1)):
                kmask[j, rows, :] = jnp.where(spare(h), low, keys).astype(BF16)

    def softmax_of(qm, h):
        s = dot_nt(jnp.where(spare(h), 1.0, qm).astype(BF16), kmask[0 if h < heads - 1 else 1])
        e = jnp.exp(s - jnp.max(s, axis=1, keepdims=True))
        return e * (1.0 / jnp.sum(e, axis=1, keepdims=True))

    def attention(l, r, which):
        rows = round_rows(r)
        qc = qkv[l, rows, qcols].astype(F32)
        values = qkv[l, :, vcols]
        for h in which:
            m = head_mask(h)
            qm = jnp.where(m, qc * (HD ** -0.5), 0.0)
            p = softmax_of(qm, h).astype(BF16)
            mixed = dot_nn(p, values)
            pair = slice(h // 2 * 2 * HD, (h // 2 + 1) * 2 * HD)
            old = o[l, rows, pair]
            o[l, rows, pair] = jnp.where(m[:, pair], mixed[:, pair], old.astype(F32)).astype(BF16)

    def attention_back(l, r):
        rows = round_rows(r)
        qc = qkv[l, rows, qcols].astype(F32)
        oc = ob[rows, :].astype(F32)
        keys, values = qkv[l, :, kcols], qkv[l, :, vcols]
        dq = jnp.zeros((QC, hq), F32)
        for h in range(heads):
            m = head_mask(h)
            qm = jnp.where(m, qc * (HD ** -0.5), 0.0)
            om = jnp.where(m, oc, 0.0).astype(BF16)
            p = softmax_of(qm, h)
            dprob = dot_nt(om, values)
            inner = jnp.sum(dprob * p, axis=1, keepdims=True)
            ds = (p * (dprob - inner)).astype(BF16)
            dq = jnp.where(m, dot_nn(ds, keys), dq)
            dk = dot_tn(ds, qm.astype(BF16))
            dv = dot_tn(p.astype(BF16), om)
            if r == 0 and h == 0:
                dk_acc[...] = dk
                dv_acc[...] = dv
            else:
                dk_acc[...] += dk
                dv_acc[...] += dv
        dqkv[rows, qcols] = (dq * (HD ** -0.5)).astype(BF16)
        if r == 1:
            dqkv[:, kcols] = dk_acc[...].astype(BF16)
            dqkv[:, vcols] = dv_acc[...].astype(BF16)

    parts = [(u, every) for u in range(units)] + [(0, ocols)]
    parts[0] = (0, qkvcols)

    def kept(u):
        return units - 1 if u == 0 else u

    def rs1(p):
        u, cols = parts[p]
        for rows, j, to in ((diag_blk, 0, xn), (diag_blk + kb, 1, yn)):
            ref = W.at[kept(u), pl.ds(rows, kb), cols]
            rc(ref, recv1.at[u, j, :, cols], g1s.at[p, j], g1r.at[p, j], to).start()
        for rows, j, to in ((x_blk, 0, xn), (y_blk + kb, 1, yn)):
            ref = W.at[kept(u), pl.ds(rows, kb), cols]
            rc(ref, recv2.at[u, j, pl.ds(j * kb, kb), cols],
               g2s.at[p, j, j], g2r.at[p, j, j], to).start()

    RT = 64

    def add_rows(w, cols, at, refs, n):
        def step(i):
            off = aligned(i * RT, RT)
            rows = pl.ds(aligned(at + off, RT), RT)
            v = W[w, rows, cols].astype(F32)
            for ref in refs:
                v = v + ref[pl.ds(off, RT), cols].astype(F32)
            W[w, rows, cols] = v.astype(BF16)

        loop(n // RT, step)

    def rs2(p):
        u, cols = parts[p]
        for j in range(2):
            wait(recv1.at[u, j, :, cols], g1r.at[p, j])
            wait(recv1.at[u, j, :, cols], g1s.at[p, j])
        for rows, j, i, to in ((y_blk, 1, 0, yn), (x_blk + kb, 0, 1, xn)):
            add_rows(kept(u), cols, rows, [recv1.at[u, i]], kb)
            ref = W.at[kept(u), pl.ds(rows, kb), cols]
            rc(ref, recv2.at[u, j, pl.ds(i * kb, kb), cols],
               g2s.at[p, j, i], g2r.at[p, j, i], to).start()

    def rs3(p):
        u, cols = parts[p]
        for j in range(2):
            for i in range(2):
                part = recv2.at[u, j, pl.ds(i * kb, kb), cols]
                wait(part, g2r.at[p, j, i])
                wait(part, g2s.at[p, j, i])
        add_rows(kept(u), cols, own_blk, [recv2.at[u, 0], recv2.at[u, 1]], blk)

        @pl.when(home)
        def _():
            ref = W.at[kept(u), pl.ds(aligned(own_blk + (1 - c) * kb, kb), kb), cols]
            rc(ref, recv4.at[u, 0, :, cols], g4s.at[p, 0], g4r.at[p, 0], sib).start()
            ref = W.at[kept(u), pl.ds(aligned(own_blk + c * kb, kb), kb), cols]
            pltpu.make_async_copy(ref, recv4.at[u, 0, :, cols], g4r.at[p, 0]).start()

        @pl.when(jnp.logical_not(home))
        def _():
            for j in range(2):
                ref = W.at[kept(u), pl.ds(own_blk + j * kb, kb), cols]
                rc(ref, recv4.at[u, 1, :, cols], g4s.at[p, j], g4r.at[p, 1],
                   dev(y, x, j, z2)).start()

    def rs4(p):
        u, cols = parts[p]
        for j in range(2):
            wait(recv4.at[u, j, :, cols], g4r.at[p, j])
        wait(recv4.at[u, 0, :, cols], g4s.at[p, 0])

        @pl.when(jnp.logical_not(home))
        def _():
            wait(recv4.at[u, 0, :, cols], g4s.at[p, 1])

        slot_of = stored.index(None) if None in stored else len(order) % 2
        if stored[slot_of] is not None:
            store_wait(slot_of)

        def step(i):
            rows = pl.ds(aligned(i * RT, RT), RT)
            stage[slot_of, rows, cols] = (recv4[u, 0, rows, cols].astype(F32)
                                          + recv4[u, 1, rows, cols].astype(F32))

        loop(kb // RT, step)
        stored[slot_of] = p
        order.append(p)
        for src, dst, sem in stores(slot_of):
            pltpu.make_async_copy(src, dst, sem).start()

    stored, order = [None, None], []

    def stores(slot_of):
        p = stored[slot_of]
        u = parts[p][0]
        l, part = u // 3, u % 3
        if part:
            return [(stage.at[slot_of], (gup, gdown)[part - 1].at[l], sts.at[slot_of, 0])]
        both = [(stage.at[slot_of, :, qkvcols], gqkv.at[l], sts.at[slot_of, 0]),
                (stage.at[slot_of, :, ocols], gout.at[l], sts.at[slot_of, 1])]
        return both if u else both[:1] if p == 0 else both[1:]

    def store_wait(slot_of):
        for src, dst, sem in stores(slot_of):
            pltpu.make_async_copy(src, dst, sem).wait()

    def project(l, r):
        rows = round_rows(r)
        for j in range(3):
            cols = slice(j * hq, (j + 1) * hq)
            v = dot_nn(a1[l, rows, :], W[3 * l, :, cols])
            qkv[l, rows, cols] = (v + qb[8 * l + j:8 * l + j + 1, :]).astype(BF16)

    def expand(l, r):
        rows = round_rows(r)

        def step(j):
            cols = pl.ds(aligned(j * NT, NT), NT)
            u = dot_nn(a2[l, rows, :], W[3 * l + 1, :, cols]) + upb[8 * l:8 * l + 1, cols]
            phi = 0.5 * (1.0 + lax.erf(u * ROOT_HALF))
            act[l, rows, cols] = (u * phi).astype(BF16)
            density = INV_ROOT_2PI * jnp.exp(-0.5 * u * u)
            dgl[l, rows, cols] = (phi + u * density).astype(BF16)

        loop(fq // NT, step)

    def expand_back(l, r):
        rows = round_rows(r)

        def step(j):
            cols = pl.ds(aligned(j * NT, NT), NT)
            v = dot_nn(gb[rows, :], W[3 * l + 2, :, cols]) * dgl[l, rows, cols].astype(F32)
            low = v.astype(BF16)
            ub[rows, cols] = low
            upg[8 * l:8 * l + 1, cols] += jnp.sum(low.astype(F32), axis=0, keepdims=True)

        loop(fq // NT, step)

    def mix_back(l, r):
        rows = round_rows(r)
        ob[rows, :] = dot_nn(hb[rows, :], W[3 * l, :, ocols]).astype(BF16)

    def weight_grad(u, lhs, rhs, cols):
        def step(t):
            rows = pl.ds(aligned(t * NT, NT), NT)
            W[kept(u), rows, cols] = dot_tn(lhs[:, rows], rhs[...]).astype(BF16)

        loop(wn, step)

    def acc_add(j, v):
        acc[j] += jnp.sum(v.reshape(TILE // 8, 8, width), axis=0)

    once = (zl == 0).astype(F32)

    def acc_out(j, row, share):
        v = jnp.sum(acc[j], axis=0, keepdims=True)
        sg[row:row + 1, :] = v if share is None else v * share

    def acc_clear():
        acc[...] = jnp.zeros_like(acc)

    def norm_back_tile(k, r, at, l, which, n_ref, r_ref, low_ref):
        rows = stream_rows(r, at)
        da = total(k, r, pl.ds(at, TILE))
        n = n_ref[l, rows, :].astype(F32)
        e = da * smf[pl.ds(16 * l + 2 * which, 1), :]
        inner = jnp.mean(e * n, axis=1, keepdims=True)
        middle = jnp.mean(e, axis=1, keepdims=True)
        g = gs[rows, :] + r_ref[l, rows, :] * (e - middle - n * inner)
        acc_add(0, da * n)
        acc_add(1, da)
        if low_ref is None:
            tokst[0, pl.ds(at, TILE), :] = g.astype(BF16)
        else:
            acc_add(2, g)
            gs[rows, :] = g
            low_ref[full_rows(r, at), :] = g.astype(BF16)

    def norm_back(k, r, l, which, n_ref, r_ref, low_ref, low_k):
        sum_wait(k, r)
        if r == 0:
            acc_clear()
        tiles(lambda at: norm_back_tile(k, r, at, l, which, n_ref, r_ref, low_ref))
        share_start(low_ref, low_k, r)
        sum_sent(k, r)
        if r == 1:
            acc_out(0, 16 * l + 2 * which, once)
            acc_out(1, 16 * l + 2 * which + 1, once)
            acc_out(2, 16 * l + 4 if which == 1 else 16 * (l - 1) + 5, once)

    window = vecs[0].shape[1]
    place = (lax.broadcasted_iota(jnp.int32, (window, tile_lanes), 1)
             == z * window + lax.broadcasted_iota(jnp.int32, (window, tile_lanes), 0))
    place = jnp.where(place, 1.0, 0.0).astype(BF16)
    smrows[...] = jnp.zeros_like(smrows)
    for j, ref in enumerate(vecs):
        v = dot_nn(ref[...], place)
        for l in range(layers):
            smrows[16 * l + j:16 * l + j + 1, :] = v[l:l + 1]
    for l in range(layers):
        smrows[16 * l + 6:16 * l + 8, :] = dot_nn(qv_in[l], place)
        smrows[pl.ds(16 * l + 8 + z, 1), :] = up_in[l:l + 1, :].astype(F32)
    small_in[...] = smrows[...].astype(BF16)
    column_start(small_in, smz, smzs, smzr)
    land_start(tok, tokst, tks, tkr)
    s0_start(0)
    s0_start(1)
    sg[...] = jnp.zeros_like(sg)
    qb[...] = jnp.zeros_like(qb)
    upg[...] = jnp.zeros_like(upg)
    small_gather()
    s0_wait(0)
    s1_start(0)
    s0_start(2)
    smf[...] = small[...].astype(F32)
    mine = pl.ds(aligned(q * hq, hq), hq)
    up_tiles = [(slice(j * tile_lanes, (j + 1) * tile_lanes), j % 4, 2 * q + j // 4)
                for j in range(fq // tile_lanes)]
    for l in range(layers):
        for j, row in ((0, 6), (2, 7)):
            qb[8 * l + j:8 * l + j + 1, :] = smf[16 * l + row:16 * l + row + 1, mine]
        for cols, row, at in up_tiles:
            row = 16 * l + 8 + row
            upb[8 * l:8 * l + 1, cols] = smf[row:row + 1, lanes_at(at, 1)]

    s0_wait(1)
    s1_start(1)
    s0_start(3)
    s1_wait(0, 0)
    s2_start(0)
    land_wait(tok, tokst, tks, tkr)
    for r in range(2):
        def first(at, r=r):
            v = tokst[r, pl.ds(at, TILE), :].astype(F32)
            xs[stream_rows(r, at), :] = v
            norm_tile(v, r, at, 0, 0, n1, r1, a1)

        tiles(first)
        share_start(a1.at[0], 0, r)
    pump(1)
    ready(0)
    for r in range(2):
        share_wait(a1.at[0], 0, r)
        project(0, r)

    def stream_step(k, r, l_bias, row, l, which, n_ref, r_ref, a_ref, share_k):
        sum_wait(k, r)

        def body(at):
            rows = stream_rows(r, at)
            v = xs[rows, :] + total(k, r, pl.ds(at, TILE)) + smf[pl.ds(16 * l_bias + row, 1), :]
            xs[rows, :] = v
            norm_tile(v, r, at, l, which, n_ref, r_ref, a_ref)

        tiles(body)
        share_start(a_ref.at[l], share_k, r)
        sum_sent(k, r)

    for l in range(layers):
        final = l + 1 == layers
        k = 2 * l
        mask_keys(l)
        attention(l, 0, range(heads))
        if l == 0:
            pump(2)
        sum_part(k, 0, o.at[l], slice(0, hq), 3 * l, ocols)
        attention(l, 1, range(heads // 2))
        sum_mid(k, 0)
        attention(l, 1, range(heads // 2, heads))
        sum_part(k, 1, o.at[l], slice(0, hq), 3 * l, ocols)
        sum_mid(k, 1)
        if final:
            if layers == 1:
                land_pass(cot, cotst, cts, ctr)
            land_wait(cot, cotst, cts, ctr)
            acc_clear()
            for r in range(2):
                def first_back(at, r=r):
                    low = cotst[r, pl.ds(at, TILE), :]
                    gs[stream_rows(r, at), :] = low.astype(F32)
                    gb[full_rows(r, at), :] = low
                    acc_add(2, low.astype(F32))

                tiles(first_back)
                share_start(gb, 2 * layers, r)
            acc_out(2, 16 * (layers - 1) + 5, once)
        if final:
            pump(3 * l + 3)
        stream_step(k, 0, l, 4, l, 1, n2, r2, a2, 2 * l + 1)
        if not final:
            pump(3 * l + 3)
        ready(3 * l + 1)
        share_wait(a2.at[l], 2 * l + 1, 0)
        expand(l, 0)
        stream_step(k, 1, l, 4, l, 1, n2, r2, a2, 2 * l + 1)
        share_wait(a2.at[l], 2 * l + 1, 1)
        expand(l, 1)
        ready(3 * l + 2)
        if not final:
            for r in range(2):
                sum_part(k + 1, r, act.at[l], every, 3 * l + 2, every)
            for r in range(2):
                sum_mid(k + 1, r)
            pump(3 * l + 4)
            stream_step(k + 1, 0, l, 5, l + 1, 0, n1, r1, a1, 2 * l + 2)
            ready(3 * l + 3)
            share_wait(a1.at[l + 1], 2 * l + 2, 0)
            project(l + 1, 0)
            stream_step(k + 1, 1, l, 5, l + 1, 0, n1, r1, a1, 2 * l + 2)
            pump(3 * l + 5)
            share_wait(a1.at[l + 1], 2 * l + 2, 1)
            project(l + 1, 1)
            if l + 2 == layers:
                land_pass(cot, cotst, cts, ctr)

    land_sent(tok, tks)
    k = 2 * layers
    ks = 2 * layers

    def start_round(l, k, ks, r):
        share_wait(gb, ks, r)
        expand_back(l, r)
        if l == layers - 1 and r == 1:
            sum_mid(k, 0)
        sum_part(k, r, ub, every, 3 * l + 1, every)

    start_round(layers - 1, k, ks, 0)
    for l in reversed(range(layers)):
        top, bottom = l == layers - 1, l == 0
        start_round(l, k, ks, 1)
        sum_mid(k, 1)
        if top:
            for r in range(2):
                sum_part(last_out, r, act.at[l], every, 3 * l + 2, every)
            for r in range(2):
                sum_mid(last_out, r)
            sum_only(last_out)
        for u in (3 * l + 2, 3 * l + 1):
            sends_done(u)
        weight_grad(3 * l + 2, gb, act.at[l], every)
        rs1(3 * l + 2)
        weight_grad(3 * l + 1, a2.at[l], ub, every)
        rs1(3 * l + 1)
        if top:
            wait(recvB.at[bank(last_out), zl], br.at[last_out, 0])

            def finish(at):
                v = (xs[stream_rows(zl, at), :] + total(last_out, zl, pl.ds(at, TILE))
                     + smf[pl.ds(16 * l + 5, 1), :])
                tokst[0, pl.ds(at, TILE), :] = v.astype(BF16)

            tiles(finish)
            wait(sendB.at[bank(last_out), 1 - zl], bs.at[last_out, 0])
            back_start(tokst.at[0], out_ref, oss.at[0], osr.at[0])
        else:
            rs3(3 * l + 4)
            rs4(3 * l + 5)
        mask_keys(l)
        norm_back(k, 0, l, 1, n2, r2, hb, ks + 1)
        rs2(3 * l + 2)
        share_wait(hb, ks + 1, 0)
        mix_back(l, 0)
        attention_back(l, 0)
        norm_back(k, 1, l, 1, n2, r2, hb, ks + 1)
        rs2(3 * l + 1)
        if not top:
            rs3(3 * l + 3)
        share_wait(hb, ks + 1, 1)
        mix_back(l, 1)
        if bottom:
            weight_grad(0, hb, o.at[l], ocols)
            rs1(units)
        attention_back(l, 1)
        k += 1
        if bottom:
            weight_grad(0, a1.at[l], dqkv, qkvcols)
            rs1(0)
        sum_part(k, 0, dqkv, qkvcols, 3 * l, qkvcols)
        sum_part(k, 1, dqkv, qkvcols, 3 * l, qkvcols)
        sum_mid(k, 0)
        sum_mid(k, 1)
        if bottom:
            sum_only(k)
        for row, cols in ((6, qcols), (7, vcols)):
            sg[16 * l + row:16 * l + row + 1, mine] = jnp.sum(
                dqkv[:, cols].astype(F32), axis=0, keepdims=True)
        sends_done(3 * l)
        if not bottom:
            weight_grad(3 * l, a1.at[l], dqkv, qkvcols)
            weight_grad(3 * l, hb, o.at[l], ocols)
            rs1(3 * l)
            rs3(3 * l + 2)
            if top:
                back_wait(tokst.at[0], out_ref, oss.at[0], osr.at[0])
            norm_back(k, 0, l, 0, n1, r1, gb, ks + 2)
            rs2(3 * l)
            start_round(l - 1, k + 1, ks + 2, 0)
            norm_back(k, 1, l, 0, n1, r1, gb, ks + 2)
            sum_mid(k + 1, 0)
        else:
            rs3(2)
            rs2(units)
            rs4(4)
            rs3(1)
            rs2(0)
            wait(recvB.at[bank(k), zl], br.at[k, 0])
            acc_clear()
            tiles(lambda at: norm_back_tile(k, zl, at, l, 0, n1, r1, None))
            acc_out(0, 16 * l, None)
            acc_out(1, 16 * l + 1, None)
            wait(sendB.at[bank(k), 1 - zl], bs.at[k, 0])
            back_start(tokst.at[0], igrecv, oss.at[1], osr.at[1])
            rs3(units)
        k += 1
        ks += 2

    for l in range(layers):
        for cols, row, at in up_tiles:
            row = 16 * l + 8 + row
            sg[row:row + 1, lanes_at(at, 1)] = upg[8 * l:8 * l + 1, cols]
    small_scatter(0)
    rs3(0)
    for j in range(1, 4):
        small_scatter(j)
    rs4(3)
    rs4(2)
    rs4(1)
    rs4(units)
    back_wait(tokst.at[0], igrecv, oss.at[1], osr.at[1])
    ig_ref[...] = igrecv[...].astype(F32)
    rs4(0)
    store_wait(0)
    store_wait(1)
    land_sent(cot, cts)


def shards(tokens, cotangent, image_mask, qkv_weight, out_weight, up_weight, down_weight,
           qv_bias, up_bias, out_bias, down_bias, attn_gain, attn_shift, mlp_gain, mlp_shift):
    images_here, rows_real, width = tokens.shape
    layers = qkv_weight.shape[0]
    hq = qkv_weight.shape[3]
    fq = up_weight.shape[2]
    lanes = lax.axis_size("tensor")
    groups = lax.axis_size("dp") // 8
    assert images_here == 1 and lanes == 4 and layers > 1 and width == fq == 4 * hq
    kb = width // 8
    slot = -(-rows_real // TILE) * TILE
    half = 2 * slot
    rows_all = 4 * slot
    units = 3 * layers
    dp = lax.axis_index("dp")
    z = lax.axis_index("tensor")
    d8 = dp % 8

    position = z * rows_real + jnp.arange(rows_real)
    keep = (position < VALID).astype(BF16)[:, None] * image_mask.astype(BF16)[0]
    pad = ((0, slot - rows_real), (0, 0))
    tok = jnp.pad(tokens[0], pad)
    cot = jnp.pad(cotangent[0] * keep, pad)

    here = qkv_weight.shape[1]
    weights = (qkv_weight.reshape(layers, here, 3 * hq), out_weight, up_weight, down_weight)
    smalls = (attn_gain, attn_shift, mlp_gain, mlp_shift, out_bias, down_bias, qv_bias, up_bias)
    if groups > 1:
        weights = tuple(lax.dynamic_slice_in_dim(
            lax.all_gather(w, "dp", axis=1, tiled=True), d8 * kb, kb, 1) for w in weights)
        both = ("dp", "tensor")
        at = d8 * lanes + z
        smalls = tuple(lax.dynamic_slice_in_dim(
            lax.all_gather(v, both, axis=v.ndim - 1, tiled=True),
            at * (n // (8 * lanes)), n // (8 * lanes), v.ndim - 1)
            for v, n in zip(smalls, (width,) * 7 + (4 * fq,)))

    window = smalls[0].shape[1]
    tile = lanes * window

    out_shapes = (
        jax.ShapeDtypeStruct((slot, width), BF16),
        jax.ShapeDtypeStruct((slot, width), F32),
        jax.ShapeDtypeStruct((layers, kb, 3 * hq), F32),
        jax.ShapeDtypeStruct((layers, kb, hq), F32),
        jax.ShapeDtypeStruct((layers, kb, fq), F32),
        jax.ShapeDtypeStruct((layers, kb, fq), F32),
        jax.ShapeDtypeStruct((16 * layers, tile), F32),
    )
    V = pltpu.VMEM
    D = lambda *s: pltpu.SemaphoreType.DMA(s)
    sums, shares = 4 * layers, 4 * layers
    scratch = [
        V((units, width, fq), BF16),
        V((half, width), F32), V((half, width), F32),
        V((layers, half, width), BF16), V((layers, half, width), BF16),
        V((layers, half, 1), F32), V((layers, half, 1), F32),
        V((layers, rows_all, width), BF16), V((layers, rows_all, width), BF16),
        V((layers, rows_all, 3 * hq), BF16), V((layers, rows_all, hq), BF16),
        V((layers, rows_all, fq), BF16), V((layers, rows_all, fq), BF16),
        V((rows_all, width), BF16), V((rows_all, width), BF16),
        V((rows_all, fq), BF16), V((rows_all, hq), BF16), V((rows_all, 3 * hq), BF16),
        V((rows_all, hq), F32), V((rows_all, hq), F32), V((3, 8, width), F32),
        V((2, rows_all, hq), BF16),
        V((2, slot, width), F32),
        V((2, slot, width), BF16), V((2, 2, slot, width), BF16),
        V((3, 2, slot, width), BF16), V((3, 2, slot, width), BF16),
        V((2, slot, width), BF16), V((2, slot, width), BF16),
        V((slot, width), BF16),
        V((16 * layers, width), BF16), V((4, 16 * layers, tile), BF16),
        V((16 * layers, width), F32), V((8 * layers, hq), F32),
        V((8 * layers, fq), F32), V((8 * layers, fq), F32), V((16 * layers, width), F32),
        V((16 * layers, width // 2), F32), V((16 * layers, width // 4), F32),
        V((16 * layers, tile), F32), V((4, 16 * layers, tile), F32),
        V((units, 2, kb, fq), BF16), V((units, 2, 2 * kb, fq), BF16), V((units, 2, kb, fq), BF16),
        D(units + 1, 2, 2), D(units + 1, 2, 2), D(units + 1, 2, 2), D(units + 1, 2, 2),
        D(units + 1, 2), D(units + 1, 2),
        D(sums, 2), D(sums, 2), D(sums, 2), D(sums, 2), D(shares, 2), D(shares, 2),
        D(2), D(2), D(2), D(2), D(2), D(2), D(3), D(3), D(3), D(4), D(3), D(3), D(3), D(4),
        D(units + 1, 2), D(units + 1, 2), D(units + 1, 2, 2), D(units + 1, 2, 2),
        D(units + 1, 2), D(units + 1, 2),
        V((2, kb, fq), F32), D(2, 2),
        V((16 * layers, tile), F32), V((16 * layers, tile), BF16),
    ]
    any_spec = pl.BlockSpec(memory_space=pl.ANY)
    vmem_spec = pl.BlockSpec(memory_space=pltpu.VMEM)
    out, ig, *gws, sg = pl.pallas_call(
        functools.partial(kernel, layers, rows_real),
        out_shape=out_shapes,
        in_specs=[any_spec] * 6 + [vmem_spec] * 8,
        out_specs=(any_spec, vmem_spec, any_spec, any_spec, any_spec, any_spec, vmem_spec),
        scratch_shapes=scratch,
        compiler_params=pltpu.CompilerParams(
            collective_id=0, has_side_effects=True, vmem_limit_bytes=int(63.5 * 2 ** 20)),
        cost_estimate=pl.CostEstimate(
            flops=int(1e11), bytes_accessed=int(1e8), transcendentals=0),
    )(tok, cot, *weights, *smalls)

    if groups > 1:
        wide = (jnp.zeros((layers, width, gw.shape[2]), F32) for gw in gws)
        gws = [lax.psum_scatter(lax.dynamic_update_slice_in_dim(zero, gw, d8 * kb, 1), "dp",
                                scatter_dimension=1, tiled=True) for zero, gw in zip(wide, gws)]
    sg = sg.reshape(layers, 16, tile)
    vecs = lax.dynamic_slice_in_dim(sg[:, :8], z * window, window, 2)
    ups_grad = lax.dynamic_slice_in_dim(sg[:, 8:12], z, 1, 1)[:, 0]
    if groups > 1:
        def own_part(v, n):
            wide = lax.dynamic_update_slice_in_dim(
                jnp.zeros(v.shape[:-1] + (n,), F32), v, at * v.shape[-1], v.ndim - 1)
            return lax.psum_scatter(wide, both, scatter_dimension=v.ndim - 1, tiled=True)

        vecs, ups_grad = own_part(vecs, width), own_part(ups_grad, 4 * fq)
    return (
        out[:rows_real][None],
        ig[:rows_real][None],
        gws[0].reshape(layers, here, 3, hq),
        gws[1],
        gws[2],
        gws[3],
        vecs[:, 6:8],
        ups_grad,
        vecs[:, 4],
        vecs[:, 5],
        vecs[:, 0],
        vecs[:, 1],
        vecs[:, 2],
        vecs[:, 3],
    )


def solution(mesh):
    both = ("dp", "tensor")
    rows = P("dp", "tensor", None)
    cols = P(None, "dp", "tensor")
    vec = P(None, both)
    return jax.shard_map(
        shards,
        mesh=mesh,
        in_specs=(rows, rows, P("dp"), P(None, "dp", None, "tensor"), cols, cols, cols,
                  P(None, None, both), vec, vec, vec, vec, vec, vec, vec),
        out_specs=(rows, rows, P(None, "dp", None, "tensor"), cols, cols, cols,
                   P(None, None, both), vec, vec, vec, vec, vec, vec, vec),
        check_vma=False,
    )
```

```python
import functools

import jax
import jax.numpy as jnp
from jax import lax
from jax.experimental import pallas as pl
from jax.experimental.pallas import tpu as pltpu
from jax.sharding import PartitionSpec as P

HD = 64
VALID = 577
EPS = 1e-06
ROOT_HALF = 0.7071067811865476
INV_ROOT_2PI = 0.3989422804014327
FAR_BELOW = -1e30
MESH = pl.DeviceIdType.MESH
F32 = jnp.float32
BF16 = jnp.bfloat16
TILE = 32
NT = 256


def dot_nn(a, b):
    return lax.dot_general(a, b, (((1,), (0,)), ((), ())), preferred_element_type=F32)


def dot_nt(a, b):
    return lax.dot_general(a, b, (((1,), (1,)), ((), ())), preferred_element_type=F32)


def dot_tn(a, b):
    return lax.dot_general(a, b, (((0,), (0,)), ((), ())), preferred_element_type=F32)


def loop(n, body, unroll=False):
    def step(i, carry):
        body(i)
        return carry

    lax.fori_loop(0, n, step, 0, unroll=unroll)


def aligned(v, m):
    return pl.multiple_of(v, m)


def kernel(
    layers, rows_real,
    tok, cot, wqkv, wout, wup, wdown, *more,
):
    vecs, qv_in, up_in, rest = more[:6], more[6], more[7], more[8:]
    (
        out_ref, ig_ref, gqkv, gout, gup, gdown, sg_out,
        W, xs, gs, n1, n2, r1, r2, a1, a2, qkv, o, act, dgl,
        gb, hb, ub, ob, dqkv, dk_acc, dv_acc, acc, kmask,
        own, sendA, recvA, sendB, recvB, tokst, cotst, igrecv,
        small, smz, smf, qb, upb, upg, sg, sgy, sgx, sgc, sgz,
        recv1, recv2, recv4,
        s0s, s0r, s1s, s1r, s2s, s2r,
        as_, ar, bs, br, cs, cr,
        tks, tkr, cts, ctr, oss, osr, sms, smr, smzs, smzr, sgs, sgr, sgzs, sgzr,
        g1s, g1r, g2s, g2r, g4s, g4r, stage, sts, smrows, small_in,
    ) = rest
    width = xs.shape[1]
    half = xs.shape[0]
    slot = half // 2
    rows_all = 2 * half
    kb = wup.shape[1]
    blk = 2 * kb
    hq = o.shape[2]
    fq = act.shape[2]
    heads = hq // HD
    wn = width // NT

    dp = lax.axis_index("dp")
    z = lax.axis_index("tensor")
    base = (dp // 8) * 8
    d8 = dp % 8
    y, x, c = d8 // 4, (d8 // 2) % 2, d8 % 2
    zh, zl = z // 2, z % 2
    q = zl + 2 * c
    z2 = (z + 2) % 4
    home = c == zh

    def dev(yy, xx, cc, zz):
        return (base + yy * 4 + xx * 2 + cc, zz)

    sib = dev(y, x, 1 - c, z)
    xn = dev(y, 1 - x, c, z)
    yn = dev(1 - y, x, c, z)
    zp = dev(y, x, c, z + 1 - 2 * zl)
    far = dev(y, x, c, z2)
    swap = dev(y, x, zh, 2 * c + zl)

    def rc(src, dst, ss, rs, to):
        return pltpu.make_async_remote_copy(
            src_ref=src, dst_ref=dst, send_sem=ss, recv_sem=rs,
            device_id=to, device_id_type=MESH)

    def wait(ref, sem):
        pltpu.make_async_copy(ref, ref, sem).wait()

    barrier = pltpu.get_barrier_semaphore()
    greet = [xn, yn, sib]
    for k in range(1, 4):
        for cc in range(2):
            greet.append(dev(y, x, cc, (z + k) % 4))
    for to in greet:
        pl.semaphore_signal(barrier, inc=1, device_id=to, device_id_type=MESH)
    pl.semaphore_wait(barrier, len(greet))

    def rows_of(yy, xx):
        return aligned((2 * yy + xx) * blk, blk)

    my_rows = pl.ds(aligned(d8 * kb, kb), kb)
    own_blk = rows_of(y, x)
    x_blk = rows_of(y, 1 - x)
    y_blk = rows_of(1 - y, x)
    diag_blk = rows_of(1 - y, 1 - x)

    units = 3 * layers
    cut = 2 * hq
    pieces = [(0, slice(0, cut)), (0, slice(cut, fq))] + [(u, slice(0, fq)) for u in range(1, units)]

    def piece(p, at, n):
        u, cols = pieces[p]
        return W.at[u, pl.ds(at, n), cols]

    def sources(p):
        u, cols = pieces[p]
        l, part = u // 3, u % 3
        if part:
            return [((wup, wdown)[part - 1].at[l], cols)]
        found = [(wqkv.at[l, :, slice(cols.start, min(cols.stop, 3 * hq))],
                  slice(cols.start, min(cols.stop, 3 * hq)))]
        if cols.stop > 3 * hq:
            found.append((wout.at[l], slice(3 * hq, 4 * hq)))
        return found

    def s0_start(p):
        u = pieces[p][0]
        for i, (src, cols) in enumerate(sources(p)):
            dst = W.at[u, my_rows, cols]
            rc(src, dst, s0s.at[p, 0, i], s0r.at[p, c, i], dev(y, x, zh, z2)).start()

            @pl.when(home)
            def _():
                pltpu.make_async_copy(src, dst, s0r.at[p, c, i]).start()

            @pl.when(jnp.logical_not(home))
            def _():
                rc(src, dst, s0s.at[p, 1, i], s0r.at[p, c, i], sib).start()

    def s0_wait(p):
        u = pieces[p][0]
        for j in range(2):
            for i, (src, cols) in enumerate(sources(p)):
                wait(W.at[u, pl.ds(own_blk + j * kb, kb), cols], s0r.at[p, j, i])

    def s1_start(p):
        for j in range(2):
            ref = piece(p, own_blk + j * kb, kb)
            rc(ref, ref, s1s.at[p, 0, j], s1r.at[p, 0, j], xn).start()
            ref = piece(p, own_blk + (1 - j) * kb, kb)
            rc(ref, ref, s1s.at[p, 1, j], s1r.at[p, 1, j], yn).start()

    def s1_wait(p, j):
        wait(piece(p, x_blk + j * kb, kb), s1r.at[p, 0, j])
        wait(piece(p, y_blk + (1 - j) * kb, kb), s1r.at[p, 1, j])

    def s2_start(p):
        ref = piece(p, x_blk, kb)
        rc(ref, ref, s2s.at[p, 1], s2r.at[p, 1], yn).start()
        ref = piece(p, y_blk + kb, kb)
        rc(ref, ref, s2s.at[p, 0], s2r.at[p, 0], xn).start()

    def s2_wait(p):
        s1_wait(p, 1)
        wait(piece(p, diag_blk, kb), s2r.at[p, 1])
        wait(piece(p, diag_blk + kb, kb), s2r.at[p, 0])

    def ready(u):
        for p in range(len(pieces)):
            if pieces[p][0] == u:
                s2_wait(p)

    def sends_done(unit):
        for p in range(len(pieces)):
            if pieces[p][0] != unit:
                continue
            for i, (src, cols) in enumerate(sources(p)):
                ref = W.at[unit, my_rows, cols]
                wait(ref, s0s.at[p, 0, i])

                @pl.when(jnp.logical_not(home))
                def _():
                    wait(ref, s0s.at[p, 1, i])

            ref = piece(p, own_blk, kb)
            for j in range(2):
                for i in range(2):
                    wait(ref, s1s.at[p, j, i])
                wait(ref, s2s.at[p, j])

    def pump(p):
        s1_wait(p, 0)
        s2_start(p)
        if p + 1 < len(pieces):
            s0_wait(p + 1)
            s1_start(p + 1)
        if p + 3 < len(pieces):
            s0_start(p + 3)
        elif p + 3 == len(pieces):
            land_start(cot, cotst, cts, ctr)

    def land_start(src, dst, ss, rs):
        @pl.when(home)
        def _():
            pltpu.make_async_copy(src, dst.at[zl], rs.at[zl]).start()

        @pl.when(jnp.logical_not(home))
        def _():
            rc(src, dst.at[zl], ss.at[0], rs.at[zl], swap).start()

    def land_pass(src, dst, ss, rs):
        wait(dst.at[zl], rs.at[zl])
        rc(dst.at[zl], dst.at[zl], ss.at[1], rs.at[zl], zp).start()

    def land_wait(src, dst, ss, rs):
        wait(dst.at[1 - zl], rs.at[1 - zl])

    def land_sent(src, ss):
        @pl.when(jnp.logical_not(home))
        def _():
            wait(src, ss.at[0])

        wait(src, ss.at[1])

    def back_start(src, dst, ss, rs):
        @pl.when(home)
        def _():
            pltpu.make_async_copy(src, dst, rs).start()

        @pl.when(jnp.logical_not(home))
        def _():
            rc(src, dst, ss, rs, swap).start()

    def back_wait(src, dst, ss, rs):
        wait(dst, rs)

        @pl.when(jnp.logical_not(home))
        def _():
            wait(src, ss)

    tile_lanes = small_in.shape[1]

    def lanes_at(at, n):
        return pl.ds(aligned(at * tile_lanes, tile_lanes), n * tile_lanes)

    def column_start(src, dst, ss, rs):
        for k in range(1, 4):
            rc(src, dst.at[z], ss.at[k - 1], rs.at[z], dev(y, x, c, (z + k) % 4)).start()

    def column_wait(src, dst, ss, rs):
        for k in range(1, 4):
            wait(dst.at[(z + k) % 4], rs.at[(z + k) % 4])
            wait(src, ss.at[k - 1])

    def small_gather():
        column_wait(small_in, smz, smzs, smzr)
        smz[z] = small_in[...]
        v = smz[0].astype(F32)
        for k in range(1, 4):
            v = v + smz[k].astype(F32)
        small[:, lanes_at(d8, 1)] = v.astype(BF16)
        land_pass(tok, tokst, tks, tkr)
        for k, (at, n, to) in enumerate(((d8, 1, sib), (2 * (d8 // 2), 2, xn), (4 * y, 4, yn))):
            mine_now = small.at[:, lanes_at(at, n)]
            cp = rc(mine_now, mine_now, sms.at[k], smr.at[k], to)
            cp.start()
            cp.wait()

    def small_scatter(k):
        if k < 3:
            at, other, n, into, to = (
                (4 * y, 4 * (1 - y), 4, sgy, yn),
                (4 * y + 2 * x, 4 * y + 2 * (1 - x), 2, sgx, xn),
                (d8, 4 * y + 2 * x + 1 - c, 1, sgc, sib))[k]
            cp = rc(sg.at[:, lanes_at(other, n)], into, sgs.at[k], sgr.at[k], to)
            cp.start()
            cp.wait()
            sg[:, lanes_at(at, n)] += into[...]
        else:
            sgz[z] = sg[:, lanes_at(d8, 1)]
            column_start(sgz.at[z], sgz, sgzs, sgzr)
            column_wait(sgz.at[z], sgz, sgzs, sgzr)
            sg_out[...] = (sgz[0] + sgz[1]) + (sgz[2] + sgz[3])

    def round_rows(r):
        return pl.ds(r * half, half)

    def slot_at(r, h):
        return aligned(r * half + h * slot, slot)

    def share_start(ref, k, r):
        part = ref.at[pl.ds(slot_at(r, c), slot)]
        rc(part, part, cs.at[k, r], cr.at[k, r], sib).start()

    def share_wait(ref, k, r):
        part = ref.at[pl.ds(slot_at(r, 1 - c), slot)]
        wait(part, cr.at[k, r])
        wait(part, cs.at[k, r])

    last_out = 2 * layers - 1
    last_sum = 4 * layers - 1

    def bank(k):
        return 2 if k == last_out else (k + (k > last_out)) % 2

    def sum_part(k, r, lhs, cols, u, wcols):
        def step(n):
            ncols = pl.ds(aligned(n * NT, NT), NT)
            rows = jnp.concatenate(
                [lhs[pl.ds(slot_at(r, c), slot), cols], lhs[pl.ds(slot_at(r, 1 - c), slot), cols]], 0)
            v = dot_nt(rows, W[u, ncols, wcols])
            own[r, :, ncols] = v[:slot]
            sendA[r, :, ncols] = v[slot:].astype(BF16)

        loop(wn, step, True)
        rc(sendA.at[r], recvA.at[k % 2, r], as_.at[k, r], ar.at[k, r], sib).start()

    def sum_mid(k, r):
        wait(recvA.at[k % 2, r], ar.at[k, r])
        wait(sendA.at[r], as_.at[k, r])

        def step(i):
            rows = pl.ds(aligned(i * TILE, TILE), TILE)
            sendB[bank(k), r, rows, :] = (own[r, rows, :] + recvA[k % 2, r, rows, :].astype(F32)).astype(BF16)

        loop(slot // TILE, step)
        if k not in (last_out, last_sum):
            rc(sendB.at[bank(k), r], recvB.at[bank(k), r], bs.at[k, r], br.at[k, r], zp).start()

    def sum_only(k):
        rc(sendB.at[bank(k), 1 - zl], recvB.at[bank(k), 1 - zl], bs.at[k, 0], br.at[k, 0], zp).start()

    def sum_wait(k, r):
        wait(recvB.at[bank(k), r], br.at[k, r])

    def sum_sent(k, r):
        wait(sendB.at[bank(k), r], bs.at[k, r])

    def total(k, r, rows):
        return sendB[bank(k), r, rows, :].astype(F32) + recvB[bank(k), r, rows, :].astype(F32)

    def tiles(body):
        def step(i):
            body(aligned(i * TILE, TILE))

        loop(slot // TILE, step, True)

    def stream_rows(r, at):
        return pl.ds(aligned(r * slot + at, TILE), TILE)

    def full_rows(r, at):
        return pl.ds(aligned(slot_at(r, c) + at, TILE), TILE)

    def norm_tile(v, r, at, l, which, n_ref, r_ref, a_ref):
        gain = smf[pl.ds(16 * l + 2 * which, 1), :]
        shift = smf[pl.ds(16 * l + 2 * which + 1, 1), :]
        centre = v - jnp.mean(v, axis=1, keepdims=True)
        inv = lax.rsqrt(jnp.mean(centre * centre, axis=1, keepdims=True) + EPS)
        n = centre * inv
        rows = stream_rows(r, at)
        n_ref[l, rows, :] = n.astype(BF16)
        r_ref[l, rows, :] = inv
        a_ref[l, full_rows(r, at), :] = (n * gain + shift).astype(BF16)

    lane = lax.broadcasted_iota(jnp.int32, (1, hq), 1)
    QC = half

    def head_mask(h):
        return jnp.logical_and(lane >= h * HD, lane < (h + 1) * HD)

    def spare(h):
        return lane == (hq - 1 if h < heads - 1 else 0)

    qcols = slice(0, hq)
    kcols = slice(hq, 2 * hq)
    vcols = slice(2 * hq, 3 * hq)
    qkvcols = slice(0, 3 * hq)
    ocols = slice(3 * hq, 4 * hq)
    every = slice(0, fq)

    def mask_keys(l):
        for s in range(4):
            r, h = s // 2, s % 2
            rows = pl.ds(s * slot, slot)
            within = lax.broadcasted_iota(jnp.int32, (slot, 1), 0)
            valid = jnp.logical_and(within < rows_real, (2 * h + r) * rows_real + within < VALID)
            low = jnp.where(valid, 0.0, FAR_BELOW)
            keys = qkv[l, rows, kcols].astype(F32)
            for j, h in ((0, 0), (1, heads - 1)):
                kmask[j, rows, :] = jnp.where(spare(h), low, keys).astype(BF16)

    def softmax_of(qm, h):
        s = dot_nt(jnp.where(spare(h), 1.0, qm).astype(BF16), kmask[0 if h < heads - 1 else 1])
        e = jnp.exp(s - jnp.max(s, axis=1, keepdims=True))
        return e * (1.0 / jnp.sum(e, axis=1, keepdims=True))

    def attention(l, r, which):
        rows = round_rows(r)
        qc = qkv[l, rows, qcols].astype(F32)
        values = qkv[l, :, vcols]
        for h in which:
            m = head_mask(h)
            qm = jnp.where(m, qc * (HD ** -0.5), 0.0)
            p = softmax_of(qm, h).astype(BF16)
            mixed = dot_nn(p, values)
            pair = slice(h // 2 * 2 * HD, (h // 2 + 1) * 2 * HD)
            old = o[l, rows, pair]
            o[l, rows, pair] = jnp.where(m[:, pair], mixed[:, pair], old.astype(F32)).astype(BF16)

    def attention_back(l, r):
        rows = round_rows(r)
        qc = qkv[l, rows, qcols].astype(F32)
        oc = ob[rows, :].astype(F32)
        keys, values = qkv[l, :, kcols], qkv[l, :, vcols]
        dq = jnp.zeros((QC, hq), F32)
        for h in range(heads):
            m = head_mask(h)
            qm = jnp.where(m, qc * (HD ** -0.5), 0.0)
            om = jnp.where(m, oc, 0.0).astype(BF16)
            p = softmax_of(qm, h)
            dprob = dot_nt(om, values)
            inner = jnp.sum(dprob * p, axis=1, keepdims=True)
            ds = (p * (dprob - inner)).astype(BF16)
            dq = jnp.where(m, dot_nn(ds, keys), dq)
            dk = dot_tn(ds, qm.astype(BF16))
            dv = dot_tn(p.astype(BF16), om)
            if r == 0 and h == 0:
                dk_acc[...] = dk
                dv_acc[...] = dv
            else:
                dk_acc[...] += dk
                dv_acc[...] += dv
        dqkv[rows, qcols] = (dq * (HD ** -0.5)).astype(BF16)
        if r == 1:
            dqkv[:, kcols] = dk_acc[...].astype(BF16)
            dqkv[:, vcols] = dv_acc[...].astype(BF16)

    parts = [(u, every) for u in range(units)] + [(0, ocols)]
    parts[0] = (0, qkvcols)

    def kept(u):
        return units - 1 if u == 0 else u

    def rs1(p):
        u, cols = parts[p]
        for rows, j, to in ((diag_blk, 0, xn), (diag_blk + kb, 1, yn)):
            ref = W.at[kept(u), pl.ds(rows, kb), cols]
            rc(ref, recv1.at[u, j, :, cols], g1s.at[p, j], g1r.at[p, j], to).start()
        for rows, j, to in ((x_blk, 0, xn), (y_blk + kb, 1, yn)):
            ref = W.at[kept(u), pl.ds(rows, kb), cols]
            rc(ref, recv2.at[u, j, pl.ds(j * kb, kb), cols],
               g2s.at[p, j, j], g2r.at[p, j, j], to).start()

    RT = 64

    def add_rows(w, cols, at, refs, n):
        def step(i):
            off = aligned(i * RT, RT)
            rows = pl.ds(aligned(at + off, RT), RT)
            v = W[w, rows, cols].astype(F32)
            for ref in refs:
                v = v + ref[pl.ds(off, RT), cols].astype(F32)
            W[w, rows, cols] = v.astype(BF16)

        loop(n // RT, step)

    def rs2(p):
        u, cols = parts[p]
        for j in range(2):
            wait(recv1.at[u, j, :, cols], g1r.at[p, j])
            wait(recv1.at[u, j, :, cols], g1s.at[p, j])
        for rows, j, i, to in ((y_blk, 1, 0, yn), (x_blk + kb, 0, 1, xn)):
            add_rows(kept(u), cols, rows, [recv1.at[u, i]], kb)
            ref = W.at[kept(u), pl.ds(rows, kb), cols]
            rc(ref, recv2.at[u, j, pl.ds(i * kb, kb), cols],
               g2s.at[p, j, i], g2r.at[p, j, i], to).start()

    def rs3(p):
        u, cols = parts[p]
        for j in range(2):
            for i in range(2):
                part = recv2.at[u, j, pl.ds(i * kb, kb), cols]
                wait(part, g2r.at[p, j, i])
                wait(part, g2s.at[p, j, i])
        add_rows(kept(u), cols, own_blk, [recv2.at[u, 0], recv2.at[u, 1]], blk)

        @pl.when(home)
        def _():
            ref = W.at[kept(u), pl.ds(aligned(own_blk + (1 - c) * kb, kb), kb), cols]
            rc(ref, recv4.at[u, 0, :, cols], g4s.at[p, 0], g4r.at[p, 0], sib).start()
            ref = W.at[kept(u), pl.ds(aligned(own_blk + c * kb, kb), kb), cols]
            pltpu.make_async_copy(ref, recv4.at[u, 0, :, cols], g4r.at[p, 0]).start()

        @pl.when(jnp.logical_not(home))
        def _():
            for j in range(2):
                ref = W.at[kept(u), pl.ds(own_blk + j * kb, kb), cols]
                rc(ref, recv4.at[u, 1, :, cols], g4s.at[p, j], g4r.at[p, 1],
                   dev(y, x, j, z2)).start()

    def rs4(p):
        u, cols = parts[p]
        for j in range(2):
            wait(recv4.at[u, j, :, cols], g4r.at[p, j])
        wait(recv4.at[u, 0, :, cols], g4s.at[p, 0])

        @pl.when(jnp.logical_not(home))
        def _():
            wait(recv4.at[u, 0, :, cols], g4s.at[p, 1])

        slot_of = stored.index(None) if None in stored else len(order) % 2
        if stored[slot_of] is not None:
            store_wait(slot_of)

        def step(i):
            rows = pl.ds(aligned(i * RT, RT), RT)
            stage[slot_of, rows, cols] = (recv4[u, 0, rows, cols].astype(F32)
                                          + recv4[u, 1, rows, cols].astype(F32))

        loop(kb // RT, step)
        stored[slot_of] = p
        order.append(p)
        for src, dst, sem in stores(slot_of):
            pltpu.make_async_copy(src, dst, sem).start()

    stored, order = [None, None], []

    def stores(slot_of):
        p = stored[slot_of]
        u = parts[p][0]
        l, part = u // 3, u % 3
        if part:
            return [(stage.at[slot_of], (gup, gdown)[part - 1].at[l], sts.at[slot_of, 0])]
        both = [(stage.at[slot_of, :, qkvcols], gqkv.at[l], sts.at[slot_of, 0]),
                (stage.at[slot_of, :, ocols], gout.at[l], sts.at[slot_of, 1])]
        return both if u else both[:1] if p == 0 else both[1:]

    def store_wait(slot_of):
        for src, dst, sem in stores(slot_of):
            pltpu.make_async_copy(src, dst, sem).wait()

    def project(l, r):
        rows = round_rows(r)
        for j in range(3):
            cols = slice(j * hq, (j + 1) * hq)
            v = dot_nn(a1[l, rows, :], W[3 * l, :, cols])
            qkv[l, rows, cols] = (v + qb[8 * l + j:8 * l + j + 1, :]).astype(BF16)

    def expand(l, r):
        rows = round_rows(r)

        def step(j):
            cols = pl.ds(aligned(j * NT, NT), NT)
            u = dot_nn(a2[l, rows, :], W[3 * l + 1, :, cols]) + upb[8 * l:8 * l + 1, cols]
            phi = 0.5 * (1.0 + lax.erf(u * ROOT_HALF))
            act[l, rows, cols] = (u * phi).astype(BF16)
            density = INV_ROOT_2PI * jnp.exp(-0.5 * u * u)
            dgl[l, rows, cols] = (phi + u * density).astype(BF16)

        loop(fq // NT, step)

    def expand_back(l, r):
        rows = round_rows(r)

        def step(j):
            cols = pl.ds(aligned(j * NT, NT), NT)
            v = dot_nn(gb[rows, :], W[3 * l + 2, :, cols]) * dgl[l, rows, cols].astype(F32)
            low = v.astype(BF16)
            ub[rows, cols] = low
            upg[8 * l:8 * l + 1, cols] += jnp.sum(low.astype(F32), axis=0, keepdims=True)

        loop(fq // NT, step)

    def mix_back(l, r):
        rows = round_rows(r)
        ob[rows, :] = dot_nn(hb[rows, :], W[3 * l, :, ocols]).astype(BF16)

    def weight_grad(u, lhs, rhs, cols):
        def step(t):
            rows = pl.ds(aligned(t * NT, NT), NT)
            W[kept(u), rows, cols] = dot_tn(lhs[:, rows], rhs[...]).astype(BF16)

        loop(wn, step)

    def acc_add(j, v):
        acc[j] += jnp.sum(v.reshape(TILE // 8, 8, width), axis=0)

    once = (zl == 0).astype(F32)

    def acc_out(j, row, share):
        v = jnp.sum(acc[j], axis=0, keepdims=True)
        sg[row:row + 1, :] = v if share is None else v * share

    def acc_clear():
        acc[...] = jnp.zeros_like(acc)

    def norm_back_tile(k, r, at, l, which, n_ref, r_ref, low_ref):
        rows = stream_rows(r, at)
        da = total(k, r, pl.ds(at, TILE))
        n = n_ref[l, rows, :].astype(F32)
        e = da * smf[pl.ds(16 * l + 2 * which, 1), :]
        inner = jnp.mean(e * n, axis=1, keepdims=True)
        middle = jnp.mean(e, axis=1, keepdims=True)
        g = gs[rows, :] + r_ref[l, rows, :] * (e - middle - n * inner)
        acc_add(0, da * n)
        acc_add(1, da)
        if low_ref is None:
            tokst[0, pl.ds(at, TILE), :] = g.astype(BF16)
        else:
            acc_add(2, g)
            gs[rows, :] = g
            low_ref[full_rows(r, at), :] = g.astype(BF16)

    def norm_back(k, r, l, which, n_ref, r_ref, low_ref, low_k):
        sum_wait(k, r)
        if r == 0:
            acc_clear()
        tiles(lambda at: norm_back_tile(k, r, at, l, which, n_ref, r_ref, low_ref))
        share_start(low_ref, low_k, r)
        sum_sent(k, r)
        if r == 1:
            acc_out(0, 16 * l + 2 * which, once)
            acc_out(1, 16 * l + 2 * which + 1, once)
            acc_out(2, 16 * l + 4 if which == 1 else 16 * (l - 1) + 5, once)

    window = vecs[0].shape[1]
    place = (lax.broadcasted_iota(jnp.int32, (window, tile_lanes), 1)
             == z * window + lax.broadcasted_iota(jnp.int32, (window, tile_lanes), 0))
    place = jnp.where(place, 1.0, 0.0).astype(BF16)
    smrows[...] = jnp.zeros_like(smrows)
    for j, ref in enumerate(vecs):
        v = dot_nn(ref[...], place)
        for l in range(layers):
            smrows[16 * l + j:16 * l + j + 1, :] = v[l:l + 1]
    for l in range(layers):
        smrows[16 * l + 6:16 * l + 8, :] = dot_nn(qv_in[l], place)
        smrows[pl.ds(16 * l + 8 + z, 1), :] = up_in[l:l + 1, :].astype(F32)
    small_in[...] = smrows[...].astype(BF16)
    column_start(small_in, smz, smzs, smzr)
    land_start(tok, tokst, tks, tkr)
    s0_start(0)
    s0_start(1)
    sg[...] = jnp.zeros_like(sg)
    qb[...] = jnp.zeros_like(qb)
    upg[...] = jnp.zeros_like(upg)
    small_gather()
    s0_wait(0)
    s1_start(0)
    s0_start(2)
    smf[...] = small[...].astype(F32)
    mine = pl.ds(aligned(q * hq, hq), hq)
    up_tiles = [(slice(j * tile_lanes, (j + 1) * tile_lanes), j % 4, 2 * q + j // 4)
                for j in range(fq // tile_lanes)]
    for l in range(layers):
        for j, row in ((0, 6), (2, 7)):
            qb[8 * l + j:8 * l + j + 1, :] = smf[16 * l + row:16 * l + row + 1, mine]
        for cols, row, at in up_tiles:
            row = 16 * l + 8 + row
            upb[8 * l:8 * l + 1, cols] = smf[row:row + 1, lanes_at(at, 1)]

    s0_wait(1)
    s1_start(1)
    s0_start(3)
    s1_wait(0, 0)
    s2_start(0)
    land_wait(tok, tokst, tks, tkr)
    for r in range(2):
        def first(at, r=r):
            v = tokst[r, pl.ds(at, TILE), :].astype(F32)
            xs[stream_rows(r, at), :] = v
            norm_tile(v, r, at, 0, 0, n1, r1, a1)

        tiles(first)
        share_start(a1.at[0], 0, r)
    pump(1)
    ready(0)
    for r in range(2):
        share_wait(a1.at[0], 0, r)
        project(0, r)

    def stream_step(k, r, l_bias, row, l, which, n_ref, r_ref, a_ref, share_k):
        sum_wait(k, r)

        def body(at):
            rows = stream_rows(r, at)
            v = xs[rows, :] + total(k, r, pl.ds(at, TILE)) + smf[pl.ds(16 * l_bias + row, 1), :]
            xs[rows, :] = v
            norm_tile(v, r, at, l, which, n_ref, r_ref, a_ref)

        tiles(body)
        share_start(a_ref.at[l], share_k, r)
        sum_sent(k, r)

    for l in range(layers):
        final = l + 1 == layers
        k = 2 * l
        mask_keys(l)
        attention(l, 0, range(heads))
        if l == 0:
            pump(2)
        sum_part(k, 0, o.at[l], slice(0, hq), 3 * l, ocols)
        attention(l, 1, range(heads // 2))
        sum_mid(k, 0)
        attention(l, 1, range(heads // 2, heads))
        sum_part(k, 1, o.at[l], slice(0, hq), 3 * l, ocols)
        sum_mid(k, 1)
        if final:
            if layers == 1:
                land_pass(cot, cotst, cts, ctr)
            land_wait(cot, cotst, cts, ctr)
            acc_clear()
            for r in range(2):
                def first_back(at, r=r):
                    low = cotst[r, pl.ds(at, TILE), :]
                    gs[stream_rows(r, at), :] = low.astype(F32)
                    gb[full_rows(r, at), :] = low
                    acc_add(2, low.astype(F32))

                tiles(first_back)
                share_start(gb, 2 * layers, r)
            acc_out(2, 16 * (layers - 1) + 5, once)
        if final:
            pump(3 * l + 3)
        stream_step(k, 0, l, 4, l, 1, n2, r2, a2, 2 * l + 1)
        if not final:
            pump(3 * l + 3)
        ready(3 * l + 1)
        share_wait(a2.at[l], 2 * l + 1, 0)
        expand(l, 0)
        stream_step(k, 1, l, 4, l, 1, n2, r2, a2, 2 * l + 1)
        share_wait(a2.at[l], 2 * l + 1, 1)
        expand(l, 1)
        ready(3 * l + 2)
        if not final:
            for r in range(2):
                sum_part(k + 1, r, act.at[l], every, 3 * l + 2, every)
            for r in range(2):
                sum_mid(k + 1, r)
            pump(3 * l + 4)
            stream_step(k + 1, 0, l, 5, l + 1, 0, n1, r1, a1, 2 * l + 2)
            ready(3 * l + 3)
            share_wait(a1.at[l + 1], 2 * l + 2, 0)
            project(l + 1, 0)
            stream_step(k + 1, 1, l, 5, l + 1, 0, n1, r1, a1, 2 * l + 2)
            pump(3 * l + 5)
            share_wait(a1.at[l + 1], 2 * l + 2, 1)
            project(l + 1, 1)
            if l + 2 == layers:
                land_pass(cot, cotst, cts, ctr)

    land_sent(tok, tks)
    k = 2 * layers
    ks = 2 * layers

    def start_round(l, k, ks, r):
        share_wait(gb, ks, r)
        expand_back(l, r)
        if l == layers - 1 and r == 1:
            sum_mid(k, 0)
        sum_part(k, r, ub, every, 3 * l + 1, every)

    start_round(layers - 1, k, ks, 0)
    for l in reversed(range(layers)):
        top, bottom = l == layers - 1, l == 0
        start_round(l, k, ks, 1)
        sum_mid(k, 1)
        if top:
            for r in range(2):
                sum_part(last_out, r, act.at[l], every, 3 * l + 2, every)
            for r in range(2):
                sum_mid(last_out, r)
            sum_only(last_out)
        for u in (3 * l + 2, 3 * l + 1):
            sends_done(u)
        weight_grad(3 * l + 2, gb, act.at[l], every)
        rs1(3 * l + 2)
        weight_grad(3 * l + 1, a2.at[l], ub, every)
        rs1(3 * l + 1)
        if top:
            wait(recvB.at[bank(last_out), zl], br.at[last_out, 0])

            def finish(at):
                v = (xs[stream_rows(zl, at), :] + total(last_out, zl, pl.ds(at, TILE))
                     + smf[pl.ds(16 * l + 5, 1), :])
                tokst[0, pl.ds(at, TILE), :] = v.astype(BF16)

            tiles(finish)
            wait(sendB.at[bank(last_out), 1 - zl], bs.at[last_out, 0])
            back_start(tokst.at[0], out_ref, oss.at[0], osr.at[0])
        else:
            rs3(3 * l + 4)
            rs4(3 * l + 5)
        mask_keys(l)
        norm_back(k, 0, l, 1, n2, r2, hb, ks + 1)
        rs2(3 * l + 2)
        share_wait(hb, ks + 1, 0)
        mix_back(l, 0)
        attention_back(l, 0)
        norm_back(k, 1, l, 1, n2, r2, hb, ks + 1)
        rs2(3 * l + 1)
        if not top:
            rs3(3 * l + 3)
        share_wait(hb, ks + 1, 1)
        mix_back(l, 1)
        if bottom:
            weight_grad(0, hb, o.at[l], ocols)
            rs1(units)
        attention_back(l, 1)
        k += 1
        if bottom:
            weight_grad(0, a1.at[l], dqkv, qkvcols)
            rs1(0)
        sum_part(k, 0, dqkv, qkvcols, 3 * l, qkvcols)
        sum_part(k, 1, dqkv, qkvcols, 3 * l, qkvcols)
        sum_mid(k, 0)
        sum_mid(k, 1)
        if bottom:
            sum_only(k)
        for row, cols in ((6, qcols), (7, vcols)):
            sg[16 * l + row:16 * l + row + 1, mine] = jnp.sum(
                dqkv[:, cols].astype(F32), axis=0, keepdims=True)
        sends_done(3 * l)
        if not bottom:
            weight_grad(3 * l, a1.at[l], dqkv, qkvcols)
            weight_grad(3 * l, hb, o.at[l], ocols)
            rs1(3 * l)
            rs3(3 * l + 2)
            if top:
                back_wait(tokst.at[0], out_ref, oss.at[0], osr.at[0])
            norm_back(k, 0, l, 0, n1, r1, gb, ks + 2)
            rs2(3 * l)
            start_round(l - 1, k + 1, ks + 2, 0)
            norm_back(k, 1, l, 0, n1, r1, gb, ks + 2)
            sum_mid(k + 1, 0)
        else:
            rs3(2)
            rs2(units)
            rs4(4)
            rs3(1)
            rs2(0)
            wait(recvB.at[bank(k), zl], br.at[k, 0])
            acc_clear()
            tiles(lambda at: norm_back_tile(k, zl, at, l, 0, n1, r1, None))
            acc_out(0, 16 * l, None)
            acc_out(1, 16 * l + 1, None)
            wait(sendB.at[bank(k), 1 - zl], bs.at[k, 0])
            back_start(tokst.at[0], igrecv, oss.at[1], osr.at[1])
            rs3(units)
        k += 1
        ks += 2

    for l in range(layers):
        for cols, row, at in up_tiles:
            row = 16 * l + 8 + row
            sg[row:row + 1, lanes_at(at, 1)] = upg[8 * l:8 * l + 1, cols]
    small_scatter(0)
    rs3(0)
    for j in range(1, 4):
        small_scatter(j)
    rs4(3)
    rs4(2)
    rs4(1)
    rs4(units)
    back_wait(tokst.at[0], igrecv, oss.at[1], osr.at[1])
    ig_ref[...] = igrecv[...].astype(F32)
    rs4(0)
    store_wait(0)
    store_wait(1)
    land_sent(cot, cts)


def shards(tokens, cotangent, image_mask, qkv_weight, out_weight, up_weight, down_weight,
           qv_bias, up_bias, out_bias, down_bias, attn_gain, attn_shift, mlp_gain, mlp_shift):
    images_here, rows_real, width = tokens.shape
    layers = qkv_weight.shape[0]
    hq = qkv_weight.shape[3]
    fq = up_weight.shape[2]
    lanes = lax.axis_size("tensor")
    groups = lax.axis_size("dp") // 8
    assert images_here == 1 and lanes == 4 and layers > 1 and width == fq == 4 * hq
    kb = width // 8
    slot = -(-rows_real // TILE) * TILE
    half = 2 * slot
    rows_all = 4 * slot
    units = 3 * layers
    dp = lax.axis_index("dp")
    z = lax.axis_index("tensor")
    d8 = dp % 8

    position = z * rows_real + jnp.arange(rows_real)
    keep = (position < VALID).astype(BF16)[:, None] * image_mask.astype(BF16)[0]
    pad = ((0, slot - rows_real), (0, 0))
    tok = jnp.pad(tokens[0], pad)
    cot = jnp.pad(cotangent[0] * keep, pad)

    here = qkv_weight.shape[1]
    weights = (qkv_weight.reshape(layers, here, 3 * hq), out_weight, up_weight, down_weight)
    smalls = (attn_gain, attn_shift, mlp_gain, mlp_shift, out_bias, down_bias, qv_bias, up_bias)
    if groups > 1:
        weights = tuple(lax.dynamic_slice_in_dim(
            lax.all_gather(w, "dp", axis=1, tiled=True), d8 * kb, kb, 1) for w in weights)
        both = ("dp", "tensor")
        at = d8 * lanes + z
        smalls = tuple(lax.dynamic_slice_in_dim(
            lax.all_gather(v, both, axis=v.ndim - 1, tiled=True),
            at * (n // (8 * lanes)), n // (8 * lanes), v.ndim - 1)
            for v, n in zip(smalls, (width,) * 7 + (4 * fq,)))

    window = smalls[0].shape[1]
    tile = lanes * window

    out_shapes = (
        jax.ShapeDtypeStruct((slot, width), BF16),
        jax.ShapeDtypeStruct((slot, width), F32),
        jax.ShapeDtypeStruct((layers, kb, 3 * hq), F32),
        jax.ShapeDtypeStruct((layers, kb, hq), F32),
        jax.ShapeDtypeStruct((layers, kb, fq), F32),
        jax.ShapeDtypeStruct((layers, kb, fq), F32),
        jax.ShapeDtypeStruct((16 * layers, tile), F32),
    )
    V = pltpu.VMEM
    D = lambda *s: pltpu.SemaphoreType.DMA(s)
    sums, shares = 4 * layers, 4 * layers
    scratch = [
        V((units, width, fq), BF16),
        V((half, width), F32), V((half, width), F32),
        V((layers, half, width), BF16), V((layers, half, width), BF16),
        V((layers, half, 1), F32), V((layers, half, 1), F32),
        V((layers, rows_all, width), BF16), V((layers, rows_all, width), BF16),
        V((layers, rows_all, 3 * hq), BF16), V((layers, rows_all, hq), BF16),
        V((layers, rows_all, fq), BF16), V((layers, rows_all, fq), BF16),
        V((rows_all, width), BF16), V((rows_all, width), BF16),
        V((rows_all, fq), BF16), V((rows_all, hq), BF16), V((rows_all, 3 * hq), BF16),
        V((rows_all, hq), F32), V((rows_all, hq), F32), V((3, 8, width), F32),
        V((2, rows_all, hq), BF16),
        V((2, slot, width), F32),
        V((2, slot, width), BF16), V((2, 2, slot, width), BF16),
        V((3, 2, slot, width), BF16), V((3, 2, slot, width), BF16),
        V((2, slot, width), BF16), V((2, slot, width), BF16),
        V((slot, width), BF16),
        V((16 * layers, width), BF16), V((4, 16 * layers, tile), BF16),
        V((16 * layers, width), F32), V((8 * layers, hq), F32),
        V((8 * layers, fq), F32), V((8 * layers, fq), F32), V((16 * layers, width), F32),
        V((16 * layers, width // 2), F32), V((16 * layers, width // 4), F32),
        V((16 * layers, tile), F32), V((4, 16 * layers, tile), F32),
        V((units, 2, kb, fq), BF16), V((units, 2, 2 * kb, fq), BF16), V((units, 2, kb, fq), BF16),
        D(units + 1, 2, 2), D(units + 1, 2, 2), D(units + 1, 2, 2), D(units + 1, 2, 2),
        D(units + 1, 2), D(units + 1, 2),
        D(sums, 2), D(sums, 2), D(sums, 2), D(sums, 2), D(shares, 2), D(shares, 2),
        D(2), D(2), D(2), D(2), D(2), D(2), D(3), D(3), D(3), D(4), D(3), D(3), D(3), D(4),
        D(units + 1, 2), D(units + 1, 2), D(units + 1, 2, 2), D(units + 1, 2, 2),
        D(units + 1, 2), D(units + 1, 2),
        V((2, kb, fq), F32), D(2, 2),
        V((16 * layers, tile), F32), V((16 * layers, tile), BF16),
    ]
    any_spec = pl.BlockSpec(memory_space=pl.ANY)
    vmem_spec = pl.BlockSpec(memory_space=pltpu.VMEM)
    out, ig, *gws, sg = pl.pallas_call(
        functools.partial(kernel, layers, rows_real),
        out_shape=out_shapes,
        in_specs=[any_spec] * 6 + [vmem_spec] * 8,
        out_specs=(any_spec, vmem_spec, any_spec, any_spec, any_spec, any_spec, vmem_spec),
        scratch_shapes=scratch,
        compiler_params=pltpu.CompilerParams(
            collective_id=0, has_side_effects=True, vmem_limit_bytes=int(63.5 * 2 ** 20)),
        cost_estimate=pl.CostEstimate(
            flops=int(1e11), bytes_accessed=int(1e8), transcendentals=0),
    )(tok, cot, *weights, *smalls)

    if groups > 1:
        wide = (jnp.zeros((layers, width, gw.shape[2]), F32) for gw in gws)
        gws = [lax.psum_scatter(lax.dynamic_update_slice_in_dim(zero, gw, d8 * kb, 1), "dp",
                                scatter_dimension=1, tiled=True) for zero, gw in zip(wide, gws)]
    sg = sg.reshape(layers, 16, tile)
    vecs = lax.dynamic_slice_in_dim(sg[:, :8], z * window, window, 2)
    ups_grad = lax.dynamic_slice_in_dim(sg[:, 8:12], z, 1, 1)[:, 0]
    if groups > 1:
        def own_part(v, n):
            wide = lax.dynamic_update_slice_in_dim(
                jnp.zeros(v.shape[:-1] + (n,), F32), v, at * v.shape[-1], v.ndim - 1)
            return lax.psum_scatter(wide, both, scatter_dimension=v.ndim - 1, tiled=True)

        vecs, ups_grad = own_part(vecs, width), own_part(ups_grad, 4 * fq)
    return (
        out[:rows_real][None],
        ig[:rows_real][None],
        gws[0].reshape(layers, here, 3, hq),
        gws[1],
        gws[2],
        gws[3],
        vecs[:, 6:8],
        ups_grad,
        vecs[:, 4],
        vecs[:, 5],
        vecs[:, 0],
        vecs[:, 1],
        vecs[:, 2],
        vecs[:, 3],
    )


def solution(mesh):
    both = ("dp", "tensor")
    rows = P("dp", "tensor", None)
    cols = P(None, "dp", "tensor")
    vec = P(None, both)
    return jax.shard_map(
        shards,
        mesh=mesh,
        in_specs=(rows, rows, P("dp"), P(None, "dp", None, "tensor"), cols, cols, cols,
                  P(None, None, both), vec, vec, vec, vec, vec, vec, vec),
        out_specs=(rows, rows, P(None, "dp", None, "tensor"), cols, cols, cols,
                   P(None, None, both), vec, vec, vec, vec, vec, vec, vec),
        check_vma=False,
    )
```
